32 devices in a mesh: expert: 4 (over y, x), shard: 8 (over z, core).
Axes of the slice: x: 2, y: 2, z: 4, core: 2. Of those that a mesh axis runs over, the one named last changes fastest.
Arguments:
- tokens: bfloat16 [12288, 1536], P(('expert', 'shard')), may hold values from -6 to 6
- cotangent: bfloat16 [12288, 1536], P(('expert', 'shard')), may hold values from -6 to 6
- lengths: int32 [32], P(('expert', 'shard')), may hold values from 96 to 384, as said below
- routes: int32 [12288, 8], P(('expert', 'shard')), may hold values from 0 to 15, all different within a row; in each aligned block of 384 rows (0 to 383, 384 to 767, ...) at most 288 rows name the same one
- route_gates: bfloat16 [12288, 8], P(('expert', 'shard')), may hold values from 0.25 to 0.75
- norm_gains: float32 [2, 1536], replicated, may hold values from 0.5 to 1.5
- attn_master: float32 [384, 128, 128], P(('expert', 'shard')), may hold values from -4 to 4
- attn_stats: float32 [384, 2, 128, 128], P(('expert', 'shard')), may hold values from -512 to 512
- attn_roots: float32 [384, 2, 128, 128], P(('expert', 'shard')), may hold values from -2 to 2
- attn_deal: int32 [384], replicated, may hold values from 0 to 383, as said below
- expert_master: float32 [2304, 128, 128], P(('expert', 'shard')), may hold values from -4 to 4
- expert_stats: float32 [2304, 2, 128, 128], P(('expert', 'shard')), may hold values from -512 to 512
- expert_roots: float32 [2304, 2, 128, 128], P(('expert', 'shard')), may hold values from -2 to 2
- expert_deal: int32 [4, 576], P('expert'), may hold values from 0 to 575, as said below
Outputs:
- output: bfloat16 [12288, 1536], P(('expert', 'shard'))
- input_grad: float32 [12288, 1536], P(('expert', 'shard'))
- gain_grads: float32 [2, 1536], replicated
- new_gains: float32 [2, 1536], replicated
- attn_grads: float32 [384, 128, 128], P(('expert', 'shard'))
- attn_stats_new: float32 [384, 2, 128, 128], P(('expert', 'shard'))
- attn_new: float32 [384, 128, 128], P(('expert', 'shard'))
- expert_grads: float32 [2304, 128, 128], P(('expert', 'shard'))
- expert_stats_new: float32 [2304, 2, 128, 128], P(('expert', 'shard'))
- expert_new: float32 [2304, 128, 128], P(('expert', 'shard'))
The draws below stay inside these ranges and needn't reach their ends.
Inputs may be any that keep to these rules, and one draw needn't show every extreme that they name: `routes`: in each aligned block of 384 rows (one sequence) no expert is named by more than 288 rows, a bound that some block reaches. `lengths`: some sequence uses all 384 slots. `attn_deal`: A permutation of the attention blocks. `expert_deal`: each row is a permutation of its group's blocks.
All inputs are finite; a program needn't handle non-finite values.
Results may differ from the reference program's by a relative error of at most 0.015.
Values may be sent and summed in bfloat16 or wider, within the bound.
No kernel may reach another device: no remote copies, remote signals or barrier semaphores. Data moves between devices by JAX's collectives and lax.ppermute only.
A program may use at most 384 MiB of HBM per device.

```python
import math
import jax
import jax.numpy as jnp
import numpy as np
from jax import lax

D = 1536
H = 24
KV = 8
HD = 64
FF = 512
TOP = 8
BLOCK = 128
EXP_DEV = 4
TOK_DEV = 384
CAP = 288
EXPERTS = 16
SEQS = 32
TOKENS = 12288
ATT_BLOCKS = 384
EXP_BLOCKS = 576
ALL_EXP_BLOCKS = 2304
N_EXPERT = 4


def attention_order(key):
    return jax.random.permutation(jax.random.fold_in(key, 71), ATT_BLOCKS).astype(jnp.int32)


def expert_order(key):
    seeded = jax.random.fold_in(key, 73)
    indices = jnp.arange(N_EXPERT)

    def single(number):
        return jax.random.permutation(jax.random.fold_in(seeded, number), EXP_BLOCKS)
    return jax.vmap(single)(indices).astype(jnp.int32)


def attention_scale(ordering):
    across = D // BLOCK
    boundary = across * across + across * (2 * KV * HD // BLOCK)
    return jnp.where(ordering >= boundary, 8.0, 1.0) / jnp.sqrt(jnp.float32(D))


def expert_scale(ordering):
    across = D // BLOCK
    hidden_across = FF // BLOCK
    within = ordering % (3 * across * hidden_across)
    return jnp.where(within < 2 * across * hidden_across, 1.0 / jnp.sqrt(jnp.float32(D)), 1.0 / jnp.sqrt(jnp.float32(FF)))


def symmetric_draw(key, block_count, diag_low, diag_high, spread):
    first_key = jax.random.fold_in(key, 1)
    second_key = jax.random.fold_in(key, 2)
    samples = jnp.clip(jax.random.normal(first_key, (block_count, 2, BLOCK, BLOCK), jnp.float32), -4.0, 4.0)
    mirrored = (samples + jnp.swapaxes(samples, -1, -2)) * 0.5 * spread
    diagonal = jnp.exp(jax.random.uniform(second_key, (block_count, 2, BLOCK, 1), jnp.float32, jnp.log(diag_low), jnp.log(diag_high)))
    identity = (jnp.arange(BLOCK)[:, None] == jnp.arange(BLOCK)[None, :]).astype(jnp.float32)
    return mirrored * (1.0 - identity) + diagonal * identity


def draw_attn_deal(key, part):
    return attention_order(key)


def draw_expert_deal(key, part):
    return expert_order(key)


def draw_attn_master(key, part):
    ordering = attention_order(key)
    key = jax.random.fold_in(key, 2)
    samples = jnp.clip(jax.random.normal(key, (ATT_BLOCKS, BLOCK, BLOCK), jnp.float32), -4.0, 4.0)
    return samples * attention_scale(ordering)[:, None, None]


def draw_expert_master(key, part):
    ordering = expert_order(key).reshape(-1)
    key = jax.random.fold_in(key, 3)
    samples = jnp.clip(jax.random.normal(key, (ALL_EXP_BLOCKS, BLOCK, BLOCK), jnp.float32), -4.0, 4.0)
    return samples * expert_scale(ordering)[:, None, None]


def draw_attn_stats(key, part):
    key = jax.random.fold_in(key, 4)
    return symmetric_draw(key, ATT_BLOCKS, BLOCK * 1.0, BLOCK * 4.0, jnp.sqrt(2.0 * BLOCK))


def draw_expert_stats(key, part):
    key = jax.random.fold_in(key, 5)
    return symmetric_draw(key, ALL_EXP_BLOCKS, BLOCK * 1.0, BLOCK * 4.0, jnp.sqrt(2.0 * BLOCK))


def draw_attn_roots(key, part):
    key = jax.random.fold_in(key, 6)
    return symmetric_draw(key, ATT_BLOCKS, 0.5, 2.0, 0.7 / jnp.sqrt(1.0 * BLOCK))


def draw_expert_roots(key, part):
    key = jax.random.fold_in(key, 7)
    return symmetric_draw(key, ALL_EXP_BLOCKS, 0.5, 2.0, 0.7 / jnp.sqrt(1.0 * BLOCK))


def draw_lengths(key, part):
    key = jax.random.fold_in(key, 8)
    drawn = jax.random.randint(key, (SEQS,), TOK_DEV // 4, TOK_DEV + 1, dtype=jnp.int32)
    chosen = jax.random.randint(jax.random.fold_in(key, 9), (), 0, SEQS, dtype=jnp.int32)
    return drawn.at[chosen].set(TOK_DEV)


def shard_levels(stream_key, shape, cuts, smallest, top_value):
    factor_of, own = 1.0, jax.random.fold_in(stream_key, 6)
    for dim, parts in cuts:
        draws = jnp.exp(jax.random.uniform(jax.random.fold_in(own, dim), (parts,), jnp.float32, smallest / len(cuts), top_value / len(cuts)))
        factor_of = factor_of * jnp.repeat(draws, shape[dim] // parts).reshape([-1 if axis == dim else 1 for axis in range(len(shape))])
    return factor_of


def shared_out(rng, own, number, rows, amount, top, bound, slope):
    sequence = jax.random.permutation(rng, amount)
    packed, common = portions_of(amount, rows * top, bound, slope, True), portions_of(amount, rows * top, bound, slope, False)
    places = jnp.arange(amount)

    def named(sizes, offset_by):
        used = int((sizes > 0).sum())
        fixed = max(1, used // 4)
        passed = fixed + (places - fixed + offset_by * (used - fixed)) % max(1, amount - fixed)
        return jnp.zeros((amount,), jnp.int32).at[sequence[jnp.where(places < fixed, places, passed)]].set(jnp.asarray(sizes, jnp.int32))

    sizes = jnp.where(number % 4 == 0, named(packed, number // 4), named(common, number - number // 4 - 1))
    mixed = jax.random.permutation(jax.random.fold_in(own, 3), amount)
    donor, receiver = mixed[0:amount // 2 * 2:2], mixed[1:amount // 2 * 2:2]
    margin = jnp.minimum(sizes[donor] - 1, bound - sizes[receiver]) // 2
    margin = jnp.where((donor == sequence[0]) | (receiver == sequence[0]) | (sizes[receiver] == 0), 0, jnp.maximum(margin, 0))
    passed = jax.random.randint(jax.random.fold_in(own, 4), (amount // 2,), 0, 1 << 20) % (margin + 1)
    sizes = sizes.at[donor].add(-passed).at[receiver].add(passed)
    members = jnp.searchsorted(jnp.cumsum(sizes), jnp.arange(rows * top), side="right").astype(jnp.int32)
    table = members.reshape(top, rows).T
    table = table[jax.random.permutation(jax.random.fold_in(own, 1), rows)]
    offset_by = jax.random.randint(jax.random.fold_in(own, 2), (rows, 1), 0, top)
    return jnp.take_along_axis(table, (jnp.arange(top)[None, :] + offset_by) % top, axis=1)


def portions_of(number_of, total, most, slope, full):
    loads = [(1 << 20) // math.isqrt(standing ** slope) + 1 for standing in range(1, number_of + 1)]
    largest = most if full else min(most, max(-(-total // number_of), total * loads[0] // sum(loads)))
    least = 1 if total - largest >= number_of - 1 else 0
    counts, spare = [largest] + [least] * (number_of - 1), total - largest - least * (number_of - 1)
    while spare > 0:
        free = [i for i in range(1, number_of) if counts[i] < largest] or [i for i in range(1, number_of) if counts[i] < most]
        pool, remaining = sum([loads[i] for i in free]), spare
        for i in free:
            extra = min(most - counts[i], max(1, remaining * loads[i] // pool), spare)
            counts[i] = counts[i] + extra
            spare = spare - extra
    return np.array(counts)


def scatter_about(own_key, shape, scale, most, split=(), held_as=jnp.bfloat16):
    level = shard_levels(own_key, shape, split, -0.22, 0.18) if split else 1.0
    values = jax.random.normal(own_key, shape, jnp.float32) * scale * level
    return jnp.minimum(jnp.maximum(values, -most), most).astype(held_as)


def setup_inputs(seed: int = 0) -> dict:
    splits = jax.random.split(jax.random.key(seed), 15)
    tokens = scatter_about(splits[0], (TOKENS, D), 1.0, 6.0, ((0, 32),))
    cotangent = scatter_about(splits[1], (TOKENS, D), 1.0, 6.0, ((0, 32),))
    lengths = draw_lengths(jax.random.fold_in(splits[14], 71), 0)
    routes_keys = jax.random.split(jax.random.fold_in(splits[3], 1), TOKENS // TOK_DEV)
    routes_turns = jax.random.permutation(jax.random.fold_in(splits[3], 3), TOKENS // TOK_DEV)
    routes = jax.vmap(lambda own, number: shared_out(jax.random.fold_in(splits[3], 2), own, number, TOK_DEV, EXPERTS, TOP, CAP, 1))(routes_keys, routes_turns).reshape((TOKENS, TOP))
    route_gates = jnp.clip(0.25 + 0.5 * jax.random.uniform(splits[4], (TOKENS, TOP), jnp.float32) ** shard_levels(splits[4], (TOKENS, TOP), ((0, 32),), -0.2, 0.2), 0.25, 0.75).astype(jnp.bfloat16)
    norm_gains = jnp.clip(1.0 + 0.1 * jax.random.normal(splits[5], (2, D), jnp.float32), 0.5, 1.5)
    attn_master = draw_attn_master(jax.random.fold_in(splits[14], 71), 0)
    attn_stats = draw_attn_stats(jax.random.fold_in(splits[14], 71), 0)
    attn_roots = draw_attn_roots(jax.random.fold_in(splits[14], 71), 0)
    attn_deal = draw_attn_deal(jax.random.fold_in(splits[14], 71), 0)
    expert_master = draw_expert_master(jax.random.fold_in(splits[14], 71), 0)
    expert_stats = draw_expert_stats(jax.random.fold_in(splits[14], 71), 0)
    expert_roots = draw_expert_roots(jax.random.fold_in(splits[14], 71), 0)
    expert_deal = draw_expert_deal(jax.random.fold_in(splits[14], 71), 0)
    return {"tokens": tokens, "cotangent": cotangent, "lengths": lengths, "routes": routes, "route_gates": route_gates, "norm_gains": norm_gains, "attn_master": attn_master, "attn_stats": attn_stats, "attn_roots": attn_roots, "attn_deal": attn_deal, "expert_master": expert_master, "expert_stats": expert_stats, "expert_roots": expert_roots, "expert_deal": expert_deal}


@jax.custom_vjp
def low(v):
    return lax.optimization_barrier(v.astype(jnp.bfloat16)).astype(jnp.float32)

@jax.custom_vjp
def low_back(v):
    return v

def low_keep(v):
    return (low(v), None)

def low_pass(kept, grad):
    return (grad,)

def back_keep(v):
    return (v, None)

def back_low(kept, grad):
    return (low(grad),)
low.defvjp(low_keep, low_pass)
low_back.defvjp(back_keep, back_low)
EPSILON = 1e-05
STEP_SIZE = 0.3
HIGHEST_PRECISION = lax.Precision.HIGHEST

def natural_order(slotted, dealing):
    slot_count = dealing.shape[0]
    inverse = jnp.zeros((slot_count,), jnp.int32).at[dealing].set(jnp.arange(slot_count, dtype=jnp.int32))
    return slotted[inverse]

def assemble(blocks, row_blocks, col_blocks):
    extent = blocks.shape[-1]
    return blocks.reshape(row_blocks, col_blocks, extent, extent).transpose(0, 2, 1, 3).reshape(row_blocks * extent, col_blocks * extent)

def rope_tables(positions):
    frequency = 10000.0 ** (-2.0 * jnp.arange(HD // 2, dtype=jnp.float32) / HD)
    angles = positions[:, None] * frequency[None, :]
    return (jnp.cos(angles), jnp.sin(angles))

def rotate(values, cosine_table, sine_table):
    halfway = HD // 2
    first_half = values[..., :halfway]
    second_half = values[..., halfway:]
    cosine_wide = cosine_table[:, None, :]
    sine_wide = sine_table[:, None, :]
    return jnp.concatenate([first_half * cosine_wide - second_half * sine_wide, second_half * cosine_wide + first_half * sine_wide], axis=-1)

def attend(pieces):
    queries_turned, keys_turned, values_low, length = pieces
    row_count = queries_turned.shape[0]
    grouped = queries_turned.reshape(row_count, KV, H // KV, HD)
    raw_scores = low_back(jnp.einsum('tkgd,skd->kgts', grouped, keys_turned, precision=HIGHEST_PRECISION) * HD ** (-0.5))
    places = jnp.arange(row_count)
    allowed = (places[None, :] <= places[:, None]) & (places[None, :] < length)
    scores = jnp.where(allowed, raw_scores, -1e+30)
    row_peak = lax.optimization_barrier(jnp.max(scores, axis=-1, keepdims=True))
    weights = jnp.exp(scores - row_peak)
    probs_low = low(weights / lax.optimization_barrier(jnp.sum(weights, axis=-1, keepdims=True)))
    mixed_heads = jnp.einsum('kgts,skd->tkgd', probs_low, values_low, precision=HIGHEST_PRECISION)
    return mixed_heads.reshape(row_count, H * HD)

def block_forward(tokens, norm_gains, attn_master, expert_master, lengths, routes, gate_values, attn_deal, expert_deal):
    across = D // BLOCK
    kv_across = 2 * KV * HD // BLOCK
    hidden_across = FF // BLOCK
    query_end = across * across
    keyval_end = query_end + across * kv_across
    split_at = 2 * across * hidden_across
    attn_blocks = low(natural_order(attn_master, attn_deal))
    w_query = assemble(attn_blocks[:query_end], across, across)
    w_keyval = assemble(attn_blocks[query_end:keyval_end], across, kv_across)
    w_out = assemble(attn_blocks[keyval_end:], across, across)
    grouped_master = expert_master.reshape(N_EXPERT, EXP_BLOCKS, BLOCK, BLOCK)
    expert_blocks = low(jax.vmap(natural_order)(grouped_master, expert_deal)).reshape(EXPERTS, EXP_BLOCKS // EXP_DEV, BLOCK, BLOCK)
    w_gateup = jax.vmap(lambda blocks: assemble(blocks, across, 2 * hidden_across))(expert_blocks[:, :split_at])
    w_down = jax.vmap(lambda blocks: assemble(blocks, hidden_across, across))(expert_blocks[:, split_at:])
    unit_one = tokens * lax.rsqrt(lax.optimization_barrier(jnp.mean(tokens * tokens, axis=-1, keepdims=True)) + EPSILON)
    normed_one = low(unit_one * norm_gains[0])
    queries = low_back(jnp.dot(normed_one, w_query, precision=HIGHEST_PRECISION))
    keyval = low_back(jnp.dot(normed_one, w_keyval, precision=HIGHEST_PRECISION))
    positions = (jnp.arange(TOKENS) % TOK_DEV).astype(jnp.float32)
    cosine_table, sine_table = rope_tables(positions)
    queries_turned = low(rotate(queries.reshape(TOKENS, H, HD), cosine_table, sine_table))
    keys_turned = low(rotate(keyval[:, :KV * HD].reshape(TOKENS, KV, HD), cosine_table, sine_table))
    values_low = low(keyval[:, KV * HD:].reshape(TOKENS, KV, HD))
    mixed_heads = lax.map(jax.checkpoint(attend), (queries_turned.reshape(SEQS, TOK_DEV, H, HD), keys_turned.reshape(SEQS, TOK_DEV, KV, HD), values_low.reshape(SEQS, TOK_DEV, KV, HD), lengths))
    mixed_heads = low_back(low(mixed_heads.reshape(TOKENS, H * HD)))
    middle = tokens + low_back(jnp.dot(mixed_heads, w_out, precision=HIGHEST_PRECISION))
    unit_two = middle * lax.rsqrt(lax.optimization_barrier(jnp.mean(middle * middle, axis=-1, keepdims=True)) + EPSILON)
    normed_two = low(unit_two * norm_gains[1])
    route_hits = (routes[:, :, None] == jnp.arange(EXPERTS)[None, None, :]).astype(jnp.float32)
    combine = lax.optimization_barrier(jnp.sum(route_hits * gate_values[:, :, None], axis=1))

    def expert_step(running, pieces):
        gateup_one, down_one, weight_one = pieces
        rows_in = low_back(normed_two)
        gate_up = low_back(jnp.dot(rows_in, gateup_one, precision=HIGHEST_PRECISION))
        hidden = low(jax.nn.silu(gate_up[:, :FF]) * gate_up[:, FF:])
        produced = low_back(low(jnp.dot(hidden, down_one, precision=HIGHEST_PRECISION)))
        return (running + weight_one[:, None] * produced, None)
    moe_sum, unused = lax.scan(jax.checkpoint(expert_step), jnp.zeros((TOKENS, D), jnp.float32), (w_gateup, w_down, combine.T))
    return middle + moe_sum

def shampoo(gradient, statistics, inverse_roots, master):
    unit_grad = gradient * lax.rsqrt(lax.optimization_barrier(jnp.mean(gradient * gradient, axis=(1, 2), keepdims=True)) + 1e-06)
    left_new = 0.5 * statistics[:, 0] + 0.5 * jnp.einsum('nij,nkj->nik', unit_grad, unit_grad, precision=HIGHEST_PRECISION)
    right_new = 0.5 * statistics[:, 1] + 0.5 * jnp.einsum('nji,njk->nik', unit_grad, unit_grad, precision=HIGHEST_PRECISION)
    turned = jnp.einsum('nij,njk->nik', inverse_roots[:, 0], gradient, precision=HIGHEST_PRECISION)
    turned = jnp.einsum('nij,njk->nik', turned, inverse_roots[:, 1], precision=HIGHEST_PRECISION)
    direction = turned * lax.rsqrt(lax.optimization_barrier(jnp.mean(turned * turned, axis=(1, 2), keepdims=True)) + 1e-06)
    spread = jnp.sqrt(lax.optimization_barrier(jnp.mean(master * master, axis=(1, 2), keepdims=True)))
    return (jnp.stack([left_new, right_new], axis=1), master - STEP_SIZE * spread * direction)

def reference(tokens, cotangent, lengths, routes, route_gates, norm_gains, attn_master, attn_stats, attn_roots, attn_deal, expert_master, expert_stats, expert_roots, expert_deal):
    gate_values = route_gates.astype(jnp.float32)

    def forward(inputs, gain_pair, attn_slots, expert_slots):
        return block_forward(inputs, gain_pair, attn_slots, expert_slots, lengths, routes, gate_values, attn_deal, expert_deal)
    primal, pullback = jax.vjp(forward, tokens.astype(jnp.float32), norm_gains, attn_master, expert_master)
    places = jnp.arange(TOKENS) % TOK_DEV
    valid_rows = (places < jnp.repeat(lengths, TOK_DEV)).astype(jnp.float32)
    input_grad, gain_grads, attn_grads, expert_grads = pullback(cotangent.astype(jnp.float32) * valid_rows[:, None])
    new_gains = norm_gains - STEP_SIZE * gain_grads * lax.rsqrt(lax.optimization_barrier(jnp.mean(gain_grads * gain_grads, axis=-1, keepdims=True)) + 1e-06)
    attn_stats_new, attn_new = shampoo(attn_grads, attn_stats, attn_roots, attn_master)
    expert_stats_new, expert_new = shampoo(expert_grads, expert_stats, expert_roots, expert_master)
    return (primal.astype(jnp.bfloat16), input_grad, gain_grads, new_gains, attn_grads, attn_stats_new, attn_new, expert_grads, expert_stats_new, expert_new)
```

```python
import jax
import jax.numpy as jnp
from jax import lax
from jax.experimental import pallas as pl
from jax.experimental.pallas import tpu as pltpu
from jax.sharding import PartitionSpec as P

D = 1536
H = 24
KV = 8
HD = 64
FF = 512
TOP = 8
BLOCK = 128
EXP_DEV = 4
LANES = 128
VMEM_BYTES = 60 * 1024 * 1024
BF16 = jnp.bfloat16
F32 = jnp.float32


EPSILON = 1e-05
STEP_SIZE = 0.3


def rope_tables(positions):
    frequency = 10000.0 ** (-2.0 * jnp.arange(HD // 2, dtype=jnp.float32) / HD)
    angles = positions[:, None] * frequency[None, :]
    return (jnp.cos(angles), jnp.sin(angles))


def dot_nn(left, right):
    return lax.dot_general(left, right, (((1,), (0,)), ((), ())), preferred_element_type=F32)


def dot_nt(left, right):
    return lax.dot_general(left, right, (((1,), (1,)), ((), ())), preferred_element_type=F32)


def dot_tn(left, right):
    return lax.dot_general(left, right, (((0,), (0,)), ((), ())), preferred_element_type=F32)


def params(**more):
    return pltpu.CompilerParams(vmem_limit_bytes=VMEM_BYTES, **more)


def whole(memory_space):
    return pl.BlockSpec(memory_space=memory_space)


def held(shape):
    return pl.BlockSpec(shape, lambda *_: (0,) * len(shape))


def inverse_of(dealing):
    slot_count = dealing.shape[0]
    return (
        jnp.zeros((slot_count,), jnp.int32)
        .at[dealing]
        .set(jnp.arange(slot_count, dtype=jnp.int32), unique_indices=True)
    )


def assemble_experts(blocks, inverse):
    across, wide, tall = D // BLOCK, 2 * FF // BLOCK, FF // BLOCK
    first, second = across * wide, tall * across

    def kernel(inverse_ref, blocks_ref, gateup_ref, down_ref, gateup_two, down_two, sems):
        def out(expert):
            half = expert % 2
            return [
                pltpu.make_async_copy(gateup_two.at[half], gateup_ref.at[expert], sems.at[2 + half]),
                pltpu.make_async_copy(down_two.at[half], down_ref.at[expert], sems.at[2 + half]),
            ]

        for expert in range(EXP_DEV):
            base, half = expert * (first + second), expert % 2
            if expert >= 2:
                for copy in out(expert - 2):
                    copy.wait()

            def gateup_block(i, _):
                pltpu.make_async_copy(
                    blocks_ref.at[inverse_ref[base + i]],
                    block_at(gateup_two.at[half], i // wide, i % wide),
                    sems.at[half],
                ).start()
                return 0

            def down_block(i, _):
                pltpu.make_async_copy(
                    blocks_ref.at[inverse_ref[base + first + i]],
                    block_at(down_two.at[half], i // across, i % across),
                    sems.at[half],
                ).start()
                return 0

            lax.fori_loop(0, first, gateup_block, 0, unroll=4)
            lax.fori_loop(0, second, down_block, 0, unroll=4)
            pltpu.make_async_copy(gateup_two.at[half], gateup_two.at[half], sems.at[half]).wait()
            pltpu.make_async_copy(down_two.at[half], down_two.at[half], sems.at[half]).wait()
            for copy in out(expert):
                copy.start()
        for expert in (EXP_DEV - 2, EXP_DEV - 1):
            for copy in out(expert):
                copy.wait()

    return pl.pallas_call(
        kernel,
        name="assemble_experts",
        out_shape=(
            jax.ShapeDtypeStruct((EXP_DEV, D, 2 * FF), BF16),
            jax.ShapeDtypeStruct((EXP_DEV, FF, D), BF16),
        ),
        in_specs=[whole(pltpu.SMEM), whole(pl.ANY)],
        out_specs=(whole(pl.ANY), whole(pl.ANY)),
        scratch_shapes=[
            pltpu.VMEM((2, D, 2 * FF), BF16),
            pltpu.VMEM((2, FF, D), BF16),
            pltpu.SemaphoreType.DMA((4,)),
        ],
        compiler_params=params(),
        cost_estimate=pl.CostEstimate(flops=0, bytes_accessed=4 * blocks.size, transcendentals=0),
    )(inverse, blocks)


def weight_of(packed, expert):
    lane = lax.broadcasted_iota(jnp.int32, packed.shape, 1)
    return jnp.sum(jnp.where(lane == expert, packed.astype(F32), 0.0), axis=1, keepdims=True)


def expert_front(group, rows, packed, w_gateup, w_down):
    count = rows.shape[0]

    def kernel(group_ref, rows_ref, packed_ref, gateup_ref, down_ref, hidden_ref, both_ref, out_ref, total):
        step = pl.program_id(0)
        weight = weight_of(packed_ref[:, D:], group_ref[0] * EXP_DEV + step)
        gate_up = dot_nn(rows_ref[...], gateup_ref[0])
        gate, up = gate_up[:, :FF], gate_up[:, FF:]
        sigmoid = jax.nn.sigmoid(gate)
        silu = gate * sigmoid
        hidden_ref[0] = (silu * up).astype(BF16)
        grad_rows = (weight * packed_ref[:, :D].astype(F32)).astype(BF16)
        grad_hidden = dot_nt(grad_rows, down_ref[0])
        both_ref[0, :, :FF] = (grad_hidden * up * sigmoid * (1.0 + gate * (1.0 - sigmoid))).astype(BF16)
        both_ref[0, :, FF:] = (grad_hidden * silu).astype(BF16)
        route = dot_nt(both_ref[0], gateup_ref[0]).astype(BF16).astype(F32)

        @pl.when(step == 0)
        def _():
            total[...] = route

        @pl.when(step > 0)
        def _():
            total[...] += route

        @pl.when(step == EXP_DEV - 1)
        def _():
            out_ref[...] = total[...].astype(BF16)

    return pl.pallas_call(
        kernel,
        name="expert_front",
        grid=(EXP_DEV,),
        out_shape=(
            jax.ShapeDtypeStruct((EXP_DEV, count, FF), BF16),
            jax.ShapeDtypeStruct((EXP_DEV, count, 2 * FF), BF16),
            jax.ShapeDtypeStruct((count, D), BF16),
        ),
        in_specs=[
            whole(pltpu.SMEM),
            held((count, D)),
            held((count, D + LANES)),
            pl.BlockSpec((1, D, 2 * FF), lambda j: (j, 0, 0)),
            pl.BlockSpec((1, FF, D), lambda j: (j, 0, 0)),
        ],
        out_specs=(
            pl.BlockSpec((1, count, FF), lambda j: (j, 0, 0)),
            pl.BlockSpec((1, count, 2 * FF), lambda j: (j, 0, 0)),
            held((count, D)),
        ),
        scratch_shapes=[pltpu.VMEM((count, D), F32)],
        compiler_params=params(dimension_semantics=("arbitrary",)),
        cost_estimate=pl.CostEstimate(
            flops=EXP_DEV * 2 * 5 * count * D * FF,
            bytes_accessed=EXP_DEV * 3 * D * FF * 2,
            transcendentals=EXP_DEV * count * FF,
        ),
    )(group, rows, packed, w_gateup, w_down)


def expert_weight_grads(group, inverse, rows, packed, hidden, both):
    parts = len(rows)
    count = rows[0].shape[0]
    slots = inverse.shape[0]
    across, wide, tall = D // BLOCK, 2 * FF // BLOCK, FF // BLOCK
    first, second = across * wide, tall * across
    tile = 256

    def kernel(group_ref, inverse_ref, *refs):
        rows_refs, packed_refs = refs[:parts], refs[parts : 2 * parts]
        hidden_refs, both_refs = refs[2 * parts : 3 * parts], refs[3 * parts : 4 * parts]
        out_ref, stage_gateup, stage_down, sems = refs[4 * parts :]
        step = pl.program_id(0)
        base = step * (first + second)

        def wait_gateup():
            pltpu.make_async_copy(stage_gateup, stage_gateup, sems.at[0]).wait()

        def wait_down():
            pltpu.make_async_copy(stage_down, stage_down, sems.at[1]).wait()

        pl.when(step > 0)(wait_gateup)
        for at in range(0, 2 * FF, tile):
            span = slice(at, at + tile)
            stage_gateup[:, span] = sum(
                dot_tn(x[...], b[0, :, span]) for x, b in zip(rows_refs, both_refs)
            ).astype(BF16)

        def gateup_block(i, _):
            row, col = i // wide, i % wide
            pltpu.make_async_copy(
                stage_gateup.at[pl.ds(pl.multiple_of(row * BLOCK, BLOCK), BLOCK), pl.ds(pl.multiple_of(col * BLOCK, BLOCK), BLOCK)],
                out_ref.at[inverse_ref[base + i]],
                sems.at[0],
            ).start()
            return 0

        lax.fori_loop(0, first, gateup_block, 0, unroll=8)
        pl.when(step > 0)(wait_down)
        weights = [
            weight_of(p[:, D:], group_ref[0] * EXP_DEV + step) for p in packed_refs
        ]
        for at in range(0, D, tile):
            span = slice(at, at + tile)
            stage_down[:, span] = sum(
                dot_tn(h[0], (w * p[:, span].astype(F32)).astype(BF16))
                for h, p, w in zip(hidden_refs, packed_refs, weights)
            ).astype(BF16)

        def down_block(i, _):
            row, col = i // across, i % across
            pltpu.make_async_copy(
                stage_down.at[pl.ds(pl.multiple_of(row * BLOCK, BLOCK), BLOCK), pl.ds(pl.multiple_of(col * BLOCK, BLOCK), BLOCK)],
                out_ref.at[inverse_ref[base + first + i]],
                sems.at[1],
            ).start()
            return 0

        lax.fori_loop(0, second, down_block, 0, unroll=8)

        @pl.when(step == EXP_DEV - 1)
        def _():
            wait_gateup()
            wait_down()

    return pl.pallas_call(
        kernel,
        name="expert_weight_grads",
        grid=(EXP_DEV,),
        out_shape=jax.ShapeDtypeStruct((slots, BLOCK, BLOCK), BF16),
        in_specs=[whole(pltpu.SMEM), whole(pltpu.SMEM)]
        + [held((count, D))] * parts
        + [held((count, D + LANES))] * parts
        + [pl.BlockSpec((1, count, FF), lambda j: (j, 0, 0))] * parts
        + [pl.BlockSpec((1, count, 2 * FF), lambda j: (j, 0, 0))] * parts,
        out_specs=whole(pl.ANY),
        scratch_shapes=[
            pltpu.VMEM((D, 2 * FF), BF16),
            pltpu.VMEM((FF, D), BF16),
            pltpu.SemaphoreType.DMA((2,)),
        ],
        compiler_params=params(dimension_semantics=("arbitrary",)),
        cost_estimate=pl.CostEstimate(
            flops=EXP_DEV * 2 * 3 * parts * count * D * FF,
            bytes_accessed=EXP_DEV * 3 * (parts * count * FF + D * FF) * 2,
            transcendentals=0,
        ),
    )(group, inverse, *rows, *packed, *hidden, *both)


def expert_outputs(group, packed, hidden, w_down):
    parts = len(packed)
    count = packed[0].shape[0]

    def kernel(group_ref, *refs):
        packed_refs, hidden_refs = refs[:parts], refs[parts : 2 * parts]
        down_ref = refs[2 * parts]
        out_refs, totals = refs[2 * parts + 1 : 3 * parts + 1], refs[3 * parts + 1 :]
        step = pl.program_id(0)
        for packed_ref, hidden_ref, out_ref, total in zip(packed_refs, hidden_refs, out_refs, totals):
            weight = weight_of(packed_ref[...], group_ref[0] * EXP_DEV + step)
            produced = dot_nn(hidden_ref[0], down_ref[0]).astype(BF16).astype(F32)
            term = weight * produced

            @pl.when(step == 0)
            def _():
                total[...] = term

            @pl.when(step > 0)
            def _():
                total[...] += term

            @pl.when(step == EXP_DEV - 1)
            def _():
                out_ref[...] = total[...].astype(BF16)

    return pl.pallas_call(
        kernel,
        name="expert_outputs",
        grid=(EXP_DEV,),
        out_shape=tuple(jax.ShapeDtypeStruct((count, D), BF16) for _ in range(parts)),
        in_specs=[whole(pltpu.SMEM)]
        + [pl.BlockSpec((count, LANES), lambda j: (0, D // LANES))] * parts
        + [pl.BlockSpec((1, count, FF), lambda j: (j, 0, 0))] * parts
        + [pl.BlockSpec((1, FF, D), lambda j: (j, 0, 0))],
        out_specs=tuple(held((count, D)) for _ in range(parts)),
        scratch_shapes=[pltpu.VMEM((count, D), F32)] * parts,
        compiler_params=params(dimension_semantics=("arbitrary",)),
        cost_estimate=pl.CostEstimate(
            flops=EXP_DEV * 2 * parts * count * D * FF,
            bytes_accessed=EXP_DEV * (parts * count * FF + D * FF) * 2,
            transcendentals=0,
        ),
    )(group, *packed, *hidden, w_down)


QUERY_END = H * HD
KEYVAL_END = QUERY_END + 2 * KV * HD
ACROSS = D // BLOCK
QUERY_COLS = QUERY_END // BLOCK
KEYVAL_COLS = (KEYVAL_END - QUERY_END) // BLOCK
OUT_COLS = D // BLOCK
ALL_COLS = QUERY_COLS + KEYVAL_COLS + OUT_COLS


def attention_places(natural):
    first = ACROSS * QUERY_COLS
    second = first + ACROSS * KEYVAL_COLS
    in_keyval, in_out = natural - first, natural - second
    row = jnp.where(
        natural < first,
        natural // QUERY_COLS,
        jnp.where(natural < second, in_keyval // KEYVAL_COLS, in_out // OUT_COLS),
    )
    col = jnp.where(
        natural < first,
        natural % QUERY_COLS,
        jnp.where(
            natural < second,
            QUERY_COLS + in_keyval % KEYVAL_COLS,
            QUERY_COLS + KEYVAL_COLS + in_out % OUT_COLS,
        ),
    )
    return row.astype(jnp.int32), col.astype(jnp.int32)


def block_at(ref, row, col):
    return ref.at[
        pl.ds(pl.multiple_of(row * BLOCK, BLOCK), BLOCK),
        pl.ds(pl.multiple_of(col * BLOCK, BLOCK), BLOCK),
    ]


def turn(values, cosine, sine):
    lane = lax.broadcasted_iota(jnp.int32, values.shape, 1)
    partner = jnp.where(
        lane % HD < HD // 2,
        pltpu.roll(values, LANES - HD // 2, 1),
        pltpu.roll(values, HD // 2, 1),
    )
    return values * cosine + partner * sine


def softmax_of(queries, keys, length):
    count = queries.shape[0]
    scores = dot_nt(queries, keys) * HD ** (-0.5)
    at_row = lax.broadcasted_iota(jnp.int32, (count, count), 0)
    at_col = lax.broadcasted_iota(jnp.int32, (count, count), 1)
    scores = jnp.where((at_col <= at_row) & (at_col < length), scores, -1e30)
    weights = jnp.exp(scores - jnp.max(scores, axis=1, keepdims=True))
    return weights * (1.0 / jnp.sum(weights, axis=1, keepdims=True))


def unit_rows(values):
    scale = lax.rsqrt(jnp.mean(values * values, axis=-1, keepdims=True) + EPSILON)
    return values * scale, scale


def attention_front(lengths, block_rows, block_cols, tokens, gains, cosine, sine, pieces):
    count = tokens.shape[0]
    group_size = H // KV

    def kernel(length_ref, row_ref, col_ref, tokens_ref, gains_ref, cosine_ref, sine_ref, *refs):
        piece_refs = refs[: len(pieces)]
        normed_ref, middle_ref, mixed_ref, q_ref, k_ref, v_ref, all_ref = refs[len(pieces) : -3]
        weights, heads, sems = refs[-3:]
        offset = 0
        for piece in piece_refs:

            def bring(i, _, piece=piece, offset=offset):
                pltpu.make_async_copy(
                    piece.at[i],
                    block_at(weights, row_ref[offset + i], col_ref[offset + i]),
                    sems.at[0],
                ).start()
                return 0

            lax.fori_loop(0, piece.shape[0], bring, 0, unroll=4)
            offset += piece.shape[0]
        residual = tokens_ref[...].astype(F32)
        normed = (unit_rows(residual)[0] * gains_ref[0:1, :]).astype(BF16)
        pltpu.make_async_copy(weights, weights, sems.at[0]).wait()
        keep = pltpu.make_async_copy(weights, all_ref, sems.at[1])
        keep.start()
        cosine, sine = cosine_ref[...], sine_ref[...]
        for at in range(0, KEYVAL_END, 2 * LANES):
            product = dot_nn(normed, weights[:, at : at + 2 * LANES])
            for half in range(2):
                pair = product[:, half * LANES : (half + 1) * LANES]
                column = at + half * LANES
                if column < QUERY_END + KV * HD:
                    pair = turn(pair, cosine, sine)
                pair = pair.astype(BF16)
                if column < QUERY_END:
                    target, head = q_ref, column // HD
                elif column < QUERY_END + KV * HD:
                    target, head = k_ref, (column - QUERY_END) // HD
                else:
                    target, head = v_ref, (column - QUERY_END - KV * HD) // HD
                target[head] = pair[:, :HD]
                target[head + 1] = pair[:, HD:]
        length = length_ref[0]

        def attend(j, _):
            for h in range(group_size):
                probs = softmax_of(q_ref[j * group_size + h], k_ref[j], length).astype(BF16)
                heads[j * group_size + h] = dot_nn(probs, v_ref[j]).astype(BF16)
            return 0

        lax.fori_loop(0, KV, attend, 0)
        for pair in range(H // 2):
            mixed_ref[:, pair * LANES : (pair + 1) * LANES] = jnp.concatenate(
                [heads[2 * pair], heads[2 * pair + 1]], axis=1
            )
        middle = residual + dot_nn(mixed_ref[...], weights[:, KEYVAL_END:])
        middle_ref[...] = middle
        normed_ref[...] = (unit_rows(middle)[0] * gains_ref[1:2, :]).astype(BF16)
        keep.wait()

    vmem = whole(pltpu.VMEM)
    return pl.pallas_call(
        kernel,
        name="attention_front",
        out_shape=(
            jax.ShapeDtypeStruct((count, D), BF16),
            jax.ShapeDtypeStruct((count, D), F32),
            jax.ShapeDtypeStruct((count, H * HD), BF16),
            jax.ShapeDtypeStruct((H, count, HD), BF16),
            jax.ShapeDtypeStruct((KV, count, HD), BF16),
            jax.ShapeDtypeStruct((KV, count, HD), BF16),
            jax.ShapeDtypeStruct((D, ALL_COLS * BLOCK), BF16),
        ),
        in_specs=[whole(pltpu.SMEM)] * 3 + [vmem] * 4 + [whole(pl.ANY)] * len(pieces),
        out_specs=(vmem,) * 6 + (whole(pl.ANY),),
        scratch_shapes=[
            pltpu.VMEM((D, ALL_COLS * BLOCK), BF16),
            pltpu.VMEM((H, count, HD), BF16),
            pltpu.SemaphoreType.DMA((2,)),
        ],
        compiler_params=params(),
        cost_estimate=pl.CostEstimate(
            flops=2 * count * D * ALL_COLS * BLOCK + 4 * H * count * count * HD,
            bytes_accessed=4 * D * ALL_COLS * BLOCK,
            transcendentals=H * count * count,
        ),
    )(lengths, block_rows, block_cols, tokens, gains, cosine, sine, *pieces)


def attention_back(lengths, positions, tokens, packed, gains, cosine, sine, middle, mixed, q, k, v, w_all, partials, near):
    count = tokens.shape[0]
    group_size = H // KV
    blocks = positions.shape[0]
    parts = len(partials)

    def kernel(length_ref, position_ref, tokens_ref, packed_ref, gains_ref, cosine_ref, sine_ref, middle_ref, mixed_ref,
               q_ref, k_ref, v_ref, *refs):
        partial_refs = refs[:parts]
        all_ref, input_grad_ref, gain_ref, near_ref, far_ref = refs[parts : parts + 5]
        weights, stage, grad_heads, grad_columns, sems = refs[parts + 5 :]
        bring_out = pltpu.make_async_copy(all_ref.at[:, pl.ds(KEYVAL_END, D)], weights.at[:, pl.ds(KEYVAL_END, D)], sems.at[0])
        bring_in = pltpu.make_async_copy(all_ref.at[:, pl.ds(0, KEYVAL_END)], weights.at[:, pl.ds(0, KEYVAL_END)], sems.at[1])
        bring_out.start()
        bring_in.start()

        def send(first, columns, col_offset):
            def one(i, _):
                place = position_ref[first + i]
                source = block_at(stage, i // columns, col_offset + i % columns)

                @pl.when(place < near)
                def _():
                    pltpu.make_async_copy(source, near_ref.at[place], sems.at[2]).start()

                @pl.when(place >= near)
                def _():
                    pltpu.make_async_copy(source, far_ref.at[place - near], sems.at[2]).start()

                return 0

            lax.fori_loop(0, ACROSS * columns, one, 0, unroll=4)

        grad_normed = partial_refs[0][...].astype(F32)
        for ref in partial_refs[1:]:
            grad_normed = grad_normed + ref[...].astype(F32)
        unit, scale = unit_rows(middle_ref[...])
        gain_ref[1:2, :] = jnp.sum(grad_normed * unit, axis=0, keepdims=True)
        scaled = grad_normed * gains_ref[1:2, :]
        grad_middle = packed_ref[:, :D].astype(F32) + scale * (
            scaled - unit * jnp.mean(scaled * unit, axis=-1, keepdims=True)
        )
        input_grad_ref[...] = grad_middle
        grad_attn = grad_middle.astype(BF16)
        for at in range(0, D, 4 * LANES):
            stage[:, KEYVAL_END + at : KEYVAL_END + at + 4 * LANES] = dot_tn(
                mixed_ref[...], grad_attn[:, at : at + 4 * LANES]
            ).astype(BF16)
        send(ACROSS * (QUERY_COLS + KEYVAL_COLS), OUT_COLS, QUERY_COLS + KEYVAL_COLS)
        bring_out.wait()
        for at in range(0, H * HD, 2 * LANES):
            product = dot_nt(grad_attn, weights[at : at + 2 * LANES, KEYVAL_END:]).astype(BF16)
            for part in range(2 * LANES // HD):
                grad_heads[at // HD + part] = product[:, part * HD : (part + 1) * HD]
        length = length_ref[0]

        def attend(j, _):
            keys, values = k_ref[j], v_ref[j]
            grad_keys = jnp.zeros((count, HD), F32)
            grad_values = jnp.zeros((count, HD), F32)
            for h in range(group_size):
                head = j * group_size + h
                queries, grad_mixed = q_ref[head], grad_heads[head]
                probs = softmax_of(queries, keys, length)
                grad_values = grad_values + dot_tn(probs.astype(BF16), grad_mixed)
                grad_probs = dot_nt(grad_mixed, values)
                inner = jnp.sum(probs * grad_probs, axis=1, keepdims=True)
                grad_scores = (probs * (grad_probs - inner)).astype(BF16)
                grad_columns[head] = dot_nn(grad_scores, keys) * HD ** (-0.5)
                grad_keys = grad_keys + dot_tn(grad_scores, queries)
            grad_columns[H + j] = grad_keys * HD ** (-0.5)
            grad_columns[H + KV + j] = grad_values
            return 0

        lax.fori_loop(0, KV, attend, 0)
        cosine, sine = cosine_ref[...], -sine_ref[...]
        residual = tokens_ref[...].astype(F32)
        unit_one, scale_one = unit_rows(residual)
        normed = (unit_one * gains_ref[0:1, :]).astype(BF16)
        bring_in.wait()
        grad_normed_one = jnp.zeros((count, D), F32)
        for at in range(0, KEYVAL_END, 4 * LANES):
            pairs = []
            for column in range(at, at + 4 * LANES, LANES):
                head = column // HD
                pair = jnp.concatenate([grad_columns[head], grad_columns[head + 1]], axis=1)
                if column < QUERY_END + KV * HD:
                    pair = turn(pair, cosine, sine)
                pairs.append(pair.astype(BF16))
            columns = jnp.concatenate(pairs, axis=1)
            span = slice(at, at + 4 * LANES)
            stage[:, span] = dot_tn(normed, columns).astype(BF16)
            grad_normed_one = grad_normed_one + dot_nt(columns, weights[:, span])
        send(0, QUERY_COLS, 0)
        send(ACROSS * QUERY_COLS, KEYVAL_COLS, QUERY_COLS)
        gain_ref[0:1, :] = jnp.sum(grad_normed_one * unit_one, axis=0, keepdims=True)
        scaled_one = grad_normed_one * gains_ref[0:1, :]
        input_grad_ref[...] += scale_one * (
            scaled_one - unit_one * jnp.mean(scaled_one * unit_one, axis=-1, keepdims=True)
        )
        pltpu.make_async_copy(stage, stage, sems.at[2]).wait()

    vmem, any_space = whole(pltpu.VMEM), whole(pl.ANY)
    return pl.pallas_call(
        kernel,
        name="attention_back",
        out_shape=(
            jax.ShapeDtypeStruct((count, D), F32),
            jax.ShapeDtypeStruct((2, D), F32),
            jax.ShapeDtypeStruct((near, BLOCK, BLOCK), BF16),
            jax.ShapeDtypeStruct((max(blocks - near, 1), BLOCK, BLOCK), BF16),
        ),
        in_specs=[whole(pltpu.SMEM)] * 2 + [vmem] * (10 + parts) + [any_space],
        out_specs=(vmem, vmem, any_space, any_space),
        scratch_shapes=[
            pltpu.VMEM((D, ALL_COLS * BLOCK), BF16),
            pltpu.VMEM((D, ALL_COLS * BLOCK), BF16),
            pltpu.VMEM((H, count, HD), BF16),
            pltpu.VMEM((H + 2 * KV, count, HD), F32),
            pltpu.SemaphoreType.DMA((3,)),
        ],
        compiler_params=params(),
        cost_estimate=pl.CostEstimate(
            flops=4 * count * D * ALL_COLS * BLOCK + 10 * H * count * count * HD,
            bytes_accessed=4 * D * ALL_COLS * BLOCK,
            transcendentals=H * count * count,
        ),
    )(lengths, positions, tokens, packed, gains, cosine, sine, middle, mixed, q, k, v, *partials, w_all)


def split_low(values):
    high = values.astype(BF16)
    return high, (values - high.astype(F32)).astype(BF16)


def shampoo(gradient, statistics, inverse_roots, master):
    terms = len(gradient)
    slots = master.shape[0]
    many = next(n for n in (6, 4, 3, 2, 1) if slots % n == 0)

    def kernel(*refs):
        term_refs = refs[:terms]
        stats_ref, roots_ref, master_ref, grad_ref, stats_out, master_out = refs[terms:]
        for i in range(many):
            total = term_refs[0][i].astype(F32)
            for ref in term_refs[1:]:
                total = total + ref[i].astype(F32)
            low = total.astype(BF16)
            grad = low.astype(F32)
            grad_ref[i] = grad
            scale = 0.5 / (jnp.mean(grad * grad) + 1e-06)
            stats_out[i, 0] = 0.5 * stats_ref[i, 0] + scale * dot_nt(low, low)
            stats_out[i, 1] = 0.5 * stats_ref[i, 1] + scale * dot_tn(low, low)
            left_high, left_low = split_low(roots_ref[i, 0])
            turned_high, turned_low = split_low(dot_nn(left_high, low) + dot_nn(left_low, low))
            right_high, right_low = split_low(roots_ref[i, 1])
            turned = (
                dot_nn(turned_high, right_high)
                + dot_nn(turned_low, right_high)
                + dot_nn(turned_high, right_low)
            )
            direction = turned * lax.rsqrt(jnp.mean(turned * turned) + 1e-06)
            own = master_ref[i]
            spread = jnp.sqrt(jnp.mean(own * own))
            master_out[i] = own - STEP_SIZE * spread * direction

    one = pl.BlockSpec((many, BLOCK, BLOCK), lambda i: (i, 0, 0))
    two = pl.BlockSpec((many, 2, BLOCK, BLOCK), lambda i: (i, 0, 0, 0))
    return pl.pallas_call(
        kernel,
        name="shampoo",
        grid=(slots // many,),
        out_shape=(
            jax.ShapeDtypeStruct((slots, BLOCK, BLOCK), F32),
            jax.ShapeDtypeStruct((slots, 2, BLOCK, BLOCK), F32),
            jax.ShapeDtypeStruct((slots, BLOCK, BLOCK), F32),
        ),
        in_specs=[one] * terms + [two, two, one],
        out_specs=(one, two, one),
        compiler_params=params(dimension_semantics=("arbitrary",)),
        cost_estimate=pl.CostEstimate(
            flops=slots * 7 * 2 * BLOCK**3,
            bytes_accessed=slots * BLOCK * BLOCK * (2 * terms + 36),
            transcendentals=0,
        ),
    )(*gradient, statistics, inverse_roots, master)


def move(array, pairs):
    return lax.ppermute(array, "shard", pairs)


def sibling(array):
    return move(array, [(i, i ^ 1) for i in range(lax.axis_size("shard"))])


def along(array, distance):
    size = lax.axis_size("shard")
    return move(array, [(i, (i + 2 * distance) % size) for i in range(size)])


def two_ways(array, other_first):
    one, two = swap(array, 1), swap(array, 2)
    three = swap(two, 1) if other_first else swap(one, 2)
    return one, two, three


def gather_attention(own, deal):
    size, groups = lax.axis_size("shard"), lax.axis_size("expert")
    slots = own.shape[0]
    by_device = deal.reshape(groups, size, slots)
    if groups != 4 or size != 8:
        return [lax.all_gather(own, ("expert", "shard"), axis=0, tiled=True)], deal
    me_e, me_s = lax.axis_index("expert"), lax.axis_index("shard")
    pieces, names, far_names = [], [], []
    lines = [own] + [along(own, d) for d in range(1, size // 2)]
    for d, line in enumerate(lines):
        four = jnp.concatenate([line, *two_ways(line, d % 2 == 1)], axis=0)
        pieces.append(four)
        source = (me_s - 2 * d) % size
        for m in range(groups):
            names.append(by_device[me_e ^ m, source])
            far_names.append(by_device[me_e ^ m, source ^ 1])
    pieces += [sibling(piece) for piece in pieces]
    return pieces, jnp.concatenate(names + far_names)


def attention_positions(deal, slots):
    size, groups = lax.axis_size("shard"), lax.axis_size("expert")
    inverse = inverse_of(deal)
    if groups != 4 or size != 8:
        return inverse
    owner, within = inverse // slots, inverse % slots
    mask = (owner // size) ^ lax.axis_index("expert")
    me = lax.axis_index("shard")
    core = (owner % 2) ^ (me % 2)
    distance = ((owner % size) // 2 - me // 2) % (size // 2)
    return ((((core * groups + mask) * (size // 2)) + distance) * slots + within).astype(jnp.int32)


def add_low(left, right):
    return (left.astype(F32) + right.astype(F32)).astype(BF16)


def scatter_attention(near, far, slots):
    size, groups = lax.axis_size("shard"), lax.axis_size("expert")
    if groups != 4 or size != 8:
        return [lax.psum_scatter(near, ("expert", "shard"), scatter_dimension=0, tiled=True)]
    half = size // 4
    total = add_low(near, sibling(far)).reshape(groups, 2, half * slots, BLOCK, BLOCK)
    lines = []
    for part, (first, second) in enumerate(((1, 2), (2, 1))):
        mine = jnp.concatenate([total[0, part], total[second, part]], axis=0)
        theirs = jnp.concatenate([total[first, part], total[3, part]], axis=0)
        mine = add_low(mine, swap(theirs, first))
        mine, theirs = mine[: half * slots], mine[half * slots :]
        lines.append(add_low(mine, swap(theirs, second)))
    terms = [line[i * slots : (i + 1) * slots] for line in lines for i in range(half)]
    return [terms[0]] + [along(terms[d], d) for d in range(1, size // 2)]


def sum_everywhere(values):
    size, groups = lax.axis_size("shard"), lax.axis_size("expert")
    if groups != 4 or size != 8:
        return lax.psum(values, ("expert", "shard"))
    for mask in (1, 2, 4):
        values = values + move(values, [(i, i ^ mask) for i in range(size)])
    for mask in (1, 2):
        values = values + swap(values, mask)
    return values


def swap(array, mask):
    if mask == 0:
        return array
    return lax.ppermute(array, "expert", [(i, i ^ mask) for i in range(lax.axis_size("expert"))])


def per_device(
    tokens,
    cotangent,
    lengths,
    routes,
    route_gates,
    norm_gains,
    attn_master,
    attn_stats,
    attn_roots,
    attn_deal,
    expert_master,
    expert_stats,
    expert_roots,
    expert_deal,
):
    row_count = tokens.shape[0]
    groups = lax.axis_size("expert")
    group = lax.axis_index("expert").astype(jnp.int32).reshape(1)
    pieces, natural = gather_attention(attn_master.astype(BF16), attn_deal)
    expert_all = lax.all_gather(expert_master.astype(BF16), "shard", axis=0, tiled=True)
    places = jnp.arange(row_count)
    valid_rows = places < lengths[0]
    grad_low = jnp.where(valid_rows[:, None], cotangent, jnp.zeros_like(cotangent))
    expert_lane = jnp.arange(LANES, dtype=jnp.int32)
    weights_row = sum(
        jnp.where(routes[:, k, None] == expert_lane, route_gates[:, k, None], jnp.zeros((), BF16))
        for k in range(TOP)
    )
    packed = [swap(jnp.concatenate([grad_low, weights_row], axis=1), m) for m in range(groups)]
    cosine, sine = rope_tables(jnp.arange(row_count, dtype=F32))
    cosine = jnp.concatenate([cosine] * 4, axis=1)
    sine = jnp.concatenate([-sine, sine] * 2, axis=1)
    block_rows, block_cols = attention_places(natural)
    normed_two, middle, mixed, q, k, v, w_all = attention_front(
        lengths, block_rows, block_cols, tokens, norm_gains, cosine, sine, pieces
    )
    expert_inverse = inverse_of(expert_deal[0])
    w_gateup, w_down = assemble_experts(expert_all, expert_inverse)
    rows = [swap(normed_two, m) for m in range(groups)]
    fronts = {}
    for m in [*range(1, groups), 0]:
        fronts[m] = expert_front(group, rows[m], packed[m], w_gateup, w_down)
    hidden = [fronts[m][0] for m in range(groups)]
    both = [fronts[m][1] for m in range(groups)]
    partials = [swap(fronts[m][2], m) for m in range(groups)]
    expert_term = expert_weight_grads(group, expert_inverse, rows, packed, hidden, both)
    moe_parts = expert_outputs(group, packed, hidden, w_down)
    moe_sum = sum(swap(moe_parts[m], m).astype(F32) for m in range(groups))
    output = (middle + moe_sum).astype(BF16)
    slots = attn_master.shape[0]
    positions = attention_positions(attn_deal, slots)
    near = positions.shape[0] // (2 if groups == 4 and lax.axis_size("shard") == 8 else 1)
    input_grad, gain_parts, near_blocks, far_blocks = attention_back(
        lengths, positions, tokens, packed[0], norm_gains, cosine, sine, middle, mixed, q, k, v, w_all, partials, near
    )
    attn_terms = scatter_attention(near_blocks, far_blocks, slots)
    expert_term = lax.psum_scatter(expert_term, "shard", scatter_dimension=0, tiled=True)
    gain_grads = sum_everywhere(gain_parts)
    new_gains = norm_gains - STEP_SIZE * gain_grads * lax.rsqrt(
        jnp.mean(gain_grads * gain_grads, axis=-1, keepdims=True) + 1e-06
    )
    expert_grads, expert_stats_new, expert_new = shampoo(
        [expert_term], expert_stats, expert_roots, expert_master
    )
    attn_grads, attn_stats_new, attn_new = shampoo(attn_terms, attn_stats, attn_roots, attn_master)
    return (
        output,
        input_grad,
        gain_grads,
        new_gains,
        attn_grads,
        attn_stats_new,
        attn_new,
        expert_grads,
        expert_stats_new,
        expert_new,
    )


def solution(mesh):
    in_specs = (
        P(("expert", "shard"), None),
        P(("expert", "shard"), None),
        P(("expert", "shard")),
        P(("expert", "shard"), None),
        P(("expert", "shard"), None),
        P(),
        P(("expert", "shard"), None, None),
        P(("expert", "shard"), None, None, None),
        P(("expert", "shard"), None, None, None),
        P(),
        P(("expert", "shard"), None, None),
        P(("expert", "shard"), None, None, None),
        P(("expert", "shard"), None, None, None),
        P("expert", None),
    )
    out_specs = (
        P(("expert", "shard"), None),
        P(("expert", "shard"), None),
        P(),
        P(),
        P(("expert", "shard"), None, None),
        P(("expert", "shard"), None, None, None),
        P(("expert", "shard"), None, None),
        P(("expert", "shard"), None, None),
        P(("expert", "shard"), None, None, None),
        P(("expert", "shard"), None, None),
    )
    return jax.shard_map(
        per_device, mesh=mesh, in_specs=in_specs, out_specs=out_specs, check_vma=False
    )
```

```python
import jax
import jax.numpy as jnp
from jax import lax
from jax.experimental import pallas as pl
from jax.experimental.pallas import tpu as pltpu
from jax.sharding import PartitionSpec as P

D = 1536
H = 24
KV = 8
HD = 64
FF = 512
TOP = 8
BLOCK = 128
EXP_DEV = 4
LANES = 128
VMEM_BYTES = 60 * 1024 * 1024
BF16 = jnp.bfloat16
F32 = jnp.float32


EPSILON = 1e-05
STEP_SIZE = 0.3


QUERY_END = H * HD
KEYVAL_END = QUERY_END + 2 * KV * HD
ACROSS = D // BLOCK
QUERY_COLS = QUERY_END // BLOCK
KEYVAL_COLS = (KEYVAL_END - QUERY_END) // BLOCK
OUT_COLS = D // BLOCK
ALL_COLS = QUERY_COLS + KEYVAL_COLS + OUT_COLS


def rope_tables(positions):
    frequency = 10000.0 ** (-2.0 * jnp.arange(HD // 2, dtype=jnp.float32) / HD)
    angles = positions[:, None] * frequency[None, :]
    return (jnp.cos(angles), jnp.sin(angles))


def dot_nn(left, right):
    return lax.dot_general(left, right, (((1,), (0,)), ((), ())), preferred_element_type=F32)


def dot_nt(left, right):
    return lax.dot_general(left, right, (((1,), (1,)), ((), ())), preferred_element_type=F32)


def dot_tn(left, right):
    return lax.dot_general(left, right, (((0,), (0,)), ((), ())), preferred_element_type=F32)


def params(**more):
    return pltpu.CompilerParams(vmem_limit_bytes=VMEM_BYTES, **more)


def cost(microseconds):
    return pl.CostEstimate(flops=int(microseconds * 1.15e9), bytes_accessed=1024, transcendentals=0)


def whole(memory_space):
    return pl.BlockSpec(memory_space=memory_space)


def held(shape):
    return pl.BlockSpec(shape, lambda *_: (0,) * len(shape))


def inverse_of(dealing):
    place = jnp.arange(dealing.shape[0], dtype=jnp.int32)
    return jnp.sum(jnp.where(dealing[None, :] == place[:, None], place[None, :], 0), axis=1)


def weight_of(packed, expert):
    lane = lax.broadcasted_iota(jnp.int32, packed.shape, 1)
    return jnp.sum(jnp.where(lane == expert, packed.astype(F32), 0.0), axis=1, keepdims=True)


def aligned(block):
    return block * BLOCK if isinstance(block, int) else pl.multiple_of(block * BLOCK, BLOCK)


def block_at(ref, row, col):
    return ref.at[
        pl.ds(aligned(row), BLOCK),
        pl.ds(aligned(col), BLOCK),
    ]


def stacked_copies(sources, target, sem):
    count = sources[0].shape[-2]
    return [
        pltpu.make_async_copy(
            source, target.at[pl.ds(i * count, count), :], sem
        )
        for i, source in enumerate(sources)
    ]


def expert_step(weight, rows, packed, matrix):
    gate_up = dot_nn(rows[...], matrix[:, : 2 * FF])
    grad_hidden = dot_nt(packed[:, :FF], matrix[:FF, 2 * FF :])
    for at in range(FF, D, FF):
        grad_hidden = grad_hidden + dot_nt(packed[:, at : at + FF], matrix[at : at + FF, 2 * FF :])
    gate, up = gate_up[:, :FF], gate_up[:, FF:]
    sigmoid = 0.5 * jnp.tanh(0.5 * gate) + 0.5
    silu = gate * sigmoid
    hidden = (silu * up * weight).astype(BF16)
    slope = grad_hidden * sigmoid * weight
    both = jnp.concatenate(
        [(slope * up * (1.0 + gate - silu)).astype(BF16), (slope * gate).astype(BF16)], axis=1
    )
    return hidden, both, dot_nt(both, matrix[:, : 2 * FF])


def expert_front(group, inverse, blocks, rows, packed):
    parts = len(rows)
    count = rows[0].shape[0]
    across, wide, tall = D // BLOCK, 2 * FF // BLOCK, FF // BLOCK
    first, second = across * wide, tall * across

    def kernel(group_ref, inverse_ref, blocks_ref, *refs):
        refs = list(refs)
        take = lambda n: [refs.pop(0) for _ in range(n)]
        rows_refs, packed_refs = take(parts), take(parts)
        hidden_refs, both_refs, out_refs = take(parts), take(parts), take(parts)
        kept_ref, rows_all, packed_all, total, matrices, block_sems, keep_sems, sems = refs
        step = pl.program_id(0)
        half = step % 2

        def bring(expert, half):
            base = expert * (first + second)

            for i in range(first + second):
                row, col = i // wide, i % wide
                if i >= first:
                    down = (i - first) % across
                    row, col = down // tall * tall + (i - first) // across, wide + down % tall
                pltpu.make_async_copy(
                    blocks_ref.at[inverse_ref[base + i]],
                    block_at(matrices.at[half], row, col),
                    block_sems.at[half],
                ).start()

        def keep(expert, half):
            return pltpu.make_async_copy(
                matrices.at[half, :, pl.ds(2 * FF, FF)], kept_ref.at[expert], keep_sems.at[half]
            )

        loads = [
            pltpu.make_async_copy(source, target.at[i], sems.at[n, i])
            for i in range(parts)
            for n, (source, target) in enumerate(
                ((rows_refs[i], rows_all), (packed_refs[i], packed_all))
            )
        ]

        @pl.when(step == 0)
        def _():
            for load in loads[:2]:
                load.start()
            bring(0, 0)
            for load in loads[2:]:
                load.start()

        @pl.when(step > 0)
        def _():
            keep(step - 1, 1 - half).wait()

        @pl.when(step < EXP_DEV - 1)
        def _():
            bring(step + 1, 1 - half)

        matrix = matrices.at[half]
        pltpu.make_async_copy(matrix, matrix, block_sems.at[half]).wait()
        keep(step, half).start()

        @pl.when(step == 0)
        def _():
            total[...] = jnp.zeros_like(total)
            for load in loads:
                load.wait()

        for i in range(parts):
            weight = weight_of(packed_all[i, :, D:], group_ref[0] * EXP_DEV + step)
            hidden, both, route = expert_step(weight, rows_all.at[i], packed_all.at[i], matrix)
            hidden_refs[i][0] = hidden
            both_refs[i][0] = both
            total[i] += route

        @pl.when(step == EXP_DEV - 1)
        def _():
            for i in range(parts):
                out_refs[i][...] = total[i].astype(BF16)
            keep(step, half).wait()

    any_space, smem = whole(pl.ANY), whole(pltpu.SMEM)
    out = pl.pallas_call(
        kernel,
        name="expert_front",
        grid=(EXP_DEV,),
        out_shape=(
            [jax.ShapeDtypeStruct((EXP_DEV, count, FF), BF16)] * parts
            + [jax.ShapeDtypeStruct((EXP_DEV, count, 2 * FF), BF16)] * parts
            + [jax.ShapeDtypeStruct((count, D), BF16)] * parts
            + [jax.ShapeDtypeStruct((EXP_DEV, D, FF), BF16)]
        ),
        in_specs=[smem] * 2 + [any_space] * (1 + 2 * parts),
        out_specs=(
            [pl.BlockSpec((1, count, FF), lambda j: (j, 0, 0))] * parts
            + [pl.BlockSpec((1, count, 2 * FF), lambda j: (j, 0, 0))] * parts
            + [held((count, D))] * parts
            + [any_space]
        ),
        scratch_shapes=[
            pltpu.VMEM((parts, count, D), BF16),
            pltpu.VMEM((parts, count, D + LANES), BF16),
            pltpu.VMEM((parts, count, D), F32),
            pltpu.VMEM((2, D, 3 * FF), BF16),
            pltpu.SemaphoreType.DMA((2,)),
            pltpu.SemaphoreType.DMA((2,)),
            pltpu.SemaphoreType.DMA((2, parts)),
        ],
        compiler_params=params(dimension_semantics=("arbitrary",)),
        cost_estimate=cost(100),
    )(group, inverse, blocks, *rows, *packed)
    return out[:parts], out[parts : 2 * parts], out[2 * parts : 3 * parts], out[-1]


def expert_weight_grads(positions, rows, packed, hidden, both):
    parts = len(rows)
    count = rows[0].shape[0]
    total_rows = parts * count
    slots = positions.shape[0]
    across, wide, tall = D // BLOCK, 2 * FF // BLOCK, FF // BLOCK
    first, second = across * wide, tall * across
    tile = 256

    def kernel(position_ref, *refs):
        refs = list(refs)
        take = lambda n: [refs.pop(0) for _ in range(n)]
        rows_refs, packed_refs, hidden_refs, both_refs = take(parts), take(parts), take(parts), take(parts)
        out_ref, rows_all, packed_all, hidden_two, both_two, stage_gateup, stage_down, sems = refs
        step = pl.program_id(0)
        half = step % 2
        base = step * (first + second)

        def loads(expert, half):
            return stacked_copies([r.at[expert] for r in hidden_refs], hidden_two.at[half], sems.at[2 + half]) + stacked_copies(
                [r.at[expert] for r in both_refs], both_two.at[half], sems.at[4 + half]
            )

        once = stacked_copies(rows_refs, rows_all, sems.at[6]) + stacked_copies(packed_refs, packed_all, sems.at[7])

        @pl.when(step == 0)
        def _():
            for load in once[:parts] + loads(0, 0) + once[parts:]:
                load.start()

        for load in loads(step, half):
            load.wait()

        @pl.when(step < EXP_DEV - 1)
        def _():
            for load in loads(step + 1, 1 - half):
                load.start()

        @pl.when(step == 0)
        def _():
            for load in once[:parts]:
                load.wait()

        def wait_gateup():
            pltpu.make_async_copy(stage_gateup, stage_gateup, sems.at[0]).wait()

        def wait_down():
            pltpu.make_async_copy(stage_down, stage_down, sems.at[1]).wait()

        def send(stage, sem, start, blocks, columns):
            for i in range(blocks):
                pltpu.make_async_copy(
                    block_at(stage, i // columns, i % columns), out_ref.at[position_ref[start + i]], sem
                ).start()

        pl.when(step > 0)(wait_gateup)
        for at in range(0, 2 * FF, tile):
            stage_gateup[:, at : at + tile] = dot_tn(
                rows_all[...], both_two[half, :, at : at + tile]
            ).astype(BF16)
        send(stage_gateup, sems.at[0], base, first, wide)
        pl.when(step > 0)(wait_down)

        @pl.when(step == 0)
        def _():
            for load in once[parts:]:
                load.wait()

        for at in range(0, D, tile):
            stage_down[:, at : at + tile] = dot_tn(
                hidden_two[half], packed_all[:, at : at + tile]
            ).astype(BF16)
        send(stage_down, sems.at[1], base + first, second, across)

        @pl.when(step == EXP_DEV - 1)
        def _():
            wait_gateup()
            wait_down()

    any_space, smem = whole(pl.ANY), whole(pltpu.SMEM)
    return pl.pallas_call(
        kernel,
        name="expert_weight_grads",
        grid=(EXP_DEV,),
        out_shape=jax.ShapeDtypeStruct((slots, BLOCK, BLOCK), BF16),
        in_specs=[smem] + [any_space] * (4 * parts),
        out_specs=any_space,
        scratch_shapes=[
            pltpu.VMEM((total_rows, D), BF16),
            pltpu.VMEM((total_rows, D + LANES), BF16),
            pltpu.VMEM((2, total_rows, FF), BF16),
            pltpu.VMEM((2, total_rows, 2 * FF), BF16),
            pltpu.VMEM((D, 2 * FF), BF16),
            pltpu.VMEM((FF, D), BF16),
            pltpu.SemaphoreType.DMA((8,)),
        ],
        compiler_params=params(dimension_semantics=("arbitrary",)),
        cost_estimate=cost(100),
    )(positions, *rows, *packed, *hidden, *both)


def expert_outputs(hidden, matrices):
    parts = len(hidden)
    count = hidden[0].shape[1]

    def kernel(*refs):
        hidden_refs, matrix_ref, out_refs = refs[:parts], refs[parts], refs[parts + 1 :]
        for hidden_ref, out_ref in zip(hidden_refs, out_refs):
            out_ref[...] = sum(
                dot_nn(hidden_ref[expert], matrix_ref[expert]) for expert in range(EXP_DEV)
            ).astype(BF16)

    return pl.pallas_call(
        kernel,
        name="expert_outputs",
        grid=(D // FF,),
        out_shape=tuple(jax.ShapeDtypeStruct((count, D), BF16) for _ in range(parts)),
        in_specs=[held((EXP_DEV, count, FF))] * parts
        + [pl.BlockSpec((EXP_DEV, FF, FF), lambda j: (0, j, 0))],
        out_specs=tuple(pl.BlockSpec((count, FF), lambda j: (0, j)) for _ in range(parts)),
        compiler_params=params(dimension_semantics=("arbitrary",)),
        cost_estimate=cost(30),
    )(*hidden, matrices)


def attention_places(natural):
    first = ACROSS * QUERY_COLS
    second = first + ACROSS * KEYVAL_COLS
    in_keyval, in_out = natural - first, natural - second
    row = jnp.where(
        natural < first,
        natural // QUERY_COLS,
        jnp.where(natural < second, in_keyval // KEYVAL_COLS, in_out // OUT_COLS),
    )
    col = jnp.where(
        natural < first,
        natural % QUERY_COLS,
        jnp.where(
            natural < second,
            QUERY_COLS + in_keyval % KEYVAL_COLS,
            QUERY_COLS + KEYVAL_COLS + in_out % OUT_COLS,
        ),
    )
    return row.astype(jnp.int32), col.astype(jnp.int32)


def turn(values, cosine, sine):
    lane = lax.broadcasted_iota(jnp.int32, values.shape, 1)
    partner = jnp.where(
        lane % HD < HD // 2,
        pltpu.roll(values, LANES - HD // 2, 1),
        pltpu.roll(values, HD // 2, 1),
    )
    return values * cosine + partner * sine


def softmax_of(queries, keys, length):
    count = queries.shape[0]
    scores = dot_nt(queries, keys) * HD ** (-0.5)
    at_row = lax.broadcasted_iota(jnp.int32, (count, count), 0)
    at_col = lax.broadcasted_iota(jnp.int32, (count, count), 1)
    scores = jnp.where((at_col <= at_row) & (at_col < length), scores, -1e30)
    weights = jnp.exp(scores - jnp.max(scores, axis=1, keepdims=True))
    return weights * (1.0 / jnp.sum(weights, axis=1, keepdims=True))


def unit_rows(values):
    scale = lax.rsqrt(jnp.mean(values * values, axis=-1, keepdims=True) + EPSILON)
    return values * scale, scale


def attention_front(lengths, block_rows, block_cols, tokens, gains, cosine, sine, pieces):
    count = tokens.shape[0]
    group_size = H // KV

    def kernel(length_ref, row_ref, col_ref, tokens_ref, gains_ref, cosine_ref, sine_ref, *refs):
        piece_refs = refs[: len(pieces)]
        normed_ref, middle_ref, mixed_ref, q_ref, k_ref, v_ref, all_ref = refs[len(pieces) : -3]
        weights, heads, sems = refs[-3:]
        offset = 0
        for piece in piece_refs:

            def bring(i, _, piece=piece, offset=offset):
                pltpu.make_async_copy(
                    piece.at[i],
                    block_at(weights, row_ref[offset + i], col_ref[offset + i]),
                    sems.at[0],
                ).start()
                return 0

            lax.fori_loop(0, piece.shape[0], bring, 0, unroll=4)
            offset += piece.shape[0]
        residual = tokens_ref[...].astype(F32)
        normed = (unit_rows(residual)[0] * gains_ref[0:1, :]).astype(BF16)
        pltpu.make_async_copy(weights, weights, sems.at[0]).wait()
        keep = pltpu.make_async_copy(weights, all_ref, sems.at[1])
        keep.start()
        cosine, sine = cosine_ref[...], sine_ref[...]
        for at in range(0, KEYVAL_END, 2 * LANES):
            product = dot_nn(normed, weights[:, at : at + 2 * LANES])
            for half in range(2):
                pair = product[:, half * LANES : (half + 1) * LANES]
                column = at + half * LANES
                if column < QUERY_END + KV * HD:
                    pair = turn(pair, cosine, sine)
                pair = pair.astype(BF16)
                if column < QUERY_END:
                    target, head = q_ref, column // HD
                elif column < QUERY_END + KV * HD:
                    target, head = k_ref, (column - QUERY_END) // HD
                else:
                    target, head = v_ref, (column - QUERY_END - KV * HD) // HD
                target[head] = pair[:, :HD]
                target[head + 1] = pair[:, HD:]
        length = length_ref[0]

        def attend(j, _):
            for h in range(group_size):
                probs = softmax_of(q_ref[j * group_size + h], k_ref[j], length).astype(BF16)
                heads[j * group_size + h] = dot_nn(probs, v_ref[j]).astype(BF16)
            return 0

        lax.fori_loop(0, KV, attend, 0)
        for pair in range(H // 2):
            mixed_ref[:, pair * LANES : (pair + 1) * LANES] = jnp.concatenate(
                [heads[2 * pair], heads[2 * pair + 1]], axis=1
            )
        middle = residual + dot_nn(mixed_ref[...], weights[:, KEYVAL_END:])
        middle_ref[...] = middle
        normed_ref[...] = (unit_rows(middle)[0] * gains_ref[1:2, :]).astype(BF16)
        keep.wait()

    vmem = whole(pltpu.VMEM)
    return pl.pallas_call(
        kernel,
        name="attention_front",
        out_shape=(
            jax.ShapeDtypeStruct((count, D), BF16),
            jax.ShapeDtypeStruct((count, D), F32),
            jax.ShapeDtypeStruct((count, H * HD), BF16),
            jax.ShapeDtypeStruct((H, count, HD), BF16),
            jax.ShapeDtypeStruct((KV, count, HD), BF16),
            jax.ShapeDtypeStruct((KV, count, HD), BF16),
            jax.ShapeDtypeStruct((D, ALL_COLS * BLOCK), BF16),
        ),
        in_specs=[whole(pltpu.SMEM)] * 3 + [vmem] * 4 + [whole(pl.ANY)] * len(pieces),
        out_specs=(vmem,) * 6 + (whole(pl.ANY),),
        scratch_shapes=[
            pltpu.VMEM((D, ALL_COLS * BLOCK), BF16),
            pltpu.VMEM((H, count, HD), BF16),
            pltpu.SemaphoreType.DMA((2,)),
        ],
        compiler_params=params(),
        cost_estimate=cost(100),
    )(lengths, block_rows, block_cols, tokens, gains, cosine, sine, *pieces)


def attention_back(lengths, positions, tokens, packed, gains, cosine, sine, middle, mixed, q, k, v, w_all, partials, near):
    count = tokens.shape[0]
    group_size = H // KV
    blocks = positions.shape[0]
    parts = len(partials)

    def kernel(length_ref, position_ref, tokens_ref, packed_ref, gains_ref, cosine_ref, sine_ref, middle_ref, mixed_ref,
               q_ref, k_ref, v_ref, *refs):
        partial_refs = refs[:parts]
        all_ref, input_grad_ref, gain_ref, near_ref, far_ref = refs[parts : parts + 5]
        weights, stage, grad_heads, grad_columns, sems = refs[parts + 5 :]
        bring_out = pltpu.make_async_copy(all_ref.at[:, pl.ds(KEYVAL_END, D)], weights.at[:, pl.ds(KEYVAL_END, D)], sems.at[0])
        bring_in = pltpu.make_async_copy(all_ref.at[:, pl.ds(0, KEYVAL_END)], weights.at[:, pl.ds(0, KEYVAL_END)], sems.at[1])
        bring_out.start()
        bring_in.start()

        def send(first, columns, col_offset):
            def one(i, _):
                place = position_ref[first + i]
                source = block_at(stage, i // columns, col_offset + i % columns)

                @pl.when(place < near)
                def _():
                    pltpu.make_async_copy(source, near_ref.at[place], sems.at[2]).start()

                @pl.when(place >= near)
                def _():
                    pltpu.make_async_copy(source, far_ref.at[place - near], sems.at[2]).start()

                return 0

            lax.fori_loop(0, ACROSS * columns, one, 0, unroll=4)

        grad_normed = partial_refs[0][...].astype(F32)
        for ref in partial_refs[1:]:
            grad_normed = grad_normed + ref[...].astype(F32)
        unit, scale = unit_rows(middle_ref[...])
        gain_ref[1:2, :] = jnp.sum(grad_normed * unit, axis=0, keepdims=True)
        scaled = grad_normed * gains_ref[1:2, :]
        grad_middle = packed_ref[:, :D].astype(F32) + scale * (
            scaled - unit * jnp.mean(scaled * unit, axis=-1, keepdims=True)
        )
        input_grad_ref[...] = grad_middle
        grad_attn = grad_middle.astype(BF16)
        for at in range(0, D, 4 * LANES):
            stage[:, KEYVAL_END + at : KEYVAL_END + at + 4 * LANES] = dot_tn(
                mixed_ref[...], grad_attn[:, at : at + 4 * LANES]
            ).astype(BF16)
        send(ACROSS * (QUERY_COLS + KEYVAL_COLS), OUT_COLS, QUERY_COLS + KEYVAL_COLS)
        bring_out.wait()
        for at in range(0, H * HD, 2 * LANES):
            product = dot_nt(grad_attn, weights[at : at + 2 * LANES, KEYVAL_END:]).astype(BF16)
            for part in range(2 * LANES // HD):
                grad_heads[at // HD + part] = product[:, part * HD : (part + 1) * HD]
        length = length_ref[0]

        def attend(j, _):
            keys, values = k_ref[j], v_ref[j]
            grad_keys = jnp.zeros((count, HD), F32)
            grad_values = jnp.zeros((count, HD), F32)
            for h in range(group_size):
                head = j * group_size + h
                queries, grad_mixed = q_ref[head], grad_heads[head]
                probs = softmax_of(queries, keys, length)
                grad_values = grad_values + dot_tn(probs.astype(BF16), grad_mixed)
                grad_probs = dot_nt(grad_mixed, values)
                inner = jnp.sum(probs * grad_probs, axis=1, keepdims=True)
                grad_scores = (probs * (grad_probs - inner)).astype(BF16)
                grad_columns[head] = dot_nn(grad_scores, keys) * HD ** (-0.5)
                grad_keys = grad_keys + dot_tn(grad_scores, queries)
            grad_columns[H + j] = grad_keys * HD ** (-0.5)
            grad_columns[H + KV + j] = grad_values
            return 0

        lax.fori_loop(0, KV, attend, 0)
        cosine, sine = cosine_ref[...], -sine_ref[...]
        residual = tokens_ref[...].astype(F32)
        unit_one, scale_one = unit_rows(residual)
        normed = (unit_one * gains_ref[0:1, :]).astype(BF16)
        bring_in.wait()
        grad_normed_one = jnp.zeros((count, D), F32)
        for at in range(0, KEYVAL_END, 4 * LANES):
            pairs = []
            for column in range(at, at + 4 * LANES, LANES):
                head = column // HD
                pair = jnp.concatenate([grad_columns[head], grad_columns[head + 1]], axis=1)
                if column < QUERY_END + KV * HD:
                    pair = turn(pair, cosine, sine)
                pairs.append(pair.astype(BF16))
            columns = jnp.concatenate(pairs, axis=1)
            span = slice(at, at + 4 * LANES)
            stage[:, span] = dot_tn(normed, columns).astype(BF16)
            grad_normed_one = grad_normed_one + dot_nt(columns, weights[:, span])
        send(0, QUERY_COLS, 0)
        send(ACROSS * QUERY_COLS, KEYVAL_COLS, QUERY_COLS)
        gain_ref[0:1, :] = jnp.sum(grad_normed_one * unit_one, axis=0, keepdims=True)
        scaled_one = grad_normed_one * gains_ref[0:1, :]
        input_grad_ref[...] += scale_one * (
            scaled_one - unit_one * jnp.mean(scaled_one * unit_one, axis=-1, keepdims=True)
        )
        pltpu.make_async_copy(stage, stage, sems.at[2]).wait()

    vmem, any_space = whole(pltpu.VMEM), whole(pl.ANY)
    return pl.pallas_call(
        kernel,
        name="attention_back",
        out_shape=(
            jax.ShapeDtypeStruct((count, D), F32),
            jax.ShapeDtypeStruct((2, D), F32),
            jax.ShapeDtypeStruct((near, BLOCK, BLOCK), BF16),
            jax.ShapeDtypeStruct((max(blocks - near, 1), BLOCK, BLOCK), BF16),
        ),
        in_specs=[whole(pltpu.SMEM)] * 2 + [vmem] * (10 + parts) + [any_space],
        out_specs=(vmem, vmem, any_space, any_space),
        scratch_shapes=[
            pltpu.VMEM((D, ALL_COLS * BLOCK), BF16),
            pltpu.VMEM((D, ALL_COLS * BLOCK), BF16),
            pltpu.VMEM((H, count, HD), BF16),
            pltpu.VMEM((H + 2 * KV, count, HD), F32),
            pltpu.SemaphoreType.DMA((3,)),
        ],
        compiler_params=params(),
        cost_estimate=cost(400),
    )(lengths, positions, tokens, packed, gains, cosine, sine, middle, mixed, q, k, v, *partials, w_all)


def split_low(values):
    high = values.astype(BF16)
    return high, (values - high.astype(F32)).astype(BF16)


def shampoo(gradient, statistics, inverse_roots, master):
    terms = len(gradient)
    slots = master.shape[0]
    many = next(n for n in (6, 4, 3, 2, 1) if slots % n == 0)

    def kernel(*refs):
        term_refs = refs[:terms]
        stats_ref, roots_ref, master_ref, grad_ref, stats_out, master_out = refs[terms:]
        for i in range(many):
            total = term_refs[0][i].astype(F32)
            for ref in term_refs[1:]:
                total = total + ref[i].astype(F32)
            low = total.astype(BF16)
            grad = low.astype(F32)
            grad_ref[i] = grad
            scale = 0.5 / (jnp.mean(grad * grad) + 1e-06)
            stats_out[i, 0] = 0.5 * stats_ref[i, 0] + scale * dot_nt(low, low)
            stats_out[i, 1] = 0.5 * stats_ref[i, 1] + scale * dot_tn(low, low)
            left_high, left_low = split_low(roots_ref[i, 0])
            turned_high, turned_low = split_low(dot_nn(left_high, low) + dot_nn(left_low, low))
            right_high, right_low = split_low(roots_ref[i, 1])
            turned = (
                dot_nn(turned_high, right_high)
                + dot_nn(turned_low, right_high)
                + dot_nn(turned_high, right_low)
            )
            direction = turned * lax.rsqrt(jnp.mean(turned * turned) + 1e-06)
            own = master_ref[i]
            spread = jnp.sqrt(jnp.mean(own * own))
            master_out[i] = own - STEP_SIZE * spread * direction

    one = pl.BlockSpec((many, BLOCK, BLOCK), lambda i: (i, 0, 0))
    two = pl.BlockSpec((many, 2, BLOCK, BLOCK), lambda i: (i, 0, 0, 0))
    return pl.pallas_call(
        kernel,
        name="shampoo",
        grid=(slots // many,),
        out_shape=(
            jax.ShapeDtypeStruct((slots, BLOCK, BLOCK), F32),
            jax.ShapeDtypeStruct((slots, 2, BLOCK, BLOCK), F32),
            jax.ShapeDtypeStruct((slots, BLOCK, BLOCK), F32),
        ),
        in_specs=[one] * terms + [two, two, one],
        out_specs=(one, two, one),
        compiler_params=params(dimension_semantics=("arbitrary",)),
        cost_estimate=cost(10),
    )(*gradient, statistics, inverse_roots, master)


def move(array, pairs):
    return lax.ppermute(array, "shard", pairs)


def sibling(array):
    return move(array, [(i, i ^ 1) for i in range(lax.axis_size("shard"))])


def along(array, distance):
    size = lax.axis_size("shard")
    return move(array, [(i, (i + 2 * distance) % size) for i in range(size)])


def two_ways(array, other_first):
    one, two = swap(array, 1), swap(array, 2)
    three = swap(two, 1) if other_first else swap(one, 2)
    return one, two, three


def gather_attention(own, deal, before):
    size, groups = lax.axis_size("shard"), lax.axis_size("expert")
    slots = own.shape[0]
    by_device = deal.reshape(groups, size, slots)
    if groups != 4 or size != 8:
        return [lax.all_gather(own, ("expert", "shard"), axis=0, tiled=True)], deal, before
    me_e, me_s = lax.axis_index("expert"), lax.axis_index("shard")
    pieces, names, far_names = [], [], []
    lines = [along(own, d) for d in range(1, size // 2)]
    fours = [jnp.concatenate([own, *two_ways(own, False)], axis=0)]
    lines, before = lax.optimization_barrier((lines, before))
    fours += [jnp.concatenate([line, *two_ways(line, d % 2 == 0)], axis=0) for d, line in enumerate(lines)]
    for d, four in enumerate(fours):
        pieces.append(four)
        source = (me_s - 2 * d) % size
        for m in range(groups):
            names.append(by_device[me_e ^ m, source])
            far_names.append(by_device[me_e ^ m, source ^ 1])
    pieces += [sibling(piece) for piece in pieces]
    return pieces, jnp.concatenate(names + far_names), before


def attention_positions(deal, slots):
    size, groups = lax.axis_size("shard"), lax.axis_size("expert")
    inverse = inverse_of(deal)
    if groups != 4 or size != 8:
        return inverse
    owner, within = inverse // slots, inverse % slots
    mask = (owner // size) ^ lax.axis_index("expert")
    me = lax.axis_index("shard")
    core = (owner % 2) ^ (me % 2)
    distance = ((owner % size) // 2 - me // 2) % (size // 2)
    return ((((core * groups + mask) * (size // 2)) + distance) * slots + within).astype(jnp.int32)


def add_low(left, right):
    return (left.astype(F32) + right.astype(F32)).astype(BF16)


def scatter_attention(near, far, slots):
    size, groups = lax.axis_size("shard"), lax.axis_size("expert")
    if groups != 4 or size != 8:
        return [lax.psum_scatter(near, ("expert", "shard"), scatter_dimension=0, tiled=True)]
    half = size // 4
    total = add_low(near, sibling(far)).reshape(groups, 2, half * slots, BLOCK, BLOCK)
    lines = []
    for part, (first, second) in enumerate(((1, 2), (2, 1))):
        mine = jnp.concatenate([total[0, part], total[second, part]], axis=0)
        theirs = jnp.concatenate([total[first, part], total[3, part]], axis=0)
        mine = add_low(mine, swap(theirs, first))
        mine, theirs = mine[: half * slots], mine[half * slots :]
        lines.append(add_low(mine, swap(theirs, second)))
    terms = [line[i * slots : (i + 1) * slots] for line in lines for i in range(half)]
    return [terms[0]] + [along(terms[d], d) for d in range(1, size // 2)]


def sum_everywhere(values):
    size, groups = lax.axis_size("shard"), lax.axis_size("expert")
    if groups != 4 or size != 8:
        return lax.psum(values, ("expert", "shard"))
    for mask in (1, 2, 4):
        values = values + move(values, [(i, i ^ mask) for i in range(size)])
    for mask in (1, 2):
        values = values + swap(values, mask)
    return values


def swap(array, mask):
    if mask == 0:
        return array
    return lax.ppermute(array, "expert", [(i, i ^ mask) for i in range(lax.axis_size("expert"))])


def per_device(
    tokens,
    cotangent,
    lengths,
    routes,
    route_gates,
    norm_gains,
    attn_master,
    attn_stats,
    attn_roots,
    attn_deal,
    expert_master,
    expert_stats,
    expert_roots,
    expert_deal,
):
    row_count = tokens.shape[0]
    groups = lax.axis_size("expert")
    group = lax.axis_index("expert").astype(jnp.int32).reshape(1)
    expert_all = lax.all_gather(expert_master.astype(BF16), "shard", axis=0, tiled=True)
    places = jnp.arange(row_count)
    valid_rows = places < lengths[0]
    grad_low = jnp.where(valid_rows[:, None], cotangent, jnp.zeros_like(cotangent))
    expert_lane = jnp.arange(LANES, dtype=jnp.int32)
    weights_row = sum(
        jnp.where(routes[:, k, None] == expert_lane, route_gates[:, k, None], jnp.zeros((), BF16))
        for k in range(TOP)
    )
    packed = jnp.concatenate([grad_low, weights_row], axis=1)
    packed = [swap(packed, m) for m in range(groups)]
    pieces, natural, packed[1:3] = gather_attention(attn_master.astype(BF16), attn_deal, packed[1:3])
    cosine, sine = rope_tables(jnp.arange(row_count, dtype=F32))
    cosine = jnp.concatenate([cosine] * 4, axis=1)
    sine = jnp.concatenate([-sine, sine] * 2, axis=1)
    block_rows, block_cols = attention_places(natural)
    normed_two, middle, mixed, q, k, v, w_all = attention_front(
        lengths, block_rows, block_cols, tokens, norm_gains, cosine, sine, pieces
    )
    rows = [swap(normed_two, m) for m in range(groups)]
    expert_inverse = inverse_of(expert_deal[0])
    hidden, both, partials, w_down = expert_front(group, expert_inverse, expert_all, rows, packed)
    partials = [swap(partial, m) for m, partial in enumerate(partials)]
    expert_term = expert_weight_grads(expert_inverse, rows, packed, hidden, both)
    moe_parts = expert_outputs(hidden, w_down)
    mixed, moe_parts = lax.optimization_barrier((mixed, moe_parts))
    moe_parts = [swap(part, m) for m, part in enumerate(moe_parts)]
    slots = attn_master.shape[0]
    positions = attention_positions(attn_deal, slots)
    near = positions.shape[0] // (2 if groups == 4 and lax.axis_size("shard") == 8 else 1)
    input_grad, gain_parts, near_blocks, far_blocks = attention_back(
        lengths, positions, tokens, packed[0], norm_gains, cosine, sine, middle, mixed, q, k, v, w_all, partials, near
    )
    near_blocks, far_blocks, moe_parts = lax.optimization_barrier((near_blocks, far_blocks, moe_parts))
    output = (middle + sum(part.astype(F32) for part in moe_parts)).astype(BF16)
    attn_terms = scatter_attention(near_blocks, far_blocks, slots)
    expert_term = lax.psum_scatter(expert_term, "shard", scatter_dimension=0, tiled=True)
    gain_grads = sum_everywhere(gain_parts)
    new_gains = norm_gains - STEP_SIZE * gain_grads * lax.rsqrt(
        jnp.mean(gain_grads * gain_grads, axis=-1, keepdims=True) + 1e-06
    )
    expert_grads, expert_stats_new, expert_new = shampoo(
        [expert_term], expert_stats, expert_roots, expert_master
    )
    attn_terms, expert_new = lax.optimization_barrier((attn_terms, expert_new))
    attn_grads, attn_stats_new, attn_new = shampoo(attn_terms, attn_stats, attn_roots, attn_master)
    return (
        output,
        input_grad,
        gain_grads,
        new_gains,
        attn_grads,
        attn_stats_new,
        attn_new,
        expert_grads,
        expert_stats_new,
        expert_new,
    )


def solution(mesh):
    in_specs = (
        P(("expert", "shard"), None),
        P(("expert", "shard"), None),
        P(("expert", "shard")),
        P(("expert", "shard"), None),
        P(("expert", "shard"), None),
        P(),
        P(("expert", "shard"), None, None),
        P(("expert", "shard"), None, None, None),
        P(("expert", "shard"), None, None, None),
        P(),
        P(("expert", "shard"), None, None),
        P(("expert", "shard"), None, None, None),
        P(("expert", "shard"), None, None, None),
        P("expert", None),
    )
    out_specs = (
        P(("expert", "shard"), None),
        P(("expert", "shard"), None),
        P(),
        P(),
        P(("expert", "shard"), None, None),
        P(("expert", "shard"), None, None, None),
        P(("expert", "shard"), None, None),
        P(("expert", "shard"), None, None),
        P(("expert", "shard"), None, None, None),
        P(("expert", "shard"), None, None),
    )
    return jax.shard_map(
        per_device, mesh=mesh, in_specs=in_specs, out_specs=out_specs, check_vma=False
    )
```

```python
import jax
import jax.numpy as jnp
from jax import lax
from jax.experimental import pallas as pl
from jax.experimental.pallas import tpu as pltpu
from jax.sharding import PartitionSpec as P

D = 1536
H = 24
KV = 8
HD = 64
FF = 512
TOP = 8
BLOCK = 128
EXP_DEV = 4
LANES = 128
VMEM_BYTES = 63 * 1024 * 1024
BF16 = jnp.bfloat16
F32 = jnp.float32


EPSILON = 1e-05
STEP_SIZE = 0.3


QUERY_END = H * HD
KEYVAL_END = QUERY_END + 2 * KV * HD
ACROSS = D // BLOCK
QUERY_COLS = QUERY_END // BLOCK
KEYVAL_COLS = (KEYVAL_END - QUERY_END) // BLOCK
OUT_COLS = D // BLOCK
ALL_COLS = QUERY_COLS + KEYVAL_COLS + OUT_COLS


def rope_tables(positions):
    frequency = 10000.0 ** (-2.0 * jnp.arange(HD // 2, dtype=jnp.float32) / HD)
    angles = positions[:, None] * frequency[None, :]
    return (jnp.cos(angles), jnp.sin(angles))


def dot_nn(left, right):
    return lax.dot_general(left, right, (((1,), (0,)), ((), ())), preferred_element_type=F32)


def dot_nt(left, right):
    return lax.dot_general(left, right, (((1,), (1,)), ((), ())), preferred_element_type=F32)


def dot_tn(left, right):
    return lax.dot_general(left, right, (((0,), (0,)), ((), ())), preferred_element_type=F32)


def params(**more):
    return pltpu.CompilerParams(vmem_limit_bytes=VMEM_BYTES, **more)


def cost(microseconds):
    return pl.CostEstimate(flops=int(microseconds * 1.15e9), bytes_accessed=1024, transcendentals=0)


def whole(memory_space):
    return pl.BlockSpec(memory_space=memory_space)


def held(shape):
    return pl.BlockSpec(shape, lambda *_: (0,) * len(shape))


def inverse_of(dealing):
    place = jnp.arange(dealing.shape[0], dtype=jnp.int32)
    return jnp.sum(jnp.where(dealing[None, :] == place[:, None], place[None, :], 0), axis=1)


def weight_of(packed, expert):
    lane = lax.broadcasted_iota(jnp.int32, packed.shape, 1)
    return jnp.sum(jnp.where(lane == expert, packed.astype(F32), 0.0), axis=1, keepdims=True)


def aligned(block):
    return block * BLOCK if isinstance(block, int) else pl.multiple_of(block * BLOCK, BLOCK)


def block_at(ref, row, col):
    return ref.at[
        pl.ds(aligned(row), BLOCK),
        pl.ds(aligned(col), BLOCK),
    ]


def stacked_copies(sources, target, sem):
    count = sources[0].shape[-2]
    return [
        pltpu.make_async_copy(
            source, target.at[pl.ds(i * count, count), :], sem
        )
        for i, source in enumerate(sources)
    ]


def expert_step(weight, rows, packed, matrix):
    gate_up = dot_nn(rows[...], matrix[:, : 2 * FF])
    grad_hidden = dot_nt(packed[:, :FF], matrix[:FF, 2 * FF :])
    for at in range(FF, D, FF):
        grad_hidden = grad_hidden + dot_nt(packed[:, at : at + FF], matrix[at : at + FF, 2 * FF :])
    gate, up = gate_up[:, :FF], gate_up[:, FF:]
    sigmoid = 0.5 * jnp.tanh(0.5 * gate) + 0.5
    silu = gate * sigmoid
    hidden = (silu * up * weight).astype(BF16)
    slope = grad_hidden * sigmoid * weight
    both = jnp.concatenate(
        [(slope * up * (1.0 + gate - silu)).astype(BF16), (slope * gate).astype(BF16)], axis=1
    )
    return hidden, both


def expert_front(group, inverse, blocks, rows, packed):
    parts = len(rows)
    count = rows[0].shape[0]
    across, wide, tall = D // BLOCK, 2 * FF // BLOCK, FF // BLOCK
    first, second = across * wide, tall * across

    def kernel(group_ref, inverse_ref, blocks_ref, *refs):
        refs = list(refs)
        take = lambda n: [refs.pop(0) for _ in range(n)]
        rows_refs, packed_refs = take(parts), take(len(packed))
        hidden_refs, both_refs = take(parts), take(parts)
        out_ref, kept_ref, rows_all, packed_all, total, matrices, block_sems, keep_sems, sems = refs
        step = pl.program_id(0)
        half = step % 2

        def bring(expert, half):
            base = expert * (first + second)

            for i in range(first + second):
                row, col = i // wide, i % wide
                if i >= first:
                    down = (i - first) % across
                    row, col = down // tall * tall + (i - first) // across, wide + down % tall
                pltpu.make_async_copy(
                    blocks_ref.at[inverse_ref[base + i]],
                    block_at(matrices.at[half], row, col),
                    block_sems.at[half],
                ).start()

        def keep(expert, half):
            return pltpu.make_async_copy(matrices.at[half], kept_ref.at[expert], keep_sems.at[half])

        loads = [
            load
            for i in range(parts)
            for load in [pltpu.make_async_copy(rows_refs[i], rows_all.at[i], sems.at[0, i])]
            + stacked_copies([ref.at[group_ref[0] ^ i] for ref in packed_refs], packed_all.at[i], sems.at[1, i])
        ]

        @pl.when(step == 0)
        def _():
            for load in loads[:3]:
                load.start()
            bring(0, 0)
            for load in loads[3:]:
                load.start()

        @pl.when(step > 0)
        def _():
            keep(step - 1, 1 - half).wait()

        @pl.when(step < EXP_DEV - 1)
        def _():
            bring(step + 1, 1 - half)

        matrix = matrices.at[half]
        pltpu.make_async_copy(matrix, matrix, block_sems.at[half]).wait()
        keep(step, half).start()

        @pl.when(step == 0)
        def _():
            total[...] = jnp.zeros_like(total)
            for load in loads:
                load.wait()

        for i in range(parts):
            weight = weight_of(packed_all[i, :, D:], group_ref[0] * EXP_DEV + step)
            hidden, both = expert_step(weight, rows_all.at[i], packed_all.at[i], matrix)
            hidden_refs[i][0] = hidden
            both_refs[i][0] = both
            if i > 0:
                total[i - 1] += dot_nt(both, matrix[:, : 2 * FF])

        @pl.when(step == EXP_DEV - 1)
        def _():
            for i in range(1, parts):
                out_ref[group_ref[0] ^ i] = total[i - 1].astype(BF16)
            keep(step, half).wait()

    any_space, smem = whole(pl.ANY), whole(pltpu.SMEM)
    out = pl.pallas_call(
        kernel,
        name="expert_front",
        grid=(EXP_DEV,),
        out_shape=(
            [jax.ShapeDtypeStruct((EXP_DEV, count, FF), BF16)] * parts
            + [jax.ShapeDtypeStruct((EXP_DEV, count, 2 * FF), BF16)] * parts
            + [jax.ShapeDtypeStruct((parts, count, D), BF16)]
            + [jax.ShapeDtypeStruct((EXP_DEV, D, 3 * FF), BF16)]
        ),
        in_specs=[smem] * 2 + [any_space] * (1 + parts + len(packed)),
        out_specs=(
            [pl.BlockSpec((1, count, FF), lambda j: (j, 0, 0))] * parts
            + [pl.BlockSpec((1, count, 2 * FF), lambda j: (j, 0, 0))] * parts
            + [held((parts, count, D))]
            + [any_space]
        ),
        scratch_shapes=[
            pltpu.VMEM((parts, count, D), BF16),
            pltpu.VMEM((parts, count, D + LANES), BF16),
            pltpu.VMEM((parts - 1, count, D), F32),
            pltpu.VMEM((2, D, 3 * FF), BF16),
            pltpu.SemaphoreType.DMA((2,)),
            pltpu.SemaphoreType.DMA((2,)),
            pltpu.SemaphoreType.DMA((2, parts)),
        ],
        compiler_params=params(dimension_semantics=("arbitrary",)),
        cost_estimate=cost(100),
    )(group, inverse, blocks, *rows, *packed)
    return out[:parts], out[parts : 2 * parts], out[-2], out[-1]


def expert_weight_grads(group, positions, rows, packed, hidden, both):
    parts = len(rows)
    count = rows[0].shape[0]
    total_rows = parts * count
    slots = positions.shape[0]
    across, wide, tall = D // BLOCK, 2 * FF // BLOCK, FF // BLOCK
    first, second = across * wide, tall * across
    tile = 256

    def kernel(group_ref, position_ref, *refs):
        refs = list(refs)
        take = lambda n: [refs.pop(0) for _ in range(n)]
        rows_refs, packed_refs, hidden_refs, both_refs = take(parts), take(len(packed)), take(parts), take(parts)
        out_ref, rows_all, packed_all, hidden_two, both_two, stage_gateup, stage_down, sems = refs
        step = pl.program_id(0)
        half = step % 2
        base = step * (first + second)

        def loads(expert, half):
            return stacked_copies([r.at[expert] for r in hidden_refs], hidden_two.at[half], sems.at[2 + half]) + stacked_copies(
                [r.at[expert] for r in both_refs], both_two.at[half], sems.at[4 + half]
            )

        once = stacked_copies(rows_refs, rows_all, sems.at[6]) + stacked_copies(
            [ref.at[group_ref[0] ^ i] for i in range(parts) for ref in packed_refs], packed_all, sems.at[7]
        )

        @pl.when(step == 0)
        def _():
            for load in once[:parts] + loads(0, 0) + once[parts:]:
                load.start()

        for load in loads(step, half):
            load.wait()

        @pl.when(step < EXP_DEV - 1)
        def _():
            for load in loads(step + 1, 1 - half):
                load.start()

        @pl.when(step == 0)
        def _():
            for load in once[:parts]:
                load.wait()

        def wait_gateup():
            pltpu.make_async_copy(stage_gateup, stage_gateup, sems.at[0]).wait()

        def wait_down():
            pltpu.make_async_copy(stage_down, stage_down, sems.at[1]).wait()

        def send(stage, sem, start, blocks, columns):
            for i in range(blocks):
                pltpu.make_async_copy(
                    block_at(stage, i // columns, i % columns), out_ref.at[position_ref[start + i]], sem
                ).start()

        pl.when(step > 0)(wait_gateup)
        for at in range(0, 2 * FF, tile):
            stage_gateup[:, at : at + tile] = dot_tn(
                rows_all[...], both_two[half, :, at : at + tile]
            ).astype(BF16)
        send(stage_gateup, sems.at[0], base, first, wide)
        pl.when(step > 0)(wait_down)

        @pl.when(step == 0)
        def _():
            for load in once[parts:]:
                load.wait()

        for at in range(0, D, tile):
            stage_down[:, at : at + tile] = dot_tn(
                hidden_two[half], packed_all[:, at : at + tile]
            ).astype(BF16)
        send(stage_down, sems.at[1], base + first, second, across)

        @pl.when(step == EXP_DEV - 1)
        def _():
            wait_gateup()
            wait_down()

    any_space, smem = whole(pl.ANY), whole(pltpu.SMEM)
    return pl.pallas_call(
        kernel,
        name="expert_weight_grads",
        grid=(EXP_DEV,),
        out_shape=jax.ShapeDtypeStruct((slots, BLOCK, BLOCK), BF16),
        in_specs=[smem] * 2 + [any_space] * (3 * parts + len(packed)),
        out_specs=any_space,
        scratch_shapes=[
            pltpu.VMEM((total_rows, D), BF16),
            pltpu.VMEM((total_rows, D + LANES), BF16),
            pltpu.VMEM((2, total_rows, FF), BF16),
            pltpu.VMEM((2, total_rows, 2 * FF), BF16),
            pltpu.VMEM((D, 2 * FF), BF16),
            pltpu.VMEM((FF, D), BF16),
            pltpu.SemaphoreType.DMA((8,)),
        ],
        compiler_params=params(dimension_semantics=("arbitrary",)),
        cost_estimate=cost(100),
    )(group, positions, *rows, *packed, *hidden, *both)


def expert_route(both, matrices):
    count = both.shape[1]

    def kernel(both_ref, matrix_ref, out_ref):
        out_ref[...] = sum(
            dot_nt(both_ref[expert], matrix_ref[expert]) for expert in range(EXP_DEV)
        ).astype(BF16)

    return pl.pallas_call(
        kernel,
        name="expert_route",
        grid=(D // FF,),
        out_shape=jax.ShapeDtypeStruct((count, D), BF16),
        in_specs=[
            held((EXP_DEV, count, 2 * FF)),
            pl.BlockSpec((EXP_DEV, FF, 2 * FF), lambda j: (0, j, 0)),
        ],
        out_specs=pl.BlockSpec((count, FF), lambda j: (0, j)),
        compiler_params=params(dimension_semantics=("arbitrary",)),
        cost_estimate=cost(4),
    )(both, matrices)


def expert_outputs(group, hidden, matrices):
    parts = len(hidden)
    count = hidden[0].shape[1]

    def kernel(group_ref, *refs):
        hidden_refs, matrix_ref, out_ref = refs[:parts], refs[parts], refs[parts + 1]
        for i, hidden_ref in enumerate(hidden_refs):
            out_ref[group_ref[0] ^ i] = sum(
                dot_nn(hidden_ref[expert], matrix_ref[expert]) for expert in range(EXP_DEV)
            ).astype(BF16)

    return pl.pallas_call(
        kernel,
        name="expert_outputs",
        grid=(D // FF,),
        out_shape=jax.ShapeDtypeStruct((parts, count, D), BF16),
        in_specs=[whole(pltpu.SMEM)] + [held((EXP_DEV, count, FF))] * parts
        + [pl.BlockSpec((EXP_DEV, FF, FF), lambda j: (0, j, 2))],
        out_specs=pl.BlockSpec((parts, count, FF), lambda j: (0, 0, j)),
        compiler_params=params(dimension_semantics=("arbitrary",)),
        cost_estimate=cost(300),
    )(group, *hidden, matrices)


def attention_places(natural):
    first = ACROSS * QUERY_COLS
    second = first + ACROSS * KEYVAL_COLS
    in_keyval, in_out = natural - first, natural - second
    row = jnp.where(
        natural < first,
        natural // QUERY_COLS,
        jnp.where(natural < second, in_keyval // KEYVAL_COLS, in_out // OUT_COLS),
    )
    col = jnp.where(
        natural < first,
        natural % QUERY_COLS,
        jnp.where(
            natural < second,
            QUERY_COLS + in_keyval % KEYVAL_COLS,
            QUERY_COLS + KEYVAL_COLS + in_out % OUT_COLS,
        ),
    )
    return row.astype(jnp.int32), col.astype(jnp.int32)


def turn(values, cosine, sine):
    lane = lax.broadcasted_iota(jnp.int32, values.shape, 1)
    partner = jnp.where(
        lane % HD < HD // 2,
        pltpu.roll(values, LANES - HD // 2, 1),
        pltpu.roll(values, HD // 2, 1),
    )
    return values * cosine + partner * sine


def score_bias(length, first, heads, columns):
    shape = (heads * BLOCK, columns)
    at_row = first + lax.broadcasted_iota(jnp.int32, shape, 0) % BLOCK
    at_col = lax.broadcasted_iota(jnp.int32, shape, 1)
    return jnp.where((at_col <= at_row) & (at_col < length), 0.0, -1e30)


def softmax_of(queries, keys, bias):
    scores = dot_nt(queries, keys) + bias
    weights = jnp.exp(scores - jnp.max(scores, axis=1, keepdims=True))
    return weights * (1.0 / jnp.sum(weights, axis=1, keepdims=True))


def head_rows(ref, head, heads, first):
    return ref[pl.ds(head, heads), first : first + BLOCK, :].reshape(heads * BLOCK, HD)


def unit_rows(values):
    scale = lax.rsqrt(jnp.mean(values * values, axis=-1, keepdims=True) + EPSILON)
    return values * scale, scale


def attention_front(lengths, block_rows, block_cols, tokens, gains, cosine, sine, pieces):
    count = tokens.shape[0]
    group_size = H // KV

    def kernel(length_ref, row_ref, col_ref, tokens_ref, gains_ref, cosine_ref, sine_ref, *refs):
        piece_refs = refs[: len(pieces)]
        normed_ref, middle_ref, mixed_ref, q_ref, k_ref, v_ref, all_ref = refs[len(pieces) : -4]
        weights, heads, bias_ref, sems = refs[-4:]
        offset = 0
        for piece in piece_refs:

            def bring(i, _, piece=piece, offset=offset):
                pltpu.make_async_copy(
                    piece.at[i],
                    block_at(weights, row_ref[offset + i], col_ref[offset + i]),
                    sems.at[0],
                ).start()
                return 0

            lax.fori_loop(0, piece.shape[0], bring, 0, unroll=4)
            offset += piece.shape[0]
        residual = tokens_ref[...].astype(F32)
        normed = (unit_rows(residual)[0] * gains_ref[0:1, :]).astype(BF16)
        pltpu.make_async_copy(weights, weights, sems.at[0]).wait()
        keep = pltpu.make_async_copy(weights, all_ref, sems.at[1])
        keep.start()
        cosine, sine = cosine_ref[...], sine_ref[...]
        for at in range(0, KEYVAL_END, 2 * LANES):
            product = dot_nn(normed, weights[:, at : at + 2 * LANES])
            for half in range(2):
                pair = product[:, half * LANES : (half + 1) * LANES]
                column = at + half * LANES
                if column < QUERY_END + KV * HD:
                    pair = turn(pair, cosine, sine)
                if column < QUERY_END:
                    pair = pair * HD ** (-0.5)
                pair = pair.astype(BF16)
                if column < QUERY_END:
                    target, head = q_ref, column // HD
                elif column < QUERY_END + KV * HD:
                    target, head = k_ref, (column - QUERY_END) // HD
                else:
                    target, head = v_ref, (column - QUERY_END - KV * HD) // HD
                target[head] = pair[:, :HD]
                target[head + 1] = pair[:, HD:]
        for first in range(0, count, BLOCK):
            bias_ref[first // BLOCK] = score_bias(length_ref[0], first, group_size, count)

        def attend(j, _):
            for first in range(0, count, BLOCK):
                seen = slice(0, first + BLOCK)
                probs = softmax_of(
                    head_rows(q_ref, j * group_size, group_size, first),
                    k_ref[j, seen],
                    bias_ref[first // BLOCK, :, seen],
                ).astype(BF16)
                heads[pl.ds(j * group_size, group_size), first : first + BLOCK, :] = (
                    dot_nn(probs, v_ref[j, seen]).astype(BF16).reshape(group_size, BLOCK, HD)
                )
            return 0

        lax.fori_loop(0, KV, attend, 0, unroll=2)
        for pair in range(H // 2):
            mixed_ref[:, pair * LANES : (pair + 1) * LANES] = jnp.concatenate(
                [heads[2 * pair], heads[2 * pair + 1]], axis=1
            )
        middle = residual + dot_nn(mixed_ref[...], weights[:, KEYVAL_END:])
        middle_ref[...] = middle
        normed_ref[...] = (unit_rows(middle)[0] * gains_ref[1:2, :]).astype(BF16)
        keep.wait()

    vmem = whole(pltpu.VMEM)
    return pl.pallas_call(
        kernel,
        name="attention_front",
        out_shape=(
            jax.ShapeDtypeStruct((count, D), BF16),
            jax.ShapeDtypeStruct((count, D), F32),
            jax.ShapeDtypeStruct((count, H * HD), BF16),
            jax.ShapeDtypeStruct((H, count, HD), BF16),
            jax.ShapeDtypeStruct((KV, count, HD), BF16),
            jax.ShapeDtypeStruct((KV, count, HD), BF16),
            jax.ShapeDtypeStruct((D, ALL_COLS * BLOCK), BF16),
        ),
        in_specs=[whole(pltpu.SMEM)] * 3 + [vmem] * 4 + [whole(pl.ANY)] * len(pieces),
        out_specs=(vmem,) * 6 + (whole(pl.ANY),),
        scratch_shapes=[
            pltpu.VMEM((D, ALL_COLS * BLOCK), BF16),
            pltpu.VMEM((H, count, HD), BF16),
            pltpu.VMEM((count // BLOCK, group_size * BLOCK, count), F32),
            pltpu.SemaphoreType.DMA((2,)),
        ],
        compiler_params=params(),
        cost_estimate=cost(100),
    )(lengths, block_rows, block_cols, tokens, gains, cosine, sine, *pieces)


def attention_back(lengths, positions, tokens, packed, gains, cosine, sine, middle, mixed, q, k, v, w_all, group, own, partials, near):
    count = tokens.shape[0]
    group_size = H // KV
    blocks = positions.shape[0]
    parts = partials.shape[0]

    def kernel(group_ref, length_ref, position_ref, tokens_ref, packed_ref, gains_ref, cosine_ref, sine_ref, middle_ref, mixed_ref,
               q_ref, k_ref, v_ref, *refs):
        own_ref, partial_ref, all_ref, input_grad_ref, gain_ref, near_ref, far_ref = refs[:7]
        weights, stage, grad_heads, grad_columns, bias_ref, sems = refs[7:]
        bring_out = pltpu.make_async_copy(all_ref.at[:, pl.ds(KEYVAL_END, D)], weights.at[:, pl.ds(KEYVAL_END, D)], sems.at[0])
        bring_in = pltpu.make_async_copy(all_ref.at[:, pl.ds(0, KEYVAL_END)], weights.at[:, pl.ds(0, KEYVAL_END)], sems.at[1])
        bring_out.start()
        bring_in.start()

        def send(first, columns, col_offset):
            def one(i, _):
                place = position_ref[first + i]
                source = block_at(stage, i // columns, col_offset + i % columns)

                @pl.when(place < near)
                def _():
                    pltpu.make_async_copy(source, near_ref.at[place], sems.at[2]).start()

                @pl.when(place >= near)
                def _():
                    pltpu.make_async_copy(source, far_ref.at[place - near], sems.at[2]).start()

                return 0

            lax.fori_loop(0, ACROSS * columns, one, 0, unroll=4)

        grad_normed = own_ref[...].astype(F32)
        for i in range(1, parts):
            grad_normed = grad_normed + partial_ref[group_ref[0] ^ i].astype(F32)
        unit, scale = unit_rows(middle_ref[...])
        gain_ref[1:2, :] = jnp.sum(grad_normed * unit, axis=0, keepdims=True)
        scaled = grad_normed * gains_ref[1:2, :]
        grad_middle = packed_ref[:, :D].astype(F32) + scale * (
            scaled - unit * jnp.mean(scaled * unit, axis=-1, keepdims=True)
        )
        input_grad_ref[...] = grad_middle
        grad_attn = grad_middle.astype(BF16)
        for at in range(0, D, 4 * LANES):
            stage[:, KEYVAL_END + at : KEYVAL_END + at + 4 * LANES] = dot_tn(
                mixed_ref[...], grad_attn[:, at : at + 4 * LANES]
            ).astype(BF16)
        send(ACROSS * (QUERY_COLS + KEYVAL_COLS), OUT_COLS, QUERY_COLS + KEYVAL_COLS)
        bring_out.wait()
        for at in range(0, H * HD, 2 * LANES):
            product = dot_nt(grad_attn, weights[at : at + 2 * LANES, KEYVAL_END:]).astype(BF16)
            for part in range(2 * LANES // HD):
                grad_heads[at // HD + part] = product[:, part * HD : (part + 1) * HD]
        for first in range(0, count, BLOCK):
            bias_ref[first // BLOCK] = score_bias(length_ref[0], first, group_size, count)

        def attend(j, _):
            blocks_here = count // BLOCK
            grad_keys, grad_values = [0.0] * blocks_here, [0.0] * blocks_here
            for block in range(blocks_here):
                first = block * BLOCK
                seen = slice(0, first + BLOCK)
                keys, values = k_ref[j, seen], v_ref[j, seen]
                queries = head_rows(q_ref, j * group_size, group_size, first)
                grad_mixed = head_rows(grad_heads, j * group_size, group_size, first)
                probs = softmax_of(queries, keys, bias_ref[block, :, seen])
                more_values = dot_tn(probs.astype(BF16), grad_mixed)
                grad_probs = dot_nt(grad_mixed, values)
                inner = jnp.sum(probs * grad_probs, axis=1, keepdims=True)
                grad_scores = (probs * (grad_probs - inner)).astype(BF16)
                grad_columns[pl.ds(j * group_size, group_size), first : first + BLOCK, :] = (
                    dot_nn(grad_scores, keys) * HD ** (-0.5)
                ).reshape(group_size, BLOCK, HD)
                more_keys = dot_tn(grad_scores, queries)
                for i in range(block + 1):
                    rows = slice(i * BLOCK, (i + 1) * BLOCK)
                    grad_keys[i] = grad_keys[i] + more_keys[rows]
                    grad_values[i] = grad_values[i] + more_values[rows]
            for i in range(blocks_here):
                rows = slice(i * BLOCK, (i + 1) * BLOCK)
                grad_columns[H + j, rows] = grad_keys[i]
                grad_columns[H + KV + j, rows] = grad_values[i]
            return 0

        lax.fori_loop(0, KV, attend, 0, unroll=2)
        cosine, sine = cosine_ref[...], -sine_ref[...]
        residual = tokens_ref[...].astype(F32)
        unit_one, scale_one = unit_rows(residual)
        normed = (unit_one * gains_ref[0:1, :]).astype(BF16)
        bring_in.wait()
        grad_normed_one = jnp.zeros((count, D), F32)
        for at in range(0, KEYVAL_END, 4 * LANES):
            pairs = []
            for column in range(at, at + 4 * LANES, LANES):
                head = column // HD
                pair = jnp.concatenate([grad_columns[head], grad_columns[head + 1]], axis=1)
                if column < QUERY_END + KV * HD:
                    pair = turn(pair, cosine, sine)
                pairs.append(pair.astype(BF16))
            columns = jnp.concatenate(pairs, axis=1)
            span = slice(at, at + 4 * LANES)
            stage[:, span] = dot_tn(normed, columns).astype(BF16)
            grad_normed_one = grad_normed_one + dot_nt(columns, weights[:, span])
        send(0, QUERY_COLS, 0)
        send(ACROSS * QUERY_COLS, KEYVAL_COLS, QUERY_COLS)
        gain_ref[0:1, :] = jnp.sum(grad_normed_one * unit_one, axis=0, keepdims=True)
        scaled_one = grad_normed_one * gains_ref[0:1, :]
        input_grad_ref[...] += scale_one * (
            scaled_one - unit_one * jnp.mean(scaled_one * unit_one, axis=-1, keepdims=True)
        )
        pltpu.make_async_copy(stage, stage, sems.at[2]).wait()

    vmem, any_space = whole(pltpu.VMEM), whole(pl.ANY)
    return pl.pallas_call(
        kernel,
        name="attention_back",
        out_shape=(
            jax.ShapeDtypeStruct((count, D), F32),
            jax.ShapeDtypeStruct((2, D), F32),
            jax.ShapeDtypeStruct((near, BLOCK, BLOCK), BF16),
            jax.ShapeDtypeStruct((max(blocks - near, 1), BLOCK, BLOCK), BF16),
        ),
        in_specs=[whole(pltpu.SMEM)] * 3 + [vmem] * 12 + [any_space],
        out_specs=(vmem, vmem, any_space, any_space),
        scratch_shapes=[
            pltpu.VMEM((D, ALL_COLS * BLOCK), BF16),
            pltpu.VMEM((D, ALL_COLS * BLOCK), BF16),
            pltpu.VMEM((H, count, HD), BF16),
            pltpu.VMEM((H + 2 * KV, count, HD), F32),
            pltpu.VMEM((count // BLOCK, group_size * BLOCK, count), F32),
            pltpu.SemaphoreType.DMA((3,)),
        ],
        compiler_params=params(),
        cost_estimate=cost(150),
    )(group, lengths, positions, tokens, packed, gains, cosine, sine, middle, mixed, q, k, v, own, partials, w_all)


def split_low(values):
    high = values.astype(BF16)
    return high, (values - high.astype(F32)).astype(BF16)


def batched(left, right, left_dim, right_dim):
    return lax.dot_general(
        left, right, (((left_dim,), (right_dim,)), ((0,), (0,))), preferred_element_type=F32
    )


def block_mean(values):
    return jnp.mean(values, axis=(1, 2), keepdims=True)


def shampoo(gradient, statistics, inverse_roots, master):
    terms = len(gradient)
    slots = master.shape[0]
    many = max(n for n in range(1, 19) if slots % n == 0 and (n == 1 or slots // n > 1))

    def kernel(*refs):
        stats_ref, roots_ref, master_ref, grad_ref, stats_out, master_out = refs[terms:]
        low = sum(ref[...].astype(F32) for ref in refs[:terms]).astype(BF16)
        grad = low.astype(F32)
        grad_ref[...] = grad
        scale = 0.5 / (block_mean(grad * grad) + 1e-06)
        stats_out[:, 0] = 0.5 * stats_ref[:, 0] + scale * batched(low, low, 2, 2)
        stats_out[:, 1] = 0.5 * stats_ref[:, 1] + scale * batched(low, low, 1, 1)
        left = jnp.concatenate(split_low(roots_ref[:, 0]), axis=2)
        turned = jnp.concatenate(
            split_low(batched(left, jnp.concatenate([low, low], axis=1), 2, 1)), axis=2
        )
        high, rest = split_low(roots_ref[:, 1])
        turned = batched(turned, jnp.concatenate([high, high], axis=1), 2, 1) + batched(
            turned[:, :, :BLOCK], rest, 2, 1
        )
        direction = turned * lax.rsqrt(block_mean(turned * turned) + 1e-06)
        own = master_ref[...]
        master_out[...] = own - STEP_SIZE * jnp.sqrt(block_mean(own * own)) * direction

    one = pl.BlockSpec((many, BLOCK, BLOCK), lambda i: (i, 0, 0))
    two = pl.BlockSpec((many, 2, BLOCK, BLOCK), lambda i: (i, 0, 0, 0))
    return pl.pallas_call(
        kernel,
        name="shampoo",
        grid=(slots // many,),
        out_shape=(
            jax.ShapeDtypeStruct((slots, BLOCK, BLOCK), F32),
            jax.ShapeDtypeStruct((slots, 2, BLOCK, BLOCK), F32),
            jax.ShapeDtypeStruct((slots, BLOCK, BLOCK), F32),
        ),
        in_specs=[one] * terms + [two, two, one],
        out_specs=(one, two, one),
        compiler_params=params(dimension_semantics=("arbitrary",)),
        cost_estimate=cost(10),
    )(*gradient, statistics, inverse_roots, master)


def move(array, pairs):
    return lax.ppermute(array, "shard", pairs)


def sibling(array):
    return move(array, [(i, i ^ 1) for i in range(lax.axis_size("shard"))])


def along(array, distance):
    size = lax.axis_size("shard")
    return move(array, [(i, (i + 2 * distance) % size) for i in range(size)])


def give_back(parts):
    return lax.all_to_all(parts, "expert", split_axis=0, concat_axis=0, tiled=True)


def spread(array):
    copies = jnp.broadcast_to(array[None], (lax.axis_size("expert"), *array.shape))
    return lax.all_to_all(copies, "expert", split_axis=0, concat_axis=0, tiled=True)


def two_ways(array, other_first):
    one, two = swap(array, 1), swap(array, 2)
    three = swap(two, 1) if other_first else swap(one, 2)
    return one, two, three


def gather_attention(own, deal, later):
    size, groups = lax.axis_size("shard"), lax.axis_size("expert")
    slots = own.shape[0]
    by_device = deal.reshape(groups, size, slots)
    if groups != 4 or size != 8:
        pieces = [lax.all_gather(own, ("expert", "shard"), axis=0, tiled=True)]
        return pieces, deal, later
    me_e, me_s = lax.axis_index("expert"), lax.axis_index("shard")
    lines = [along(own, d) for d in range(1, size // 2)]
    beside = [swap(own, 1), swap(own, 2)]
    lines, beside, later = lax.optimization_barrier((lines, beside, later))
    fours = [jnp.concatenate([own, *beside, swap(beside[0], 2)], axis=0)]
    fours += [jnp.concatenate([line, *two_ways(line, d % 2 == 0)], axis=0) for d, line in enumerate(lines)]
    pieces, names, far_names = [], [], []
    for d, four in enumerate(fours):
        pieces.append(four)
        source = (me_s - 2 * d) % size
        for m in range(groups):
            names.append(by_device[me_e ^ m, source])
            far_names.append(by_device[me_e ^ m, source ^ 1])
    pieces += [sibling(piece) for piece in pieces]
    return pieces, jnp.concatenate(names + far_names), later


def attention_positions(deal, slots):
    size, groups = lax.axis_size("shard"), lax.axis_size("expert")
    inverse = inverse_of(deal)
    if groups != 4 or size != 8:
        return inverse
    owner, within = inverse // slots, inverse % slots
    mask = (owner // size) ^ lax.axis_index("expert")
    me = lax.axis_index("shard")
    core = (owner % 2) ^ (me % 2)
    distance = ((owner % size) // 2 - me // 2) % (size // 2)
    part = distance // (size // 4)
    first, second = jnp.where(part == 0, mask % 2, mask // 2), jnp.where(part == 0, mask // 2, mask % 2)
    place = ((core * 2 + 1 - first) * 2 + part) * 2 + second
    return ((place * (size // 4) + distance % (size // 4)) * slots + within).astype(jnp.int32)


def add_low(left, right):
    return (left.astype(F32) + right.astype(F32)).astype(BF16)


def scatter_attention(near, far, slots):
    size, groups = lax.axis_size("shard"), lax.axis_size("expert")
    if groups != 4 or size != 8:
        return [lax.psum_scatter(near, ("expert", "shard"), scatter_dimension=0, tiled=True)]
    quarter = near.shape[0] // 4
    far_first, far_rest = sibling(far[: 2 * quarter]), sibling(far[2 * quarter :])
    terms = []
    for part, (first, second) in enumerate(((1, 2), (2, 1))):
        here = slice(part * quarter, (part + 1) * quarter)
        there = slice((2 + part) * quarter, (3 + part) * quarter)
        mine = add_low(near[there], far_rest[here])
        mine = add_low(mine, swap(add_low(near[here], far_first[here]), first))
        stay, leave = mine[: quarter // 2], mine[quarter // 2 :]
        line = add_low(stay, swap(leave, second))
        terms += [line[i : i + slots] for i in range(0, line.shape[0], slots)]
    return terms


def scatter_line(terms):
    return terms[:1] + [along(term, d) for d, term in enumerate(terms) if d > 0]


def sum_across(values):
    size, groups = lax.axis_size("shard"), lax.axis_size("expert")
    if groups != 4 or size != 8:
        return lax.psum(values, ("expert", "shard"))
    values = values + sibling(values)
    for mask in (1, 2):
        values = values + swap(values, mask)
    return values


def sum_line(values):
    size, groups = lax.axis_size("shard"), lax.axis_size("expert")
    if groups != 4 or size != 8:
        return values
    line = jnp.stack([values] + [along(values, d) for d in range(1, size // 2)])
    place = lax.axis_index("shard") // 2
    return sum(line[(place - z) % (size // 2)] for z in range(size // 2))


def swap(array, mask):
    if mask == 0:
        return array
    return lax.ppermute(array, "expert", [(i, i ^ mask) for i in range(lax.axis_size("expert"))])


def per_device(
    tokens,
    cotangent,
    lengths,
    routes,
    route_gates,
    norm_gains,
    attn_master,
    attn_stats,
    attn_roots,
    attn_deal,
    expert_master,
    expert_stats,
    expert_roots,
    expert_deal,
):
    row_count = tokens.shape[0]
    groups = lax.axis_size("expert")
    group = lax.axis_index("expert").astype(jnp.int32).reshape(1)
    places = jnp.arange(row_count)
    valid_rows = places < lengths[0]
    grad_low = jnp.where(valid_rows[:, None], cotangent, jnp.zeros_like(cotangent))
    expert_lane = jnp.arange(LANES, dtype=jnp.int32)
    weights_row = sum(
        jnp.where(routes[:, k, None] == expert_lane, route_gates[:, k, None], jnp.zeros((), BF16))
        for k in range(TOP)
    )
    packed = jnp.concatenate([grad_low, weights_row], axis=1)
    half = row_count // 2
    packed_top = spread(packed[:half])
    pieces, natural, expert_low = gather_attention(
        attn_master.astype(BF16), attn_deal, expert_master.astype(BF16)
    )
    pieces, packed_bottom = lax.optimization_barrier((pieces, packed[half:]))
    packed_all = [packed_top, spread(packed_bottom)]
    expert_all = lax.all_gather(expert_low, "shard", axis=0, tiled=True)
    cosine, sine = rope_tables(jnp.arange(row_count, dtype=F32))
    cosine = jnp.concatenate([cosine] * 4, axis=1)
    sine = jnp.concatenate([-sine, sine] * 2, axis=1)
    block_rows, block_cols = attention_places(natural)
    normed_two, middle, mixed, q, k, v, w_all = attention_front(
        lengths, block_rows, block_cols, tokens, norm_gains, cosine, sine, pieces
    )
    rows = [swap(normed_two, m) for m in range(groups)]
    expert_inverse = inverse_of(expert_deal[0])
    hidden, both, partials, matrices = expert_front(group, expert_inverse, expert_all, rows, packed_all)
    partials = give_back(partials)
    expert_term = expert_weight_grads(group, expert_inverse, rows, packed_all, hidden, both)
    moe_parts = expert_outputs(group, hidden, matrices)
    own_partial = expert_route(both[0], matrices)
    mixed, moe_parts = lax.optimization_barrier((mixed, moe_parts))
    moe_parts = give_back(moe_parts)
    slots = attn_master.shape[0]
    positions = attention_positions(attn_deal, slots)
    near = positions.shape[0] // (2 if groups == 4 and lax.axis_size("shard") == 8 else 1)
    input_grad, gain_parts, near_blocks, far_blocks = attention_back(
        lengths, positions, tokens, packed, norm_gains, cosine, sine, middle, mixed, q, k, v, w_all, group, own_partial, partials, near
    )
    near_blocks, far_blocks, moe_parts = lax.optimization_barrier((near_blocks, far_blocks, moe_parts))
    output = (middle + jnp.sum(moe_parts.astype(F32), axis=0)).astype(BF16)
    attn_terms = scatter_attention(near_blocks, far_blocks, slots)
    expert_term = lax.psum_scatter(expert_term, "shard", scatter_dimension=0, tiled=True)
    attn_terms, gain_parts = lax.optimization_barrier((attn_terms, gain_parts))
    gain_grads = sum_line(sum_across(gain_parts))
    expert_term, attn_terms, gain_grads = lax.optimization_barrier((expert_term, attn_terms, gain_grads))
    attn_terms = scatter_line(attn_terms)
    new_gains = norm_gains - STEP_SIZE * gain_grads * lax.rsqrt(
        jnp.mean(gain_grads * gain_grads, axis=-1, keepdims=True) + 1e-06
    )
    expert_grads, expert_stats_new, expert_new = shampoo(
        [expert_term], expert_stats, expert_roots, expert_master
    )
    attn_terms, expert_new = lax.optimization_barrier((attn_terms, expert_new))
    attn_grads, attn_stats_new, attn_new = shampoo(attn_terms, attn_stats, attn_roots, attn_master)
    return (
        output,
        input_grad,
        gain_grads,
        new_gains,
        attn_grads,
        attn_stats_new,
        attn_new,
        expert_grads,
        expert_stats_new,
        expert_new,
    )


def solution(mesh):
    in_specs = (
        P(("expert", "shard"), None),
        P(("expert", "shard"), None),
        P(("expert", "shard")),
        P(("expert", "shard"), None),
        P(("expert", "shard"), None),
        P(),
        P(("expert", "shard"), None, None),
        P(("expert", "shard"), None, None, None),
        P(("expert", "shard"), None, None, None),
        P(),
        P(("expert", "shard"), None, None),
        P(("expert", "shard"), None, None, None),
        P(("expert", "shard"), None, None, None),
        P("expert", None),
    )
    out_specs = (
        P(("expert", "shard"), None),
        P(("expert", "shard"), None),
        P(),
        P(),
        P(("expert", "shard"), None, None),
        P(("expert", "shard"), None, None, None),
        P(("expert", "shard"), None, None),
        P(("expert", "shard"), None, None),
        P(("expert", "shard"), None, None, None),
        P(("expert", "shard"), None, None),
    )
    return jax.shard_map(
        per_device, mesh=mesh, in_specs=in_specs, out_specs=out_specs, check_vma=False
    )
```

```python
import jax
import jax.numpy as jnp
from jax import lax
from jax.experimental import pallas as pl
from jax.experimental.pallas import tpu as pltpu
from jax.sharding import PartitionSpec as P

D = 1536
H = 24
KV = 8
HD = 64
FF = 512
TOP = 8
BLOCK = 128
EXP_DEV = 4
LANES = 128
BF16 = jnp.bfloat16
F32 = jnp.float32


EPSILON = 1e-05
STEP_SIZE = 0.3


QUERY_END = H * HD
KEYVAL_END = QUERY_END + 2 * KV * HD
ACROSS = D // BLOCK
QUERY_COLS = QUERY_END // BLOCK
KEYVAL_COLS = (KEYVAL_END - QUERY_END) // BLOCK
OUT_COLS = D // BLOCK
ALL_COLS = QUERY_COLS + KEYVAL_COLS + OUT_COLS


def rope_tables(positions):
    frequency = 10000.0 ** (-2.0 * jnp.arange(HD // 2, dtype=jnp.float32) / HD)
    angles = positions[:, None] * frequency[None, :]
    return (jnp.cos(angles), jnp.sin(angles))


def dot_nn(left, right):
    return lax.dot_general(left, right, (((1,), (0,)), ((), ())), preferred_element_type=F32)


def dot_nt(left, right):
    return lax.dot_general(left, right, (((1,), (1,)), ((), ())), preferred_element_type=F32)


def dot_tn(left, right):
    return lax.dot_general(left, right, (((0,), (0,)), ((), ())), preferred_element_type=F32)


def params(megabytes=63, **more):
    return pltpu.CompilerParams(vmem_limit_bytes=megabytes * 1024 * 1024, **more)


def cost(microseconds):
    return pl.CostEstimate(flops=int(microseconds * 1.15e9), bytes_accessed=1024, transcendentals=0)


def whole(memory_space):
    return pl.BlockSpec(memory_space=memory_space)


def held(shape):
    return pl.BlockSpec(shape, lambda *_: (0,) * len(shape))


def inverse_of(dealing):
    place = jnp.arange(dealing.shape[0], dtype=jnp.int32)
    return jnp.sum(jnp.where(dealing[None, :] == place[:, None], place[None, :], 0), axis=1)


def weight_of(packed, expert):
    lane = lax.broadcasted_iota(jnp.int32, packed.shape, 1)
    return jnp.sum(jnp.where(lane == expert, packed.astype(F32), 0.0), axis=1, keepdims=True)


def aligned(block):
    return block * BLOCK if isinstance(block, int) else pl.multiple_of(block * BLOCK, BLOCK)


def block_at(ref, row, col):
    return ref.at[
        pl.ds(aligned(row), BLOCK),
        pl.ds(aligned(col), BLOCK),
    ]


def stacked_copies(sources, target, sem):
    count = sources[0].shape[-2]
    return [
        pltpu.make_async_copy(
            source, target.at[pl.ds(i * count, count), :], sem
        )
        for i, source in enumerate(sources)
    ]


def expert_step(weight, rows, packed, matrix):
    gate_up = dot_nn(rows[...], matrix[:, : 2 * FF])
    grad_hidden = dot_nt(packed[:, :FF], matrix[:FF, 2 * FF :])
    for at in range(FF, D, FF):
        grad_hidden = grad_hidden + dot_nt(packed[:, at : at + FF], matrix[at : at + FF, 2 * FF :])
    gate, up = gate_up[:, :FF], gate_up[:, FF:]
    sigmoid = 0.5 * jnp.tanh(0.5 * gate) + 0.5
    silu = gate * sigmoid
    hidden = (silu * up * weight).astype(BF16)
    slope = grad_hidden * sigmoid * weight
    both = jnp.concatenate(
        [(slope * up * (1.0 + gate - silu)).astype(BF16), (slope * gate).astype(BF16)], axis=1
    )
    return hidden, both


def expert_front(group, inverse, blocks, rows, packed):
    parts = len(rows)
    count = rows[0].shape[0]
    across, wide, tall = D // BLOCK, 2 * FF // BLOCK, FF // BLOCK
    first, second = across * wide, tall * across

    def kernel(group_ref, inverse_ref, blocks_ref, *refs):
        refs = list(refs)
        take = lambda n: [refs.pop(0) for _ in range(n)]
        rows_refs, packed_refs = take(parts), take(len(packed))
        hidden_refs, both_refs = take(parts), take(parts)
        out_ref, kept_ref, rows_all, packed_all, total, matrices, block_sems, keep_sems, sems = refs
        step = pl.program_id(0)
        half = step % 2

        def bring(expert, half):
            base = expert * (first + second)

            for i in range(first + second):
                row, col = i // wide, i % wide
                if i >= first:
                    down = (i - first) % across
                    row, col = down // tall * tall + (i - first) // across, wide + down % tall
                pltpu.make_async_copy(
                    blocks_ref.at[inverse_ref[base + i]],
                    block_at(matrices.at[half], row, col),
                    block_sems.at[half],
                ).start()

        def keep(expert, half):
            return pltpu.make_async_copy(matrices.at[half], kept_ref.at[expert], keep_sems.at[half])

        loads = [
            load
            for i in range(parts)
            for load in [pltpu.make_async_copy(rows_refs[i], rows_all.at[i], sems.at[0, i])]
            + stacked_copies([ref.at[group_ref[0] ^ i] for ref in packed_refs], packed_all.at[i], sems.at[1, i])
        ]

        @pl.when(step == 0)
        def _():
            for load in loads[:3]:
                load.start()
            bring(0, 0)
            for load in loads[3:]:
                load.start()

        @pl.when(step > 0)
        def _():
            keep(step - 1, 1 - half).wait()

        @pl.when(step < EXP_DEV - 1)
        def _():
            bring(step + 1, 1 - half)

        matrix = matrices.at[half]
        pltpu.make_async_copy(matrix, matrix, block_sems.at[half]).wait()
        keep(step, half).start()

        @pl.when(step == 0)
        def _():
            total[...] = jnp.zeros_like(total)
            for load in loads:
                load.wait()

        for i in range(parts):
            weight = weight_of(packed_all[i, :, D:], group_ref[0] * EXP_DEV + step)
            hidden, both = expert_step(weight, rows_all.at[i], packed_all.at[i], matrix)
            hidden_refs[i][0] = hidden
            both_refs[i][0] = both
            if i > 0:
                total[i - 1] += dot_nt(both, matrix[:, : 2 * FF])

        @pl.when(step == EXP_DEV - 1)
        def _():
            for i in range(1, parts):
                out_ref[group_ref[0] ^ i] = total[i - 1].astype(BF16)
            keep(step, half).wait()

    any_space, smem = whole(pl.ANY), whole(pltpu.SMEM)
    out = pl.pallas_call(
        kernel,
        name="expert_front",
        grid=(EXP_DEV,),
        out_shape=(
            [jax.ShapeDtypeStruct((EXP_DEV, count, FF), BF16)] * parts
            + [jax.ShapeDtypeStruct((EXP_DEV, count, 2 * FF), BF16)] * parts
            + [jax.ShapeDtypeStruct((parts, count, D), BF16)]
            + [jax.ShapeDtypeStruct((EXP_DEV, D, 3 * FF), BF16)]
        ),
        in_specs=[smem] * 2 + [any_space] * (1 + parts + len(packed)),
        out_specs=(
            [pl.BlockSpec((1, count, FF), lambda j: (j, 0, 0))] * parts
            + [pl.BlockSpec((1, count, 2 * FF), lambda j: (j, 0, 0))] * parts
            + [held((parts, count, D))]
            + [any_space]
        ),
        scratch_shapes=[
            pltpu.VMEM((parts, count, D), BF16),
            pltpu.VMEM((parts, count, D + LANES), BF16),
            pltpu.VMEM((parts - 1, count, D), F32),
            pltpu.VMEM((2, D, 3 * FF), BF16),
            pltpu.SemaphoreType.DMA((2,)),
            pltpu.SemaphoreType.DMA((2,)),
            pltpu.SemaphoreType.DMA((2, parts)),
        ],
        compiler_params=params(dimension_semantics=("arbitrary",)),
        cost_estimate=cost(100),
    )(group, inverse, blocks, *rows, *packed)
    return out[:parts], out[parts : 2 * parts], out[-2], out[-1]


def expert_weight_grads(group, positions, rows, packed, hidden, both):
    parts = len(rows)
    count = rows[0].shape[0]
    total_rows = parts * count
    slots = positions.shape[0]
    across, wide, tall = D // BLOCK, 2 * FF // BLOCK, FF // BLOCK
    first, second = across * wide, tall * across
    tile = 256

    def kernel(group_ref, position_ref, *refs):
        refs = list(refs)
        take = lambda n: [refs.pop(0) for _ in range(n)]
        rows_refs, packed_refs, hidden_refs, both_refs = take(parts), take(len(packed)), take(parts), take(parts)
        out_ref, rows_all, packed_all, hidden_two, both_two, stage_gateup, stage_down, sems = refs
        step = pl.program_id(0)
        half = step % 2
        base = step * (first + second)

        def loads(expert, half):
            return stacked_copies([r.at[expert] for r in hidden_refs], hidden_two.at[half], sems.at[2 + half]) + stacked_copies(
                [r.at[expert] for r in both_refs], both_two.at[half], sems.at[4 + half]
            )

        once = stacked_copies(rows_refs, rows_all, sems.at[6]) + stacked_copies(
            [ref.at[group_ref[0] ^ i] for i in range(parts) for ref in packed_refs], packed_all, sems.at[7]
        )

        @pl.when(step == 0)
        def _():
            for load in once[:parts] + loads(0, 0) + once[parts:]:
                load.start()

        for load in loads(step, half):
            load.wait()

        @pl.when(step < EXP_DEV - 1)
        def _():
            for load in loads(step + 1, 1 - half):
                load.start()

        @pl.when(step == 0)
        def _():
            for load in once[:parts]:
                load.wait()

        def wait_gateup():
            pltpu.make_async_copy(stage_gateup, stage_gateup, sems.at[0]).wait()

        def wait_down():
            pltpu.make_async_copy(stage_down, stage_down, sems.at[1]).wait()

        def send(stage, sem, start, blocks, columns):
            for i in range(blocks):
                pltpu.make_async_copy(
                    block_at(stage, i // columns, i % columns), out_ref.at[position_ref[start + i]], sem
                ).start()

        pl.when(step > 0)(wait_gateup)
        for at in range(0, 2 * FF, tile):
            stage_gateup[:, at : at + tile] = dot_tn(
                rows_all[...], both_two[half, :, at : at + tile]
            ).astype(BF16)
        send(stage_gateup, sems.at[0], base, first, wide)
        pl.when(step > 0)(wait_down)

        @pl.when(step == 0)
        def _():
            for load in once[parts:]:
                load.wait()

        for at in range(0, D, tile):
            stage_down[:, at : at + tile] = dot_tn(
                hidden_two[half], packed_all[:, at : at + tile]
            ).astype(BF16)
        send(stage_down, sems.at[1], base + first, second, across)

        @pl.when(step == EXP_DEV - 1)
        def _():
            wait_gateup()
            wait_down()

    any_space, smem = whole(pl.ANY), whole(pltpu.SMEM)
    return pl.pallas_call(
        kernel,
        name="expert_weight_grads",
        grid=(EXP_DEV,),
        out_shape=jax.ShapeDtypeStruct((slots, BLOCK, BLOCK), BF16),
        in_specs=[smem] * 2 + [any_space] * (3 * parts + len(packed)),
        out_specs=any_space,
        scratch_shapes=[
            pltpu.VMEM((total_rows, D), BF16),
            pltpu.VMEM((total_rows, D + LANES), BF16),
            pltpu.VMEM((2, total_rows, FF), BF16),
            pltpu.VMEM((2, total_rows, 2 * FF), BF16),
            pltpu.VMEM((D, 2 * FF), BF16),
            pltpu.VMEM((FF, D), BF16),
            pltpu.SemaphoreType.DMA((8,)),
        ],
        compiler_params=params(dimension_semantics=("arbitrary",)),
        cost_estimate=cost(100),
    )(group, positions, *rows, *packed, *hidden, *both)


def expert_route(both, matrices):
    count = both.shape[1]

    def kernel(both_ref, matrix_ref, out_ref):
        out_ref[...] = sum(
            dot_nt(both_ref[expert], matrix_ref[expert]) for expert in range(EXP_DEV)
        ).astype(BF16)

    return pl.pallas_call(
        kernel,
        name="expert_route",
        grid=(D // FF,),
        out_shape=jax.ShapeDtypeStruct((count, D), BF16),
        in_specs=[
            held((EXP_DEV, count, 2 * FF)),
            pl.BlockSpec((EXP_DEV, FF, 2 * FF), lambda j: (0, j, 0)),
        ],
        out_specs=pl.BlockSpec((count, FF), lambda j: (0, j)),
        compiler_params=params(dimension_semantics=("arbitrary",)),
        cost_estimate=cost(4),
    )(both, matrices)


def expert_outputs(group, hidden, matrices):
    parts = len(hidden)
    count = hidden[0].shape[1]

    def kernel(group_ref, *refs):
        hidden_refs, matrix_ref, out_ref = refs[:parts], refs[parts], refs[parts + 1]
        for i, hidden_ref in enumerate(hidden_refs):
            out_ref[group_ref[0] ^ i] = sum(
                dot_nn(hidden_ref[expert], matrix_ref[expert]) for expert in range(EXP_DEV)
            ).astype(BF16)

    return pl.pallas_call(
        kernel,
        name="expert_outputs",
        grid=(D // FF,),
        out_shape=jax.ShapeDtypeStruct((parts, count, D), BF16),
        in_specs=[whole(pltpu.SMEM)] + [held((EXP_DEV, count, FF))] * parts
        + [pl.BlockSpec((EXP_DEV, FF, FF), lambda j: (0, j, 2))],
        out_specs=pl.BlockSpec((parts, count, FF), lambda j: (0, 0, j)),
        compiler_params=params(dimension_semantics=("arbitrary",)),
        cost_estimate=cost(300),
    )(group, *hidden, matrices)


def attention_places(natural):
    first = ACROSS * QUERY_COLS
    second = first + ACROSS * KEYVAL_COLS
    in_keyval, in_out = natural - first, natural - second
    row = jnp.where(
        natural < first,
        natural // QUERY_COLS,
        jnp.where(natural < second, in_keyval // KEYVAL_COLS, in_out // OUT_COLS),
    )
    col = jnp.where(
        natural < first,
        natural % QUERY_COLS,
        jnp.where(
            natural < second,
            QUERY_COLS + in_keyval % KEYVAL_COLS,
            QUERY_COLS + KEYVAL_COLS + in_out % OUT_COLS,
        ),
    )
    return row.astype(jnp.int32), col.astype(jnp.int32)


def turn(values, cosine, sine):
    lane = lax.broadcasted_iota(jnp.int32, values.shape, 1)
    partner = jnp.where(
        lane % HD < HD // 2,
        pltpu.roll(values, LANES - HD // 2, 1),
        pltpu.roll(values, HD // 2, 1),
    )
    return values * cosine + partner * sine


def score_bias(length, first, heads, columns):
    shape = (heads * BLOCK, columns)
    at_row = first + lax.broadcasted_iota(jnp.int32, shape, 0) % BLOCK
    at_col = lax.broadcasted_iota(jnp.int32, shape, 1)
    return jnp.where((at_col <= at_row) & (at_col < length), 0.0, -1e30)


def softmax_of(queries, keys, bias):
    scores = dot_nt(queries, keys) + bias
    weights = jnp.exp(scores - jnp.max(scores, axis=1, keepdims=True))
    return weights * (1.0 / jnp.sum(weights, axis=1, keepdims=True))


def head_rows(ref, head, heads, first):
    return ref[pl.ds(head, heads), first : first + BLOCK, :].reshape(heads * BLOCK, HD)


def unit_rows(values):
    scale = lax.rsqrt(jnp.mean(values * values, axis=-1, keepdims=True) + EPSILON)
    return values * scale, scale


def attention_front(lengths, block_rows, block_cols, tokens, gains, cosine, sine, pieces):
    count = tokens.shape[0]
    group_size = H // KV

    def kernel(length_ref, row_ref, col_ref, tokens_ref, gains_ref, cosine_ref, sine_ref, *refs):
        piece_refs = refs[: len(pieces)]
        normed_ref, middle_ref, mixed_ref, q_ref, k_ref, v_ref, all_ref = refs[len(pieces) : -4]
        weights, heads, bias_ref, sems = refs[-4:]
        offset = 0
        for piece in piece_refs:

            def bring(i, _, piece=piece, offset=offset):
                pltpu.make_async_copy(
                    piece.at[i],
                    block_at(weights, row_ref[offset + i], col_ref[offset + i]),
                    sems.at[0],
                ).start()
                return 0

            lax.fori_loop(0, piece.shape[0], bring, 0, unroll=4)
            offset += piece.shape[0]
        residual = tokens_ref[...].astype(F32)
        normed = (unit_rows(residual)[0] * gains_ref[0:1, :]).astype(BF16)
        pltpu.make_async_copy(weights, weights, sems.at[0]).wait()
        keep = pltpu.make_async_copy(weights, all_ref, sems.at[1])
        keep.start()
        cosine, sine = cosine_ref[...], sine_ref[...]
        for at in range(0, KEYVAL_END, 2 * LANES):
            product = dot_nn(normed, weights[:, at : at + 2 * LANES])
            for half in range(2):
                pair = product[:, half * LANES : (half + 1) * LANES]
                column = at + half * LANES
                if column < QUERY_END + KV * HD:
                    pair = turn(pair, cosine, sine)
                if column < QUERY_END:
                    pair = pair * HD ** (-0.5)
                pair = pair.astype(BF16)
                if column < QUERY_END:
                    target, head = q_ref, column // HD
                elif column < QUERY_END + KV * HD:
                    target, head = k_ref, (column - QUERY_END) // HD
                else:
                    target, head = v_ref, (column - QUERY_END - KV * HD) // HD
                target[head] = pair[:, :HD]
                target[head + 1] = pair[:, HD:]
        for first in range(0, count, BLOCK):
            bias_ref[first // BLOCK] = score_bias(length_ref[0], first, group_size, count)

        def attend(j, _):
            for first in range(0, count, BLOCK):
                seen = slice(0, first + BLOCK)
                probs = softmax_of(
                    head_rows(q_ref, j * group_size, group_size, first),
                    k_ref[j, seen],
                    bias_ref[first // BLOCK, :, seen],
                ).astype(BF16)
                heads[pl.ds(j * group_size, group_size), first : first + BLOCK, :] = (
                    dot_nn(probs, v_ref[j, seen]).astype(BF16).reshape(group_size, BLOCK, HD)
                )
            return 0

        lax.fori_loop(0, KV, attend, 0, unroll=2)
        for pair in range(H // 2):
            mixed_ref[:, pair * LANES : (pair + 1) * LANES] = jnp.concatenate(
                [heads[2 * pair], heads[2 * pair + 1]], axis=1
            )
        middle = residual + dot_nn(mixed_ref[...], weights[:, KEYVAL_END:])
        middle_ref[...] = middle
        normed_ref[...] = (unit_rows(middle)[0] * gains_ref[1:2, :]).astype(BF16)
        keep.wait()

    vmem = whole(pltpu.VMEM)
    return pl.pallas_call(
        kernel,
        name="attention_front",
        out_shape=(
            jax.ShapeDtypeStruct((count, D), BF16),
            jax.ShapeDtypeStruct((count, D), F32),
            jax.ShapeDtypeStruct((count, H * HD), BF16),
            jax.ShapeDtypeStruct((H, count, HD), BF16),
            jax.ShapeDtypeStruct((KV, count, HD), BF16),
            jax.ShapeDtypeStruct((KV, count, HD), BF16),
            jax.ShapeDtypeStruct((D, ALL_COLS * BLOCK), BF16),
        ),
        in_specs=[whole(pltpu.SMEM)] * 3 + [vmem] * 4 + [whole(pl.ANY)] * len(pieces),
        out_specs=(vmem,) * 6 + (whole(pl.ANY),),
        scratch_shapes=[
            pltpu.VMEM((D, ALL_COLS * BLOCK), BF16),
            pltpu.VMEM((H, count, HD), BF16),
            pltpu.VMEM((count // BLOCK, group_size * BLOCK, count), F32),
            pltpu.SemaphoreType.DMA((2,)),
        ],
        compiler_params=params(),
        cost_estimate=cost(100),
    )(lengths, block_rows, block_cols, tokens, gains, cosine, sine, *pieces)


def attention_back(lengths, positions, tokens, packed, gains, cosine, sine, middle, mixed, q, k, v, w_all, group, own, partials, near):
    count = tokens.shape[0]
    group_size = H // KV
    blocks = positions.shape[0]
    parts = partials.shape[0]

    def kernel(group_ref, length_ref, position_ref, tokens_ref, packed_ref, gains_ref, cosine_ref, sine_ref, middle_ref, mixed_ref,
               q_ref, k_ref, v_ref, *refs):
        own_ref, partial_ref, all_ref, input_grad_ref, gain_ref, near_ref, far_ref = refs[:7]
        weights, stage, grad_heads, grad_columns, bias_ref, sems = refs[7:]
        bring_out = pltpu.make_async_copy(all_ref.at[:, pl.ds(KEYVAL_END, D)], weights.at[:, pl.ds(KEYVAL_END, D)], sems.at[0])
        bring_in = pltpu.make_async_copy(all_ref.at[:, pl.ds(0, KEYVAL_END)], weights.at[:, pl.ds(0, KEYVAL_END)], sems.at[1])
        bring_out.start()
        bring_in.start()

        def send(first, columns, col_offset):
            def one(i, _):
                place = position_ref[first + i]
                source = block_at(stage, i // columns, col_offset + i % columns)

                @pl.when(place < near)
                def _():
                    pltpu.make_async_copy(source, near_ref.at[place], sems.at[2]).start()

                @pl.when(place >= near)
                def _():
                    pltpu.make_async_copy(source, far_ref.at[place - near], sems.at[2]).start()

                return 0

            lax.fori_loop(0, ACROSS * columns, one, 0, unroll=4)

        grad_normed = own_ref[...].astype(F32)
        for i in range(1, parts):
            grad_normed = grad_normed + partial_ref[group_ref[0] ^ i].astype(F32)
        unit, scale = unit_rows(middle_ref[...])
        gain_ref[1:2, :] = jnp.sum(grad_normed * unit, axis=0, keepdims=True)
        scaled = grad_normed * gains_ref[1:2, :]
        grad_middle = packed_ref[:, :D].astype(F32) + scale * (
            scaled - unit * jnp.mean(scaled * unit, axis=-1, keepdims=True)
        )
        input_grad_ref[...] = grad_middle
        grad_attn = grad_middle.astype(BF16)
        for at in range(0, D, 4 * LANES):
            stage[:, KEYVAL_END + at : KEYVAL_END + at + 4 * LANES] = dot_tn(
                mixed_ref[...], grad_attn[:, at : at + 4 * LANES]
            ).astype(BF16)
        send(ACROSS * (QUERY_COLS + KEYVAL_COLS), OUT_COLS, QUERY_COLS + KEYVAL_COLS)
        bring_out.wait()
        for at in range(0, H * HD, 2 * LANES):
            product = dot_nt(grad_attn, weights[at : at + 2 * LANES, KEYVAL_END:]).astype(BF16)
            for part in range(2 * LANES // HD):
                grad_heads[at // HD + part] = product[:, part * HD : (part + 1) * HD]
        for first in range(0, count, BLOCK):
            bias_ref[first // BLOCK] = score_bias(length_ref[0], first, group_size, count)

        def attend(j, _):
            blocks_here = count // BLOCK
            grad_keys, grad_values = [0.0] * blocks_here, [0.0] * blocks_here
            for block in range(blocks_here):
                first = block * BLOCK
                seen = slice(0, first + BLOCK)
                keys, values = k_ref[j, seen], v_ref[j, seen]
                queries = head_rows(q_ref, j * group_size, group_size, first)
                grad_mixed = head_rows(grad_heads, j * group_size, group_size, first)
                probs = softmax_of(queries, keys, bias_ref[block, :, seen])
                more_values = dot_tn(probs.astype(BF16), grad_mixed)
                grad_probs = dot_nt(grad_mixed, values)
                inner = jnp.sum(probs * grad_probs, axis=1, keepdims=True)
                grad_scores = (probs * (grad_probs - inner)).astype(BF16)
                grad_columns[pl.ds(j * group_size, group_size), first : first + BLOCK, :] = (
                    dot_nn(grad_scores, keys) * HD ** (-0.5)
                ).reshape(group_size, BLOCK, HD)
                more_keys = dot_tn(grad_scores, queries)
                for i in range(block + 1):
                    rows = slice(i * BLOCK, (i + 1) * BLOCK)
                    grad_keys[i] = grad_keys[i] + more_keys[rows]
                    grad_values[i] = grad_values[i] + more_values[rows]
            for i in range(blocks_here):
                rows = slice(i * BLOCK, (i + 1) * BLOCK)
                grad_columns[H + j, rows] = grad_keys[i]
                grad_columns[H + KV + j, rows] = grad_values[i]
            return 0

        lax.fori_loop(0, KV, attend, 0, unroll=2)
        cosine, sine = cosine_ref[...], -sine_ref[...]
        residual = tokens_ref[...].astype(F32)
        unit_one, scale_one = unit_rows(residual)
        normed = (unit_one * gains_ref[0:1, :]).astype(BF16)
        bring_in.wait()
        grad_normed_one = jnp.zeros((count, D), F32)
        for at in range(0, KEYVAL_END, 4 * LANES):
            pairs = []
            for column in range(at, at + 4 * LANES, LANES):
                head = column // HD
                pair = jnp.concatenate([grad_columns[head], grad_columns[head + 1]], axis=1)
                if column < QUERY_END + KV * HD:
                    pair = turn(pair, cosine, sine)
                pairs.append(pair.astype(BF16))
            columns = jnp.concatenate(pairs, axis=1)
            span = slice(at, at + 4 * LANES)
            stage[:, span] = dot_tn(normed, columns).astype(BF16)
            grad_normed_one = grad_normed_one + dot_nt(columns, weights[:, span])
        send(0, QUERY_COLS, 0)
        send(ACROSS * QUERY_COLS, KEYVAL_COLS, QUERY_COLS)
        gain_ref[0:1, :] = jnp.sum(grad_normed_one * unit_one, axis=0, keepdims=True)
        scaled_one = grad_normed_one * gains_ref[0:1, :]
        input_grad_ref[...] += scale_one * (
            scaled_one - unit_one * jnp.mean(scaled_one * unit_one, axis=-1, keepdims=True)
        )
        pltpu.make_async_copy(stage, stage, sems.at[2]).wait()

    vmem, any_space = whole(pltpu.VMEM), whole(pl.ANY)
    return pl.pallas_call(
        kernel,
        name="attention_back",
        out_shape=(
            jax.ShapeDtypeStruct((count, D), F32),
            jax.ShapeDtypeStruct((2, D), F32),
            jax.ShapeDtypeStruct((near, BLOCK, BLOCK), BF16),
            jax.ShapeDtypeStruct((max(blocks - near, 1), BLOCK, BLOCK), BF16),
        ),
        in_specs=[whole(pltpu.SMEM)] * 3 + [vmem] * 12 + [any_space],
        out_specs=(vmem, vmem, any_space, any_space),
        scratch_shapes=[
            pltpu.VMEM((D, ALL_COLS * BLOCK), BF16),
            pltpu.VMEM((D, ALL_COLS * BLOCK), BF16),
            pltpu.VMEM((H, count, HD), BF16),
            pltpu.VMEM((H + 2 * KV, count, HD), F32),
            pltpu.VMEM((count // BLOCK, group_size * BLOCK, count), F32),
            pltpu.SemaphoreType.DMA((3,)),
        ],
        compiler_params=params(),
        cost_estimate=cost(150),
    )(group, lengths, positions, tokens, packed, gains, cosine, sine, middle, mixed, q, k, v, own, partials, w_all)


def split_low(values):
    high = values.astype(BF16)
    return high, (values - high.astype(F32)).astype(BF16)


def batched(left, right, left_dim, right_dim):
    return lax.dot_general(
        left, right, (((left_dim,), (right_dim,)), ((0,), (0,))), preferred_element_type=F32
    )


def block_mean(values):
    return jnp.mean(values, axis=(1, 2), keepdims=True)


def shampoo(gradient, statistics, inverse_roots, master):
    terms = len(gradient)
    slots = master.shape[0]
    many = max(n for n in range(1, 19) if slots % n == 0 and (n == 1 or slots // n > 1))

    def kernel(*refs):
        stats_ref, roots_ref, master_ref, grad_ref, stats_out, master_out = refs[terms:]
        low = sum(ref[...].astype(F32) for ref in refs[:terms]).astype(BF16)
        grad = low.astype(F32)
        grad_ref[...] = grad
        scale = 0.5 / (block_mean(grad * grad) + 1e-06)
        stats_out[:, 0] = 0.5 * stats_ref[:, 0] + scale * batched(low, low, 2, 2)
        stats_out[:, 1] = 0.5 * stats_ref[:, 1] + scale * batched(low, low, 1, 1)
        left = jnp.concatenate(split_low(roots_ref[:, 0]), axis=2)
        turned = jnp.concatenate(
            split_low(batched(left, jnp.concatenate([low, low], axis=1), 2, 1)), axis=2
        )
        high, rest = split_low(roots_ref[:, 1])
        turned = batched(turned, jnp.concatenate([high, high], axis=1), 2, 1) + batched(
            turned[:, :, :BLOCK], rest, 2, 1
        )
        direction = turned * lax.rsqrt(block_mean(turned * turned) + 1e-06)
        own = master_ref[...]
        master_out[...] = own - STEP_SIZE * jnp.sqrt(block_mean(own * own)) * direction

    one = pl.BlockSpec((many, BLOCK, BLOCK), lambda i: (i, 0, 0))
    two = pl.BlockSpec((many, 2, BLOCK, BLOCK), lambda i: (i, 0, 0, 0))
    return pl.pallas_call(
        kernel,
        name="shampoo",
        grid=(slots // many,),
        out_shape=(
            jax.ShapeDtypeStruct((slots, BLOCK, BLOCK), F32),
            jax.ShapeDtypeStruct((slots, 2, BLOCK, BLOCK), F32),
            jax.ShapeDtypeStruct((slots, BLOCK, BLOCK), F32),
        ),
        in_specs=[one] * terms + [two, two, one],
        out_specs=(one, two, one),
        compiler_params=params(44, dimension_semantics=("arbitrary",)),
        cost_estimate=cost(10),
    )(*gradient, statistics, inverse_roots, master)


def move(array, pairs):
    return lax.ppermute(array, "shard", pairs)


def sibling(array):
    return move(array, [(i, i ^ 1) for i in range(lax.axis_size("shard"))])


def along(array, distance):
    size = lax.axis_size("shard")
    return move(array, [(i, (i + 2 * distance) % size) for i in range(size)])


def give_back(parts):
    return lax.all_to_all(parts, "expert", split_axis=0, concat_axis=0, tiled=True)


def spread(array):
    copies = jnp.broadcast_to(array[None], (lax.axis_size("expert"), *array.shape))
    return lax.all_to_all(copies, "expert", split_axis=0, concat_axis=0, tiled=True)


def two_ways(array, other_first):
    one, two = swap(array, 1), swap(array, 2)
    three = swap(two, 1) if other_first else swap(one, 2)
    return one, two, three


def gather_attention(own, deal, later):
    size, groups = lax.axis_size("shard"), lax.axis_size("expert")
    slots = own.shape[0]
    by_device = deal.reshape(groups, size, slots)
    if groups != 4 or size != 8:
        pieces = [lax.all_gather(own, ("expert", "shard"), axis=0, tiled=True)]
        return pieces, deal, later
    me_e, me_s = lax.axis_index("expert"), lax.axis_index("shard")
    lines = [along(own, d) for d in range(1, size // 2)]
    beside = [swap(own, 1), swap(own, 2)]
    lines, beside, later = lax.optimization_barrier((lines, beside, later))
    fours = [jnp.concatenate([own, *beside, swap(beside[0], 2)], axis=0)]
    fours += [jnp.concatenate([line, *two_ways(line, d % 2 == 0)], axis=0) for d, line in enumerate(lines)]
    pieces, names, far_names = [], [], []
    for d, four in enumerate(fours):
        pieces.append(four)
        source = (me_s - 2 * d) % size
        for m in range(groups):
            names.append(by_device[me_e ^ m, source])
            far_names.append(by_device[me_e ^ m, source ^ 1])
    pieces += [sibling(piece) for piece in pieces]
    return pieces, jnp.concatenate(names + far_names), later


def attention_positions(deal, slots):
    size, groups = lax.axis_size("shard"), lax.axis_size("expert")
    inverse = inverse_of(deal)
    if groups != 4 or size != 8:
        return inverse
    owner, within = inverse // slots, inverse % slots
    mask = (owner // size) ^ lax.axis_index("expert")
    me = lax.axis_index("shard")
    core = (owner % 2) ^ (me % 2)
    distance = ((owner % size) // 2) ^ (me // 2)
    part = distance // (size // 4)
    first, second = jnp.where(part == 0, mask % 2, mask // 2), jnp.where(part == 0, mask // 2, mask % 2)
    place = ((core * 2 + 1 - first) * 2 + part) * 2 + second
    return ((place * (size // 4) + distance % (size // 4)) * slots + within).astype(jnp.int32)


def add_low(left, right):
    return (left.astype(F32) + right.astype(F32)).astype(BF16)


def scatter_attention(near, far, slots):
    size, groups = lax.axis_size("shard"), lax.axis_size("expert")
    if groups != 4 or size != 8:
        return [lax.psum_scatter(near, ("expert", "shard"), scatter_dimension=0, tiled=True)]
    quarter = near.shape[0] // 4
    far_first, far_rest = sibling(far[: 2 * quarter]), sibling(far[2 * quarter :])
    terms = []
    for part, (first, second) in enumerate(((1, 2), (2, 1))):
        here = slice(part * quarter, (part + 1) * quarter)
        there = slice((2 + part) * quarter, (3 + part) * quarter)
        mine = add_low(near[there], far_rest[here])
        mine = add_low(mine, swap(add_low(near[here], far_first[here]), first))
        stay, leave = mine[: quarter // 2], mine[quarter // 2 :]
        line = add_low(stay, swap(leave, second))
        terms += [line[i : i + slots] for i in range(0, line.shape[0], slots)]
    return terms


def toward(array, mask):
    return move(array, [(i, i ^ (2 * mask)) for i in range(lax.axis_size("shard"))])


def fold_line(terms):
    if len(terms) == 1:
        return terms
    own, one, two, three = terms
    return [own, one, add_low(two, toward(three, 1))]


def scatter_line(terms):
    return terms[:1] + [toward(term, mask) for mask, term in enumerate(terms) if mask > 0]


def sum_across(values):
    size, groups = lax.axis_size("shard"), lax.axis_size("expert")
    if groups != 4 or size != 8:
        return lax.psum(values, ("expert", "shard"))
    values = values + sibling(values)
    for mask in (1, 2):
        values = values + swap(values, mask)
    return values


def sum_line(values):
    size, groups = lax.axis_size("shard"), lax.axis_size("expert")
    if groups != 4 or size != 8:
        return values
    line = jnp.stack([values] + [along(values, d) for d in range(1, size // 2)])
    place = lax.axis_index("shard") // 2
    return sum(line[(place - z) % (size // 2)] for z in range(size // 2))


def swap(array, mask):
    if mask == 0:
        return array
    return lax.ppermute(array, "expert", [(i, i ^ mask) for i in range(lax.axis_size("expert"))])


def per_device(
    tokens,
    cotangent,
    lengths,
    routes,
    route_gates,
    norm_gains,
    attn_master,
    attn_stats,
    attn_roots,
    attn_deal,
    expert_master,
    expert_stats,
    expert_roots,
    expert_deal,
):
    row_count = tokens.shape[0]
    groups = lax.axis_size("expert")
    group = lax.axis_index("expert").astype(jnp.int32).reshape(1)
    places = jnp.arange(row_count)
    valid_rows = places < lengths[0]
    grad_low = jnp.where(valid_rows[:, None], cotangent, jnp.zeros_like(cotangent))
    expert_lane = jnp.arange(LANES, dtype=jnp.int32)
    weights_row = sum(
        jnp.where(routes[:, k, None] == expert_lane, route_gates[:, k, None], jnp.zeros((), BF16))
        for k in range(TOP)
    )
    packed = jnp.concatenate([grad_low, weights_row], axis=1)
    half = row_count // 2
    packed_top = spread(packed[:half])
    pieces, natural, expert_low = gather_attention(
        attn_master.astype(BF16), attn_deal, expert_master.astype(BF16)
    )
    pieces, packed_bottom = lax.optimization_barrier((pieces, packed[half:]))
    packed_all = [packed_top, spread(packed_bottom)]
    expert_all = lax.all_gather(expert_low, "shard", axis=0, tiled=True)
    cosine, sine = rope_tables(jnp.arange(row_count, dtype=F32))
    cosine = jnp.concatenate([cosine] * 4, axis=1)
    sine = jnp.concatenate([-sine, sine] * 2, axis=1)
    block_rows, block_cols = attention_places(natural)
    normed_two, middle, mixed, q, k, v, w_all = attention_front(
        lengths, block_rows, block_cols, tokens, norm_gains, cosine, sine, pieces
    )
    rows = [swap(normed_two, m) for m in range(groups)]
    expert_inverse = inverse_of(expert_deal[0])
    hidden, both, partials, matrices = expert_front(group, expert_inverse, expert_all, rows, packed_all)
    partials = give_back(partials)
    expert_term = expert_weight_grads(group, expert_inverse, rows, packed_all, hidden, both)
    moe_parts = expert_outputs(group, hidden, matrices)
    own_partial = expert_route(both[0], matrices)
    mixed, moe_parts = lax.optimization_barrier((mixed, moe_parts))
    moe_parts = give_back(moe_parts)
    slots = attn_master.shape[0]
    positions = attention_positions(attn_deal, slots)
    near = positions.shape[0] // (2 if groups == 4 and lax.axis_size("shard") == 8 else 1)
    input_grad, gain_parts, near_blocks, far_blocks = attention_back(
        lengths, positions, tokens, packed, norm_gains, cosine, sine, middle, mixed, q, k, v, w_all, group, own_partial, partials, near
    )
    near_blocks, far_blocks, moe_parts = lax.optimization_barrier((near_blocks, far_blocks, moe_parts))
    output = (middle + jnp.sum(moe_parts.astype(F32), axis=0)).astype(BF16)
    attn_terms = scatter_attention(near_blocks, far_blocks, slots)
    expert_term = lax.psum_scatter(expert_term, "shard", scatter_dimension=0, tiled=True)
    attn_terms = fold_line(attn_terms)
    attn_terms, gain_parts = lax.optimization_barrier((attn_terms, gain_parts))
    gain_grads = sum_line(sum_across(gain_parts))
    expert_term, attn_terms, gain_grads = lax.optimization_barrier((expert_term, attn_terms, gain_grads))
    attn_terms = scatter_line(attn_terms)
    new_gains = norm_gains - STEP_SIZE * gain_grads * lax.rsqrt(
        jnp.mean(gain_grads * gain_grads, axis=-1, keepdims=True) + 1e-06
    )
    expert_grads, expert_stats_new, expert_new = shampoo(
        [expert_term], expert_stats, expert_roots, expert_master
    )
    attn_terms, expert_new = lax.optimization_barrier((attn_terms, expert_new))
    attn_grads, attn_stats_new, attn_new = shampoo(attn_terms, attn_stats, attn_roots, attn_master)
    return (
        output,
        input_grad,
        gain_grads,
        new_gains,
        attn_grads,
        attn_stats_new,
        attn_new,
        expert_grads,
        expert_stats_new,
        expert_new,
    )


def solution(mesh):
    in_specs = (
        P(("expert", "shard"), None),
        P(("expert", "shard"), None),
        P(("expert", "shard")),
        P(("expert", "shard"), None),
        P(("expert", "shard"), None),
        P(),
        P(("expert", "shard"), None, None),
        P(("expert", "shard"), None, None, None),
        P(("expert", "shard"), None, None, None),
        P(),
        P(("expert", "shard"), None, None),
        P(("expert", "shard"), None, None, None),
        P(("expert", "shard"), None, None, None),
        P("expert", None),
    )
    out_specs = (
        P(("expert", "shard"), None),
        P(("expert", "shard"), None),
        P(),
        P(),
        P(("expert", "shard"), None, None),
        P(("expert", "shard"), None, None, None),
        P(("expert", "shard"), None, None),
        P(("expert", "shard"), None, None),
        P(("expert", "shard"), None, None, None),
        P(("expert", "shard"), None, None),
    )
    return jax.shard_map(
        per_device, mesh=mesh, in_specs=in_specs, out_specs=out_specs, check_vma=False
    )
```

```python
import jax
import jax.numpy as jnp
from jax import lax
from jax.experimental import pallas as pl
from jax.experimental.pallas import tpu as pltpu
from jax.sharding import PartitionSpec as P

D = 1536
H = 24
KV = 8
HD = 64
FF = 512
TOP = 8
BLOCK = 128
EXP_DEV = 4
LANES = 128
BF16 = jnp.bfloat16
F32 = jnp.float32


EPSILON = 1e-05
STEP_SIZE = 0.3


QUERY_END = H * HD
KEYVAL_END = QUERY_END + 2 * KV * HD
ACROSS = D // BLOCK
QUERY_COLS = QUERY_END // BLOCK
KEYVAL_COLS = (KEYVAL_END - QUERY_END) // BLOCK
OUT_COLS = D // BLOCK
ALL_COLS = QUERY_COLS + KEYVAL_COLS + OUT_COLS


def rope_tables(positions):
    frequency = 10000.0 ** (-2.0 * jnp.arange(HD // 2, dtype=jnp.float32) / HD)
    angles = positions[:, None] * frequency[None, :]
    return (jnp.cos(angles), jnp.sin(angles))


def dot_nn(left, right):
    return lax.dot_general(left, right, (((1,), (0,)), ((), ())), preferred_element_type=F32)


def dot_nt(left, right):
    return lax.dot_general(left, right, (((1,), (1,)), ((), ())), preferred_element_type=F32)


def dot_tn(left, right):
    return lax.dot_general(left, right, (((0,), (0,)), ((), ())), preferred_element_type=F32)


def params(megabytes=63, **more):
    return pltpu.CompilerParams(vmem_limit_bytes=megabytes * 1024 * 1024, **more)


def cost(microseconds):
    return pl.CostEstimate(flops=int(microseconds * 1.15e9), bytes_accessed=1024, transcendentals=0)


def whole(memory_space):
    return pl.BlockSpec(memory_space=memory_space)


def held(shape):
    return pl.BlockSpec(shape, lambda *_: (0,) * len(shape))


def inverse_of(dealing):
    place = jnp.arange(dealing.shape[0], dtype=jnp.int32)
    return jnp.sum(jnp.where(dealing[None, :] == place[:, None], place[None, :], 0), axis=1)


def weight_of(packed, expert):
    lane = lax.broadcasted_iota(jnp.int32, packed.shape, 1)
    return jnp.sum(jnp.where(lane == expert, packed.astype(F32), 0.0), axis=1, keepdims=True)


def aligned(block):
    return block * BLOCK if isinstance(block, int) else pl.multiple_of(block * BLOCK, BLOCK)


def block_at(ref, row, col):
    return ref.at[
        pl.ds(aligned(row), BLOCK),
        pl.ds(aligned(col), BLOCK),
    ]


def stacked_copies(sources, target, sem):
    count = sources[0].shape[-2]
    return [
        pltpu.make_async_copy(
            source, target.at[pl.ds(i * count, count), :], sem
        )
        for i, source in enumerate(sources)
    ]


def expert_step(weight, rows, packed, matrix):
    gate_up = dot_nn(rows[...], matrix[:, : 2 * FF])
    grad_hidden = dot_nt(packed[:, :FF], matrix[:FF, 2 * FF :])
    for at in range(FF, D, FF):
        grad_hidden = grad_hidden + dot_nt(packed[:, at : at + FF], matrix[at : at + FF, 2 * FF :])
    gate, up = gate_up[:, :FF], gate_up[:, FF:]
    sigmoid = 0.5 * jnp.tanh(0.5 * gate) + 0.5
    silu = gate * sigmoid
    hidden = (silu * up * weight).astype(BF16)
    slope = grad_hidden * sigmoid * weight
    both = jnp.concatenate(
        [(slope * up * (1.0 + gate - silu)).astype(BF16), (slope * gate).astype(BF16)], axis=1
    )
    return hidden, both


def expert_front(group, inverse, blocks, rows, packed):
    parts = len(rows)
    count = rows[0].shape[0]
    across, wide, tall = D // BLOCK, 2 * FF // BLOCK, FF // BLOCK
    first, second = across * wide, tall * across

    def kernel(group_ref, inverse_ref, blocks_ref, *refs):
        refs = list(refs)
        take = lambda n: [refs.pop(0) for _ in range(n)]
        rows_refs, packed_refs = take(parts), take(len(packed))
        hidden_refs, both_refs = take(parts), take(parts)
        out_ref, kept_ref, rows_all, packed_all, total, matrices, block_sems, keep_sems, sems = refs
        step = pl.program_id(0)
        half = step % 2

        def bring(expert, half):
            base = expert * (first + second)

            for i in range(first + second):
                row, col = i // wide, i % wide
                if i >= first:
                    down = (i - first) % across
                    row, col = down // tall * tall + (i - first) // across, wide + down % tall
                pltpu.make_async_copy(
                    blocks_ref.at[inverse_ref[base + i]],
                    block_at(matrices.at[half], row, col),
                    block_sems.at[half],
                ).start()

        def keep(expert, half):
            return pltpu.make_async_copy(matrices.at[half], kept_ref.at[expert], keep_sems.at[half])

        loads = [
            load
            for i in range(parts)
            for load in [pltpu.make_async_copy(rows_refs[i], rows_all.at[i], sems.at[0, i])]
            + stacked_copies([ref.at[group_ref[0] ^ i] for ref in packed_refs], packed_all.at[i], sems.at[1, i])
        ]

        @pl.when(step == 0)
        def _():
            for load in loads[:3]:
                load.start()
            bring(0, 0)
            for load in loads[3:]:
                load.start()

        @pl.when(step > 0)
        def _():
            keep(step - 1, 1 - half).wait()

        @pl.when(step < EXP_DEV - 1)
        def _():
            bring(step + 1, 1 - half)

        matrix = matrices.at[half]
        pltpu.make_async_copy(matrix, matrix, block_sems.at[half]).wait()
        keep(step, half).start()

        @pl.when(step == 0)
        def _():
            total[...] = jnp.zeros_like(total)
            for load in loads:
                load.wait()

        for i in range(parts):
            weight = weight_of(packed_all[i, :, D:], group_ref[0] * EXP_DEV + step)
            hidden, both = expert_step(weight, rows_all.at[i], packed_all.at[i], matrix)
            hidden_refs[i][0] = hidden
            both_refs[i][0] = both
            if i > 0:
                total[i - 1] += dot_nt(both, matrix[:, : 2 * FF])

        @pl.when(step == EXP_DEV - 1)
        def _():
            for i in range(1, parts):
                out_ref[group_ref[0] ^ i] = total[i - 1].astype(BF16)
            keep(step, half).wait()

    any_space, smem = whole(pl.ANY), whole(pltpu.SMEM)
    out = pl.pallas_call(
        kernel,
        name="expert_front",
        grid=(EXP_DEV,),
        out_shape=(
            [jax.ShapeDtypeStruct((EXP_DEV, count, FF), BF16)] * parts
            + [jax.ShapeDtypeStruct((EXP_DEV, count, 2 * FF), BF16)] * parts
            + [jax.ShapeDtypeStruct((parts, count, D), BF16)]
            + [jax.ShapeDtypeStruct((EXP_DEV, D, 3 * FF), BF16)]
        ),
        in_specs=[smem] * 2 + [any_space] * (1 + parts + len(packed)),
        out_specs=(
            [pl.BlockSpec((1, count, FF), lambda j: (j, 0, 0))] * parts
            + [pl.BlockSpec((1, count, 2 * FF), lambda j: (j, 0, 0))] * parts
            + [held((parts, count, D))]
            + [any_space]
        ),
        scratch_shapes=[
            pltpu.VMEM((parts, count, D), BF16),
            pltpu.VMEM((parts, count, D + LANES), BF16),
            pltpu.VMEM((parts - 1, count, D), F32),
            pltpu.VMEM((2, D, 3 * FF), BF16),
            pltpu.SemaphoreType.DMA((2,)),
            pltpu.SemaphoreType.DMA((2,)),
            pltpu.SemaphoreType.DMA((2, parts)),
        ],
        compiler_params=params(dimension_semantics=("arbitrary",)),
        cost_estimate=cost(100),
    )(group, inverse, blocks, *rows, *packed)
    return out[:parts], out[parts : 2 * parts], out[-2], out[-1]


def expert_weight_grads(group, positions, rows, packed, hidden, both):
    parts = len(rows)
    count = rows[0].shape[0]
    total_rows = parts * count
    slots = positions.shape[0]
    across, wide, tall = D // BLOCK, 2 * FF // BLOCK, FF // BLOCK
    first, second = across * wide, tall * across
    tile = 256

    def kernel(group_ref, position_ref, *refs):
        refs = list(refs)
        take = lambda n: [refs.pop(0) for _ in range(n)]
        rows_refs, packed_refs, hidden_refs, both_refs = take(parts), take(len(packed)), take(parts), take(parts)
        out_ref, rows_all, packed_all, hidden_two, both_two, stage_gateup, stage_down, sems = refs
        step = pl.program_id(0)
        half = step % 2
        base = step * (first + second)

        def loads(expert, half):
            return stacked_copies([r.at[expert] for r in hidden_refs], hidden_two.at[half], sems.at[2 + half]) + stacked_copies(
                [r.at[expert] for r in both_refs], both_two.at[half], sems.at[4 + half]
            )

        once = stacked_copies(rows_refs, rows_all, sems.at[6]) + stacked_copies(
            [ref.at[group_ref[0] ^ i] for i in range(parts) for ref in packed_refs], packed_all, sems.at[7]
        )

        @pl.when(step == 0)
        def _():
            for load in once[:parts] + loads(0, 0) + once[parts:]:
                load.start()

        for load in loads(step, half):
            load.wait()

        @pl.when(step < EXP_DEV - 1)
        def _():
            for load in loads(step + 1, 1 - half):
                load.start()

        @pl.when(step == 0)
        def _():
            for load in once[:parts]:
                load.wait()

        def wait_gateup():
            pltpu.make_async_copy(stage_gateup, stage_gateup, sems.at[0]).wait()

        def wait_down():
            pltpu.make_async_copy(stage_down, stage_down, sems.at[1]).wait()

        def send(stage, sem, start, blocks, columns):
            for i in range(blocks):
                pltpu.make_async_copy(
                    block_at(stage, i // columns, i % columns), out_ref.at[position_ref[start + i]], sem
                ).start()

        pl.when(step > 0)(wait_gateup)
        for at in range(0, 2 * FF, tile):
            stage_gateup[:, at : at + tile] = dot_tn(
                rows_all[...], both_two[half, :, at : at + tile]
            ).astype(BF16)
        send(stage_gateup, sems.at[0], base, first, wide)
        pl.when(step > 0)(wait_down)

        @pl.when(step == 0)
        def _():
            for load in once[parts:]:
                load.wait()

        for at in range(0, D, tile):
            stage_down[:, at : at + tile] = dot_tn(
                hidden_two[half], packed_all[:, at : at + tile]
            ).astype(BF16)
        send(stage_down, sems.at[1], base + first, second, across)

        @pl.when(step == EXP_DEV - 1)
        def _():
            wait_gateup()
            wait_down()

    any_space, smem = whole(pl.ANY), whole(pltpu.SMEM)
    return pl.pallas_call(
        kernel,
        name="expert_weight_grads",
        grid=(EXP_DEV,),
        out_shape=jax.ShapeDtypeStruct((slots, BLOCK, BLOCK), BF16),
        in_specs=[smem] * 2 + [any_space] * (3 * parts + len(packed)),
        out_specs=any_space,
        scratch_shapes=[
            pltpu.VMEM((total_rows, D), BF16),
            pltpu.VMEM((total_rows, D + LANES), BF16),
            pltpu.VMEM((2, total_rows, FF), BF16),
            pltpu.VMEM((2, total_rows, 2 * FF), BF16),
            pltpu.VMEM((D, 2 * FF), BF16),
            pltpu.VMEM((FF, D), BF16),
            pltpu.SemaphoreType.DMA((8,)),
        ],
        compiler_params=params(dimension_semantics=("arbitrary",)),
        cost_estimate=cost(100),
    )(group, positions, *rows, *packed, *hidden, *both)


def expert_route(both, matrices):
    count = both.shape[1]

    def kernel(both_ref, matrix_ref, out_ref):
        out_ref[...] = sum(
            dot_nt(both_ref[expert], matrix_ref[expert]) for expert in range(EXP_DEV)
        ).astype(BF16)

    return pl.pallas_call(
        kernel,
        name="expert_route",
        grid=(D // FF,),
        out_shape=jax.ShapeDtypeStruct((count, D), BF16),
        in_specs=[
            held((EXP_DEV, count, 2 * FF)),
            pl.BlockSpec((EXP_DEV, FF, 2 * FF), lambda j: (0, j, 0)),
        ],
        out_specs=pl.BlockSpec((count, FF), lambda j: (0, j)),
        compiler_params=params(dimension_semantics=("arbitrary",)),
        cost_estimate=cost(4),
    )(both, matrices)


def expert_outputs(group, hidden, matrices):
    parts = len(hidden)
    count = hidden[0].shape[1]

    def kernel(group_ref, *refs):
        hidden_refs, matrix_ref, out_ref = refs[:parts], refs[parts], refs[parts + 1]
        for i, hidden_ref in enumerate(hidden_refs):
            out_ref[group_ref[0] ^ i] = sum(
                dot_nn(hidden_ref[expert], matrix_ref[expert]) for expert in range(EXP_DEV)
            ).astype(BF16)

    return pl.pallas_call(
        kernel,
        name="expert_outputs",
        grid=(D // FF,),
        out_shape=jax.ShapeDtypeStruct((parts, count, D), BF16),
        in_specs=[whole(pltpu.SMEM)] + [held((EXP_DEV, count, FF))] * parts
        + [pl.BlockSpec((EXP_DEV, FF, FF), lambda j: (0, j, 2))],
        out_specs=pl.BlockSpec((parts, count, FF), lambda j: (0, 0, j)),
        compiler_params=params(dimension_semantics=("arbitrary",)),
        cost_estimate=cost(300),
    )(group, *hidden, matrices)


def attention_places(natural):
    first = ACROSS * QUERY_COLS
    second = first + ACROSS * KEYVAL_COLS
    in_keyval, in_out = natural - first, natural - second
    row = jnp.where(
        natural < first,
        natural // QUERY_COLS,
        jnp.where(natural < second, in_keyval // KEYVAL_COLS, in_out // OUT_COLS),
    )
    col = jnp.where(
        natural < first,
        natural % QUERY_COLS,
        jnp.where(
            natural < second,
            QUERY_COLS + in_keyval % KEYVAL_COLS,
            QUERY_COLS + KEYVAL_COLS + in_out % OUT_COLS,
        ),
    )
    return row.astype(jnp.int32), col.astype(jnp.int32)


def turn(values, cosine, sine):
    lane = lax.broadcasted_iota(jnp.int32, values.shape, 1)
    partner = jnp.where(
        lane % HD < HD // 2,
        pltpu.roll(values, LANES - HD // 2, 1),
        pltpu.roll(values, HD // 2, 1),
    )
    return values * cosine + partner * sine


def score_bias(length, first, heads, columns):
    shape = (heads * BLOCK, columns)
    at_row = first + lax.broadcasted_iota(jnp.int32, shape, 0) % BLOCK
    at_col = lax.broadcasted_iota(jnp.int32, shape, 1)
    return jnp.where((at_col <= at_row) & (at_col < length), 0.0, -1e30)


def softmax_of(queries, keys, bias):
    scores = dot_nt(queries, keys) + bias
    weights = jnp.exp(scores - jnp.max(scores, axis=1, keepdims=True))
    return weights * (1.0 / jnp.sum(weights, axis=1, keepdims=True))


def head_rows(ref, head, heads, first):
    return ref[pl.ds(head, heads), first : first + BLOCK, :].reshape(heads * BLOCK, HD)


def unit_rows(values):
    scale = lax.rsqrt(jnp.mean(values * values, axis=-1, keepdims=True) + EPSILON)
    return values * scale, scale


def attention_front(lengths, block_rows, block_cols, tokens, gains, cosine, sine, pieces):
    count = tokens.shape[0]
    group_size = H // KV

    def kernel(length_ref, row_ref, col_ref, tokens_ref, gains_ref, cosine_ref, sine_ref, *refs):
        piece_refs = refs[: len(pieces)]
        normed_ref, middle_ref, mixed_ref, q_ref, k_ref, v_ref, all_ref = refs[len(pieces) : -4]
        weights, heads, bias_ref, sems = refs[-4:]
        offset = 0
        for piece in piece_refs:

            def bring(i, _, piece=piece, offset=offset):
                pltpu.make_async_copy(
                    piece.at[i],
                    block_at(weights, row_ref[offset + i], col_ref[offset + i]),
                    sems.at[0],
                ).start()
                return 0

            lax.fori_loop(0, piece.shape[0], bring, 0, unroll=4)
            offset += piece.shape[0]
        residual = tokens_ref[...].astype(F32)
        normed = (unit_rows(residual)[0] * gains_ref[0:1, :]).astype(BF16)
        pltpu.make_async_copy(weights, weights, sems.at[0]).wait()
        keep = pltpu.make_async_copy(weights, all_ref, sems.at[1])
        keep.start()
        cosine, sine = cosine_ref[...], sine_ref[...]
        for at in range(0, KEYVAL_END, 2 * LANES):
            product = dot_nn(normed, weights[:, at : at + 2 * LANES])
            for half in range(2):
                pair = product[:, half * LANES : (half + 1) * LANES]
                column = at + half * LANES
                if column < QUERY_END + KV * HD:
                    pair = turn(pair, cosine, sine)
                if column < QUERY_END:
                    pair = pair * HD ** (-0.5)
                pair = pair.astype(BF16)
                if column < QUERY_END:
                    target, head = q_ref, column // HD
                elif column < QUERY_END + KV * HD:
                    target, head = k_ref, (column - QUERY_END) // HD
                else:
                    target, head = v_ref, (column - QUERY_END - KV * HD) // HD
                target[head] = pair[:, :HD]
                target[head + 1] = pair[:, HD:]
        for first in range(0, count, BLOCK):
            bias_ref[first // BLOCK] = score_bias(length_ref[0], first, group_size, count)

        def attend(j, _):
            for first in range(0, count, BLOCK):
                seen = slice(0, first + BLOCK)
                probs = softmax_of(
                    head_rows(q_ref, j * group_size, group_size, first),
                    k_ref[j, seen],
                    bias_ref[first // BLOCK, :, seen],
                ).astype(BF16)
                heads[pl.ds(j * group_size, group_size), first : first + BLOCK, :] = (
                    dot_nn(probs, v_ref[j, seen]).astype(BF16).reshape(group_size, BLOCK, HD)
                )
            return 0

        lax.fori_loop(0, KV, attend, 0, unroll=2)
        for pair in range(H // 2):
            mixed_ref[:, pair * LANES : (pair + 1) * LANES] = jnp.concatenate(
                [heads[2 * pair], heads[2 * pair + 1]], axis=1
            )
        middle = residual + dot_nn(mixed_ref[...], weights[:, KEYVAL_END:])
        middle_ref[...] = middle
        normed_ref[...] = (unit_rows(middle)[0] * gains_ref[1:2, :]).astype(BF16)
        keep.wait()

    vmem = whole(pltpu.VMEM)
    return pl.pallas_call(
        kernel,
        name="attention_front",
        out_shape=(
            jax.ShapeDtypeStruct((count, D), BF16),
            jax.ShapeDtypeStruct((count, D), F32),
            jax.ShapeDtypeStruct((count, H * HD), BF16),
            jax.ShapeDtypeStruct((H, count, HD), BF16),
            jax.ShapeDtypeStruct((KV, count, HD), BF16),
            jax.ShapeDtypeStruct((KV, count, HD), BF16),
            jax.ShapeDtypeStruct((D, ALL_COLS * BLOCK), BF16),
        ),
        in_specs=[whole(pltpu.SMEM)] * 3 + [vmem] * 4 + [whole(pl.ANY)] * len(pieces),
        out_specs=(vmem,) * 6 + (whole(pl.ANY),),
        scratch_shapes=[
            pltpu.VMEM((D, ALL_COLS * BLOCK), BF16),
            pltpu.VMEM((H, count, HD), BF16),
            pltpu.VMEM((count // BLOCK, group_size * BLOCK, count), F32),
            pltpu.SemaphoreType.DMA((2,)),
        ],
        compiler_params=params(),
        cost_estimate=cost(100),
    )(lengths, block_rows, block_cols, tokens, gains, cosine, sine, *pieces)


def attention_back(lengths, positions, tokens, packed, gains, cosine, sine, middle, mixed, q, k, v, w_all, group, own, partials, near):
    count = tokens.shape[0]
    group_size = H // KV
    blocks = positions.shape[0]
    parts = partials.shape[0]

    def kernel(group_ref, length_ref, position_ref, tokens_ref, packed_ref, gains_ref, cosine_ref, sine_ref, middle_ref, mixed_ref,
               q_ref, k_ref, v_ref, *refs):
        own_ref, partial_ref, all_ref, input_grad_ref, gain_ref, near_ref, far_ref = refs[:7]
        weights, stage, grad_heads, grad_columns, bias_ref, sems = refs[7:]
        bring_out = pltpu.make_async_copy(all_ref.at[:, pl.ds(KEYVAL_END, D)], weights.at[:, pl.ds(KEYVAL_END, D)], sems.at[0])
        bring_in = pltpu.make_async_copy(all_ref.at[:, pl.ds(0, KEYVAL_END)], weights.at[:, pl.ds(0, KEYVAL_END)], sems.at[1])
        bring_out.start()
        bring_in.start()

        def send(first, columns, col_offset):
            def one(i, _):
                place = position_ref[first + i]
                source = block_at(stage, i // columns, col_offset + i % columns)

                @pl.when(place < near)
                def _():
                    pltpu.make_async_copy(source, near_ref.at[place], sems.at[2]).start()

                @pl.when(place >= near)
                def _():
                    pltpu.make_async_copy(source, far_ref.at[place - near], sems.at[2]).start()

                return 0

            lax.fori_loop(0, ACROSS * columns, one, 0, unroll=4)

        grad_normed = own_ref[...].astype(F32)
        for i in range(1, parts):
            grad_normed = grad_normed + partial_ref[group_ref[0] ^ i].astype(F32)
        unit, scale = unit_rows(middle_ref[...])
        gain_ref[1:2, :] = jnp.sum(grad_normed * unit, axis=0, keepdims=True)
        scaled = grad_normed * gains_ref[1:2, :]
        grad_middle = packed_ref[:, :D].astype(F32) + scale * (
            scaled - unit * jnp.mean(scaled * unit, axis=-1, keepdims=True)
        )
        input_grad_ref[...] = grad_middle
        grad_attn = grad_middle.astype(BF16)
        for at in range(0, D, 4 * LANES):
            stage[:, KEYVAL_END + at : KEYVAL_END + at + 4 * LANES] = dot_tn(
                mixed_ref[...], grad_attn[:, at : at + 4 * LANES]
            ).astype(BF16)
        send(ACROSS * (QUERY_COLS + KEYVAL_COLS), OUT_COLS, QUERY_COLS + KEYVAL_COLS)
        bring_out.wait()
        for at in range(0, H * HD, 2 * LANES):
            product = dot_nt(grad_attn, weights[at : at + 2 * LANES, KEYVAL_END:]).astype(BF16)
            for part in range(2 * LANES // HD):
                grad_heads[at // HD + part] = product[:, part * HD : (part + 1) * HD]
        for first in range(0, count, BLOCK):
            bias_ref[first // BLOCK] = score_bias(length_ref[0], first, group_size, count)

        def attend(j, _):
            blocks_here = count // BLOCK
            grad_keys, grad_values = [0.0] * blocks_here, [0.0] * blocks_here
            for block in range(blocks_here):
                first = block * BLOCK
                seen = slice(0, first + BLOCK)
                keys, values = k_ref[j, seen], v_ref[j, seen]
                queries = head_rows(q_ref, j * group_size, group_size, first)
                grad_mixed = head_rows(grad_heads, j * group_size, group_size, first)
                probs = softmax_of(queries, keys, bias_ref[block, :, seen])
                more_values = dot_tn(probs.astype(BF16), grad_mixed)
                grad_probs = dot_nt(grad_mixed, values)
                inner = jnp.sum(probs * grad_probs, axis=1, keepdims=True)
                grad_scores = (probs * (grad_probs - inner)).astype(BF16)
                grad_columns[pl.ds(j * group_size, group_size), first : first + BLOCK, :] = (
                    dot_nn(grad_scores, keys) * HD ** (-0.5)
                ).reshape(group_size, BLOCK, HD)
                more_keys = dot_tn(grad_scores, queries)
                for i in range(block + 1):
                    rows = slice(i * BLOCK, (i + 1) * BLOCK)
                    grad_keys[i] = grad_keys[i] + more_keys[rows]
                    grad_values[i] = grad_values[i] + more_values[rows]
            for i in range(blocks_here):
                rows = slice(i * BLOCK, (i + 1) * BLOCK)
                grad_columns[H + j, rows] = grad_keys[i]
                grad_columns[H + KV + j, rows] = grad_values[i]
            return 0

        lax.fori_loop(0, KV, attend, 0, unroll=2)
        cosine, sine = cosine_ref[...], -sine_ref[...]
        residual = tokens_ref[...].astype(F32)
        unit_one, scale_one = unit_rows(residual)
        normed = (unit_one * gains_ref[0:1, :]).astype(BF16)
        bring_in.wait()
        grad_normed_one = jnp.zeros((count, D), F32)
        for at in range(0, KEYVAL_END, 4 * LANES):
            pairs = []
            for column in range(at, at + 4 * LANES, LANES):
                head = column // HD
                pair = jnp.concatenate([grad_columns[head], grad_columns[head + 1]], axis=1)
                if column < QUERY_END + KV * HD:
                    pair = turn(pair, cosine, sine)
                pairs.append(pair.astype(BF16))
            columns = jnp.concatenate(pairs, axis=1)
            span = slice(at, at + 4 * LANES)
            stage[:, span] = dot_tn(normed, columns).astype(BF16)
            grad_normed_one = grad_normed_one + dot_nt(columns, weights[:, span])
        send(0, QUERY_COLS, 0)
        send(ACROSS * QUERY_COLS, KEYVAL_COLS, QUERY_COLS)
        gain_ref[0:1, :] = jnp.sum(grad_normed_one * unit_one, axis=0, keepdims=True)
        scaled_one = grad_normed_one * gains_ref[0:1, :]
        input_grad_ref[...] += scale_one * (
            scaled_one - unit_one * jnp.mean(scaled_one * unit_one, axis=-1, keepdims=True)
        )
        pltpu.make_async_copy(stage, stage, sems.at[2]).wait()

    vmem, any_space = whole(pltpu.VMEM), whole(pl.ANY)
    return pl.pallas_call(
        kernel,
        name="attention_back",
        out_shape=(
            jax.ShapeDtypeStruct((count, D), F32),
            jax.ShapeDtypeStruct((2, D), F32),
            jax.ShapeDtypeStruct((near, BLOCK, BLOCK), BF16),
            jax.ShapeDtypeStruct((max(blocks - near, 1), BLOCK, BLOCK), BF16),
        ),
        in_specs=[whole(pltpu.SMEM)] * 3 + [vmem] * 12 + [any_space],
        out_specs=(vmem, vmem, any_space, any_space),
        scratch_shapes=[
            pltpu.VMEM((D, ALL_COLS * BLOCK), BF16),
            pltpu.VMEM((D, ALL_COLS * BLOCK), BF16),
            pltpu.VMEM((H, count, HD), BF16),
            pltpu.VMEM((H + 2 * KV, count, HD), F32),
            pltpu.VMEM((count // BLOCK, group_size * BLOCK, count), F32),
            pltpu.SemaphoreType.DMA((3,)),
        ],
        compiler_params=params(),
        cost_estimate=cost(150),
    )(group, lengths, positions, tokens, packed, gains, cosine, sine, middle, mixed, q, k, v, own, partials, w_all)


def split_low(values):
    high = values.astype(BF16)
    return high, (values - high.astype(F32)).astype(BF16)


def batched(left, right, left_dim, right_dim):
    return lax.dot_general(
        left, right, (((left_dim,), (right_dim,)), ((0,), (0,))), preferred_element_type=F32
    )


def block_mean(values):
    return jnp.mean(values, axis=(1, 2), keepdims=True)


def shampoo(gradient, statistics, inverse_roots, master):
    terms = len(gradient)
    slots = master.shape[0]
    many = max(n for n in range(1, 19) if slots % n == 0 and (n == 1 or slots // n > 1))

    def kernel(*refs):
        stats_ref, roots_ref, master_ref, grad_ref, stats_out, master_out = refs[terms:]
        low = sum(ref[...].astype(F32) for ref in refs[:terms]).astype(BF16)
        grad = low.astype(F32)
        grad_ref[...] = grad
        scale = 0.5 / (block_mean(grad * grad) + 1e-06)
        stats_out[:, 0] = 0.5 * stats_ref[:, 0] + scale * batched(low, low, 2, 2)
        stats_out[:, 1] = 0.5 * stats_ref[:, 1] + scale * batched(low, low, 1, 1)
        left = jnp.concatenate(split_low(roots_ref[:, 0]), axis=2)
        turned = jnp.concatenate(
            split_low(batched(left, jnp.concatenate([low, low], axis=1), 2, 1)), axis=2
        )
        high, rest = split_low(roots_ref[:, 1])
        turned = batched(turned, jnp.concatenate([high, high], axis=1), 2, 1) + batched(
            turned[:, :, :BLOCK], rest, 2, 1
        )
        direction = turned * lax.rsqrt(block_mean(turned * turned) + 1e-06)
        own = master_ref[...]
        master_out[...] = own - STEP_SIZE * jnp.sqrt(block_mean(own * own)) * direction

    one = pl.BlockSpec((many, BLOCK, BLOCK), lambda i: (i, 0, 0))
    two = pl.BlockSpec((many, 2, BLOCK, BLOCK), lambda i: (i, 0, 0, 0))
    return pl.pallas_call(
        kernel,
        name="shampoo",
        grid=(slots // many,),
        out_shape=(
            jax.ShapeDtypeStruct((slots, BLOCK, BLOCK), F32),
            jax.ShapeDtypeStruct((slots, 2, BLOCK, BLOCK), F32),
            jax.ShapeDtypeStruct((slots, BLOCK, BLOCK), F32),
        ),
        in_specs=[one] * terms + [two, two, one],
        out_specs=(one, two, one),
        compiler_params=params(44, dimension_semantics=("arbitrary",)),
        cost_estimate=cost(10),
    )(*gradient, statistics, inverse_roots, master)


def move(array, pairs):
    return lax.ppermute(array, "shard", pairs)


def sibling(array):
    return move(array, [(i, i ^ 1) for i in range(lax.axis_size("shard"))])


def along(array, distance):
    size = lax.axis_size("shard")
    return move(array, [(i, (i + 2 * distance) % size) for i in range(size)])


def give_back(parts):
    return lax.all_to_all(parts, "expert", split_axis=0, concat_axis=0, tiled=True)


def spread(array):
    copies = jnp.broadcast_to(array[None], (lax.axis_size("expert"), *array.shape))
    return lax.all_to_all(copies, "expert", split_axis=0, concat_axis=0, tiled=True)


def two_ways(array, other_first):
    one, two = swap(array, 1), swap(array, 2)
    three = swap(two, 1) if other_first else swap(one, 2)
    return one, two, three


def gather_attention(own, deal, later):
    size, groups = lax.axis_size("shard"), lax.axis_size("expert")
    slots = own.shape[0]
    by_device = deal.reshape(groups, size, slots)
    if groups != 4 or size != 8:
        pieces = [lax.all_gather(own, ("expert", "shard"), axis=0, tiled=True)]
        return pieces, deal, later
    me_e, me_s = lax.axis_index("expert"), lax.axis_index("shard")
    near, across = toward(own, 1), toward(own, 2)
    lines = [near, across, toward(across, 1)]
    beside = [swap(own, 1), swap(own, 2)]
    lines, beside, later = lax.optimization_barrier((lines, beside, later))
    fours = [jnp.concatenate([own, *beside, swap(beside[0], 2)], axis=0)]
    fours += [jnp.concatenate([line, *two_ways(line, d % 2 == 0)], axis=0) for d, line in enumerate(lines)]
    pieces, names, far_names = [], [], []
    for d, four in enumerate(fours):
        pieces.append(four)
        source = me_s ^ (2 * d)
        for m in range(groups):
            names.append(by_device[me_e ^ m, source])
            far_names.append(by_device[me_e ^ m, source ^ 1])
    pieces += [sibling(piece) for piece in pieces]
    return pieces, jnp.concatenate(names + far_names), later


def attention_positions(deal, slots):
    size, groups = lax.axis_size("shard"), lax.axis_size("expert")
    inverse = inverse_of(deal)
    if groups != 4 or size != 8:
        return inverse
    owner, within = inverse // slots, inverse % slots
    mask = (owner // size) ^ lax.axis_index("expert")
    me = lax.axis_index("shard")
    core = (owner % 2) ^ (me % 2)
    distance = ((owner % size) // 2) ^ (me // 2)
    part = distance // (size // 4)
    first, second = jnp.where(part == 0, mask % 2, mask // 2), jnp.where(part == 0, mask // 2, mask % 2)
    place = ((core * 2 + 1 - first) * 2 + part) * 2 + second
    return ((place * (size // 4) + distance % (size // 4)) * slots + within).astype(jnp.int32)


def add_low(left, right):
    return (left.astype(F32) + right.astype(F32)).astype(BF16)


def scatter_attention(near, far, slots):
    size, groups = lax.axis_size("shard"), lax.axis_size("expert")
    if groups != 4 or size != 8:
        return [lax.psum_scatter(near, ("expert", "shard"), scatter_dimension=0, tiled=True)]
    quarter = near.shape[0] // 4
    far_first, far_rest = sibling(far[: 2 * quarter]), sibling(far[2 * quarter :])
    terms = []
    for part, (first, second) in enumerate(((1, 2), (2, 1))):
        here = slice(part * quarter, (part + 1) * quarter)
        there = slice((2 + part) * quarter, (3 + part) * quarter)
        mine = add_low(near[there], far_rest[here])
        mine = add_low(mine, swap(add_low(near[here], far_first[here]), first))
        stay, leave = mine[: quarter // 2], mine[quarter // 2 :]
        line = add_low(stay, swap(leave, second))
        terms += [line[i : i + slots] for i in range(0, line.shape[0], slots)]
    return terms


def toward(array, mask):
    return move(array, [(i, i ^ (2 * mask)) for i in range(lax.axis_size("shard"))])


def fold_line(terms):
    if len(terms) == 1:
        return terms
    own, one, two, three = terms
    return [own, one, add_low(two, toward(three, 1))]


def scatter_line(terms):
    return terms[:1] + [toward(term, mask) for mask, term in enumerate(terms) if mask > 0]


def sum_across(values):
    size, groups = lax.axis_size("shard"), lax.axis_size("expert")
    if groups != 4 or size != 8:
        return lax.psum(values, ("expert", "shard"))
    values = values + sibling(values)
    for mask in (1, 2):
        values = values + swap(values, mask)
    return values


def sum_line(values):
    size, groups = lax.axis_size("shard"), lax.axis_size("expert")
    if groups != 4 or size != 8:
        return values
    line = jnp.stack([values] + [along(values, d) for d in range(1, size // 2)])
    place = lax.axis_index("shard") // 2
    return sum(line[(place - z) % (size // 2)] for z in range(size // 2))


def swap(array, mask):
    if mask == 0:
        return array
    return lax.ppermute(array, "expert", [(i, i ^ mask) for i in range(lax.axis_size("expert"))])


def per_device(
    tokens,
    cotangent,
    lengths,
    routes,
    route_gates,
    norm_gains,
    attn_master,
    attn_stats,
    attn_roots,
    attn_deal,
    expert_master,
    expert_stats,
    expert_roots,
    expert_deal,
):
    row_count = tokens.shape[0]
    groups = lax.axis_size("expert")
    group = lax.axis_index("expert").astype(jnp.int32).reshape(1)
    places = jnp.arange(row_count)
    valid_rows = places < lengths[0]
    grad_low = jnp.where(valid_rows[:, None], cotangent, jnp.zeros_like(cotangent))
    expert_lane = jnp.arange(LANES, dtype=jnp.int32)
    weights_row = sum(
        jnp.where(routes[:, k, None] == expert_lane, route_gates[:, k, None], jnp.zeros((), BF16))
        for k in range(TOP)
    )
    packed = jnp.concatenate([grad_low, weights_row], axis=1)
    half = row_count // 2
    packed_top = spread(packed[:half])
    pieces, natural, expert_low = gather_attention(
        attn_master.astype(BF16), attn_deal, expert_master.astype(BF16)
    )
    pieces, packed_bottom = lax.optimization_barrier((pieces, packed[half:]))
    packed_all = [packed_top, spread(packed_bottom)]
    expert_all = lax.all_gather(expert_low, "shard", axis=0, tiled=True)
    cosine, sine = rope_tables(jnp.arange(row_count, dtype=F32))
    cosine = jnp.concatenate([cosine] * 4, axis=1)
    sine = jnp.concatenate([-sine, sine] * 2, axis=1)
    block_rows, block_cols = attention_places(natural)
    normed_two, middle, mixed, q, k, v, w_all = attention_front(
        lengths, block_rows, block_cols, tokens, norm_gains, cosine, sine, pieces
    )
    rows = [swap(normed_two, m) for m in range(groups)]
    expert_inverse = inverse_of(expert_deal[0])
    hidden, both, partials, matrices = expert_front(group, expert_inverse, expert_all, rows, packed_all)
    partials = give_back(partials)
    expert_term = expert_weight_grads(group, expert_inverse, rows, packed_all, hidden, both)
    moe_parts = expert_outputs(group, hidden, matrices)
    own_partial = expert_route(both[0], matrices)
    mixed, moe_parts = lax.optimization_barrier((mixed, moe_parts))
    moe_parts = give_back(moe_parts)
    slots = attn_master.shape[0]
    positions = attention_positions(attn_deal, slots)
    near = positions.shape[0] // (2 if groups == 4 and lax.axis_size("shard") == 8 else 1)
    input_grad, gain_parts, near_blocks, far_blocks = attention_back(
        lengths, positions, tokens, packed, norm_gains, cosine, sine, middle, mixed, q, k, v, w_all, group, own_partial, partials, near
    )
    near_blocks, far_blocks, moe_parts = lax.optimization_barrier((near_blocks, far_blocks, moe_parts))
    output = (middle + jnp.sum(moe_parts.astype(F32), axis=0)).astype(BF16)
    attn_terms = scatter_attention(near_blocks, far_blocks, slots)
    expert_term = lax.psum_scatter(expert_term, "shard", scatter_dimension=0, tiled=True)
    attn_terms = fold_line(attn_terms)
    attn_terms, gain_parts = lax.optimization_barrier((attn_terms, gain_parts))
    gain_grads = sum_line(sum_across(gain_parts))
    expert_term, attn_terms, gain_grads = lax.optimization_barrier((expert_term, attn_terms, gain_grads))
    attn_terms = scatter_line(attn_terms)
    new_gains = norm_gains - STEP_SIZE * gain_grads * lax.rsqrt(
        jnp.mean(gain_grads * gain_grads, axis=-1, keepdims=True) + 1e-06
    )
    expert_grads, expert_stats_new, expert_new = shampoo(
        [expert_term], expert_stats, expert_roots, expert_master
    )
    attn_terms, expert_new = lax.optimization_barrier((attn_terms, expert_new))
    attn_grads, attn_stats_new, attn_new = shampoo(attn_terms, attn_stats, attn_roots, attn_master)
    return (
        output,
        input_grad,
        gain_grads,
        new_gains,
        attn_grads,
        attn_stats_new,
        attn_new,
        expert_grads,
        expert_stats_new,
        expert_new,
    )


def solution(mesh):
    in_specs = (
        P(("expert", "shard"), None),
        P(("expert", "shard"), None),
        P(("expert", "shard")),
        P(("expert", "shard"), None),
        P(("expert", "shard"), None),
        P(),
        P(("expert", "shard"), None, None),
        P(("expert", "shard"), None, None, None),
        P(("expert", "shard"), None, None, None),
        P(),
        P(("expert", "shard"), None, None),
        P(("expert", "shard"), None, None, None),
        P(("expert", "shard"), None, None, None),
        P("expert", None),
    )
    out_specs = (
        P(("expert", "shard"), None),
        P(("expert", "shard"), None),
        P(),
        P(),
        P(("expert", "shard"), None, None),
        P(("expert", "shard"), None, None, None),
        P(("expert", "shard"), None, None),
        P(("expert", "shard"), None, None),
        P(("expert", "shard"), None, None, None),
        P(("expert", "shard"), None, None),
    )
    return jax.shard_map(
        per_device, mesh=mesh, in_specs=in_specs, out_specs=out_specs, check_vma=False
    )
```
